256 devices in a mesh: row: 8 (over y, x_lo), col: 8 (over z), depth: 4 (over x_hi, core).
Axes of the slice: x: 4 (x_hi: 2, x_lo: 2; x = x_hi * 2 + x_lo), y: 4, z: 8, core: 2. Of those that a mesh axis runs over, the one named last changes fastest.
Arguments:
- tokens: float32 [1536, 6144], P('row', 'col'), may hold values from -6 to 6
- up_weight: float32 [12288, 6144], P(('row', 'depth'), 'col'), may hold values from -0.078125 to 0.078125
- down_weight: float32 [12288, 6144], P(('row', 'depth'), 'col'), may hold values from -0.0546875 to 0.0546875
- cotangent: float32 [1536, 6144], P('row', 'col'), may hold values from -1.25 to 1.25
Outputs:
- output: float32 [1536, 6144], P('row', ('col', 'depth'))
- grad_tokens: float32 [1536, 6144], P('row', ('col', 'depth'))
- grad_up: float32 [12288, 6144], P(('row', 'depth'), 'col')
- grad_down: float32 [12288, 6144], P(('row', 'depth'), 'col')
The draws below stay inside these ranges and needn't reach their ends.
All inputs are finite; a program needn't handle non-finite values.
Results may differ from the reference program's by a relative error of at most 0.00013.
Values sent between devices are 32-bit elements; how exact they have to be, the bound alone decides.
A program may use at most 128 MiB of HBM per device.

```python
import jax
import jax.numpy as jnp
from jax import lax

D = 6144
FF = 12288
TOKENS = 1536


def block_scale(own_key, dims, cuts, least, largest):
    gain, own = 1.0, jax.random.fold_in(own_key, 6)
    for axis_at, shards_of in cuts:
        heights = jnp.exp(jax.random.uniform(jax.random.fold_in(own, axis_at), (shards_of,), jnp.float32, least / len(cuts), largest / len(cuts)))
        gain = gain * jnp.repeat(heights, dims[axis_at] // shards_of).reshape([-1 if axis == axis_at else 1 for axis in range(len(dims))])
    return gain


def noise(stream_key, extent, scale, reach, split=(), held_as=jnp.bfloat16):
    drawn = scale * jax.random.normal(stream_key, extent, jnp.float32)
    if split:
        drawn = drawn * block_scale(stream_key, extent, split, -0.22, 0.18)
    return jnp.clip(drawn, -reach, reach).astype(held_as)


def setup_inputs(seed: int = 0) -> dict:
    streams_of = jax.random.split(jax.random.key(seed), 5)
    return {
        "tokens": noise(streams_of[0], (TOKENS, D), 1.0, 6.0, ((0, 8), (1, 8)), jnp.float32),
        "up_weight": noise(streams_of[1], (FF, D), D ** -0.5, 0.078125, ((0, 32), (1, 8)), jnp.float32),
        "down_weight": noise(streams_of[2], (FF, D), FF ** -0.5, 0.0546875, ((0, 32), (1, 8)), jnp.float32),
        "cotangent": noise(streams_of[3], (TOKENS, D), 0.2, 1.25, ((0, 8), (1, 8)), jnp.float32),
    }


full_precision = lax.Precision.HIGHEST
root_two_pi = 0.7978845608028654
cubic_coef = 0.044715


def gelu_parts(hidden):
    inner_arg = root_two_pi * (hidden + cubic_coef * hidden * hidden * hidden)
    bent_value = jnp.tanh(inner_arg)
    result = 0.5 * hidden * (1.0 + bent_value)
    slopes = 0.5 * (1.0 + bent_value) + 0.5 * hidden * (1.0 - bent_value * bent_value) * root_two_pi * (1.0 + 3.0 * cubic_coef * hidden * hidden)
    return result, slopes


def matmul(left_side, right_side):
    return jnp.dot(left_side, right_side, precision=full_precision, preferred_element_type=jnp.float32)


def reference(tokens, up_weight, down_weight, cotangent):
    hidden = matmul(tokens, up_weight.T)
    activated, slopes = gelu_parts(hidden)
    output = matmul(activated, down_weight)
    grad_act = matmul(cotangent, down_weight.T)
    grad_hidden = grad_act * slopes
    grad_tokens = matmul(grad_hidden, up_weight)
    grad_up = matmul(grad_hidden.T, tokens)
    grad_down = matmul(activated.T, cotangent)
    return output, grad_tokens, grad_up, grad_down
```

```python
import jax
import jax.numpy as jnp
from jax import lax
from jax.sharding import PartitionSpec as P

full_precision = lax.Precision.HIGH
root_two_pi = 0.7978845608028654
cubic_coef = 0.044715


def gelu_parts(hidden):
    inner_arg = root_two_pi * (hidden + cubic_coef * hidden * hidden * hidden)
    bent_value = jnp.tanh(inner_arg)
    result = 0.5 * hidden * (1.0 + bent_value)
    slopes = 0.5 * (1.0 + bent_value) + 0.5 * hidden * (
        1.0 - bent_value * bent_value
    ) * root_two_pi * (1.0 + 3.0 * cubic_coef * hidden * hidden)
    return (result, slopes)


def matmul(left_side, right_side):
    return jnp.dot(
        left_side, right_side, precision=full_precision, preferred_element_type=jnp.float32
    )


def contract_rows(left_side, right_side):
    return lax.dot_general(
        left_side,
        right_side,
        (((0,), (0,)), ((), ())),
        precision=full_precision,
        preferred_element_type=jnp.float32,
    )


def contract_cols(left_side, right_side):
    return lax.dot_general(
        left_side,
        right_side,
        (((1,), (1,)), ((), ())),
        precision=full_precision,
        preferred_element_type=jnp.float32,
    )


def width_total(partial_value):
    return lax.psum_scatter(partial_value, "col", scatter_dimension=0, tiled=True)


def units_across(piece_in):
    return lax.all_gather(piece_in, "col", axis=0, tiled=True)


def layer_total(partial_value):
    own_width = lax.psum_scatter(partial_value, "depth", scatter_dimension=1, tiled=True)
    return lax.psum_scatter(own_width, "row", scatter_dimension=0, tiled=True)


def shards(tokens, up_weight, down_weight, cotangent):
    token_all = lax.all_gather(tokens, "row", axis=0, tiled=True)
    cot_all = lax.all_gather(cotangent, "row", axis=0, tiled=True)
    hidden = width_total(contract_cols(token_all, up_weight))
    grad_act = width_total(contract_cols(cot_all, down_weight))
    activated, slopes = gelu_parts(hidden)
    act_units = units_across(activated)
    output = layer_total(matmul(act_units, down_weight))
    grad_units = units_across(grad_act * slopes)
    grad_tokens = layer_total(matmul(grad_units, up_weight))
    grad_up = contract_rows(grad_units, token_all)
    grad_down = contract_rows(act_units, cot_all)
    return (output, grad_tokens, grad_up, grad_down)


def solution(mesh):
    return jax.shard_map(
        shards,
        mesh=mesh,
        in_specs=(
            P("row", "col"),
            P(("row", "depth"), "col"),
            P(("row", "depth"), "col"),
            P("row", "col"),
        ),
        out_specs=(
            P("row", ("col", "depth")),
            P("row", ("col", "depth")),
            P(("row", "depth"), "col"),
            P(("row", "depth"), "col"),
        ),
        check_vma=False,
    )
```

```python
import jax
import jax.numpy as jnp
from jax import lax
from jax.experimental import pallas as pl
from jax.experimental.pallas import tpu as pltpu
from jax.sharding import PartitionSpec as P

F32, BF16 = jnp.float32, jnp.bfloat16
root_two_pi = 0.7978845608028654
cubic_coef = 0.044715

SLOTS = 260
BLOCK, WIDTH, UNITS, CHUNK = 192, 768, 384, 24


def gelu_parts(hidden):
    inner_arg = root_two_pi * (hidden + cubic_coef * hidden * hidden * hidden)
    bent_value = jnp.tanh(inner_arg)
    result = 0.5 * hidden * (1.0 + bent_value)
    slopes = 0.5 * (1.0 + bent_value) + 0.5 * hidden * (
        1.0 - bent_value * bent_value
    ) * root_two_pi * (1.0 + 3.0 * cubic_coef * hidden * hidden)
    return (result, slopes)


def halves(value):
    high = value.astype(BF16)
    return high, (value - high.astype(F32)).astype(BF16)


def kernel(
    tokens, up_weight, down_weight, cotangent,
    output, grad_tokens, grad_up, grad_down,
    gathered, raw, weights, partial, summed, spread, slope, fold, to_sib, from_sib,
    near, far_out, far_tok, last, ends, result, give, take,
    send_sem, recv_sem, local_sem,
):
    row, z, depth = lax.axis_index("row"), lax.axis_index("col"), lax.axis_index("depth")
    y, xl, xh, q = row // 2, row % 2, depth // 2, depth % 2
    xh_r, xh_l, xh_s = (xh + xl) % 2, (xh + xl + 1) % 2, (xh + xl + q) % 2
    sib = (row, z, xh * 2 + 1 - q)
    y_r, y_l = (((y + 1) % 4) * 2 + xl, z, depth), (((y + 3) % 4) * 2 + xl, z, depth)
    x_r, x_l = (y * 2 + 1 - xl, z, xh_r * 2 + q), (y * 2 + 1 - xl, z, xh_l * 2 + q)
    z_r, z_l = (row, (z + 1) % 8, depth), (row, (z + 7) % 8, depth)
    y_s = (((y + 1 + 2 * q) % 4) * 2 + xl, z, depth)
    x_s = (y * 2 + 1 - xl, z, xh_s * 2 + q)
    z_dev, z_sgn = (z_r, z_l), (1, 7)

    slots, pending = {}, []

    def remote(name, src, dst, device):
        at = slots.setdefault(name, len(slots))
        return pltpu.make_async_remote_copy(
            src_ref=src, dst_ref=dst, send_sem=send_sem.at[at], recv_sem=recv_sem.at[at],
            device_id=device, device_id_type=pl.DeviceIdType.MESH,
        )

    def send(name, src, dst, device):
        copy = remote(name, src, dst, device)
        copy.start()
        pending.append(copy)

    def arrive(name, dst):
        remote(name, dst, dst, sib).wait_recv()

    def rows(core, half=None):
        if half is None:
            return pl.ds(pl.multiple_of(core * 96, 8), 96)
        return pl.ds(pl.multiple_of(core * 96 + half * 48, 8), 48)

    def across_x(a, dy):
        yy = (y + dy) % 4
        for half, device in ((0, x_r), (1, x_l)):
            piece = rows(q, half)
            send(("x", a, dy, half), gathered.at[a, 0, yy, piece], gathered.at[a, 1, yy, piece], device)

    def to_core(a, g, dy):
        piece = gathered.at[a, g, (y + dy) % 4, rows(q)]
        send(("s", a, g, dy), piece, piece, sib)

    def own(a):
        piece = gathered.at[a, 0, y, rows(q)]
        send(("yr", a), piece, piece, y_r)
        send(("yl", a), piece, piece, y_l)
        across_x(a, 0)

    def get_y(a, dy):
        yy = (y + dy) % 4
        name, half, device = ("yr", 0, y_r) if dy == 3 else ("yl", 1, y_l)
        arrive((name, a), gathered.at[a, 0, yy, rows(q)])
        piece = gathered.at[a, 0, yy, rows(q, half)]
        send((name + "f", a), piece, piece, device)
        across_x(a, dy)
        to_core(a, 0, dy)

    def get_y2(a):
        yy = (y + 2) % 4
        arrive(("yrf", a), gathered.at[a, 0, yy, rows(q, 0)])
        arrive(("ylf", a), gathered.at[a, 0, yy, rows(q, 1)])
        across_x(a, 2)
        to_core(a, 0, 2)

    def get_x(a, dy):
        for half in range(2):
            arrive(("x", a, dy, half), gathered.at[a, 1, (y + dy) % 4, rows(q, half)])
        to_core(a, 1, dy)

    def get_core(a, g):
        for dy in (1, 3, 2) if g == 0 else (0, 1, 3, 2):
            arrive(("s", a, g, dy), gathered.at[a, g, (y + dy) % 4, rows(1 - q)])

    def split_weights(a):
        high, low = halves(raw[a])
        weights[a, 0:UNITS] = high
        weights[a, UNITS:2 * UNITS] = high
        weights[a, 2 * UNITS:3 * UNITS] = low

    def first_product(a, g):
        def body(pair, carry):
            high, low = halves(gathered[a, g, pl.ds(pair * 2, 2)].reshape(2 * BLOCK, WIDTH))
            w_high, w_low = weights[a, 0:UNITS], weights[a, 2 * UNITS:3 * UNITS]

            def nt(left, right):
                return lax.dot_general(left, right, (((1,), (1,)), ((), ())), preferred_element_type=F32)

            total = nt(high, w_high) + (nt(low, w_high) + nt(high, w_low))
            for j in range(2):
                partial[a, :, g, pair * 2 + j] = total[j * BLOCK:(j + 1) * BLOCK].reshape(8, CHUNK, UNITS)
            return carry

        lax.fori_loop(0, 2, body, 0)

    def z_chunk(way, distance):
        return (z + z_sgn[way] * distance) % 8

    def rs_send(a, way, step, g):
        send(("rs", a, way, step, g), partial.at[a, z_chunk(way, 5 - step), g], summed.at[a, way, step - 1, g], z_dev[way])

    def rs_get(a, way, step, g):
        arrive(("rs", a, way, step, g), summed.at[a, way, step - 1, g])

    def rs_hop(a, way, step, g):
        rs_get(a, way, step - 1, g)
        c = z_chunk(way, 5 - step)
        partial[a, c, g] = partial[a, c, g] + summed[a, way, step - 2, g]
        rs_send(a, way, step, g)

    def rs_step(a, step):
        if step == 2:
            rs_hop(a, 0, 2, 0)
            rs_hop(a, 1, 2, 1)
        else:
            for way, g in ((1, 0), (0, 1), (0, 0), (1, 1)):
                rs_hop(a, way, step, g)

    def rs_start(a, g):
        rs_send(a, g, 1, g)
        rs_send(a, 1 - g, 2, g)

    def rs_total(a, g):
        rs_get(a, 0, 4, g)
        rs_get(a, 1, 4, g)
        return partial[a, z, g] + summed[a, 0, 3, g] + summed[a, 1, 3, g]

    def ag_send(a, way, k, g):
        piece = spread.at[a, z_chunk(1 - way, k - 1), g]
        send(("ag", a, way, k, g), piece, piece, z_dev[way])

    def ag_get(a, k):
        for g in range(2):
            for way in range(2):
                if k == 4 and way != g:
                    continue
                arrive(("ag", a, way, k, g), spread.at[a, z_chunk(1 - way, k), g])
                if k < 3 or (k == 3 and way == g):
                    ag_send(a, way, k + 1, g)

    def finish_hidden():
        for g in range(2):
            activated, slopes = gelu_parts(rs_total(0, g))
            spread[0, z, g] = activated
            slope[g] = slopes
            for way in range(2):
                ag_send(0, way, 1, g)

    def finish_grad():
        for g in range(2):
            spread[1, z, g] = rs_total(1, g) * slope[g]
            for way in range(2):
                ag_send(1, way, 1, g)

    def round_chunk(r, core):
        if r == 4:
            return (z + 4 * core) % 8
        return (z + r + (8 - 2 * r) * core) % 8

    def second_product(a, c, r, dst):
        high, low = halves(spread[a, c].reshape(BLOCK, UNITS))
        total = jnp.dot(jnp.concatenate([high, low, high], axis=1), weights[1 - a], preferred_element_type=F32)
        for side in range(2):
            dst[r - 1, a, side] = total[:, side * UNITS:(side + 1) * UNITS].reshape(2, 4, CHUNK, UNITS)

    def f_mm(a, r):
        second_product(a, round_chunk(r, 1 - q), r, to_sib)
        send(("fs", a, r), to_sib.at[r - 1, a], from_sib.at[r - 1, a], sib)
        second_product(a, round_chunk(r, q), r, fold)

    def f_sib(a, r):
        i = r - 1
        arrive(("fs", a, r), from_sib.at[i, a])
        fold[i, a] = fold[i, a] + from_sib[i, a]
        if a == 0:
            send(("f1", a, r, 0), fold.at[i, 0, 1 - xh, 0, 0:2], near.at[i, a, 0], x_r)
            send(("f1", a, r, 1), fold.at[i, 0, 1 - xh, 0, 2:4], near.at[i, a, 1], x_l)
        else:
            send(("f1", a, r, 0), fold.at[i, 1, 0, :, (y + 2) % 4], near.at[i, a, 0], y_r)
            send(("f1", a, r, 1), fold.at[i, 1, 1, :, (y + 2) % 4], near.at[i, a, 1], y_l)

    def f_r1(a, r):
        i = r - 1
        arrive(("f1", a, r, 0), near.at[i, a, 0])
        if a == 0:
            fold[i, 0, xh_r, 1, 0:2] = fold[i, 0, xh_r, 1, 0:2] + near[i, 0, 0]
            send(("f2", a, r, 0), fold.at[i, 0, xh_r, 1], far_out.at[i, 0], x_r)
        else:
            fold[i, 1, 0, :, (y + 1) % 4] = fold[i, 1, 0, :, (y + 1) % 4] + near[i, 1, 0]
            send(("f2", a, r, 0), fold.at[i, 1, :, :, (y + 1) % 4], far_tok.at[i, 0], y_r)
        arrive(("f1", a, r, 1), near.at[i, a, 1])
        if a == 0:
            fold[i, 0, xh_l, 1, 2:4] = fold[i, 0, xh_l, 1, 2:4] + near[i, 0, 1]
            send(("f2", a, r, 1), fold.at[i, 0, xh_l, 1], far_out.at[i, 1], x_l)
        else:
            fold[i, 1, 1, :, (y + 3) % 4] = fold[i, 1, 1, :, (y + 3) % 4] + near[i, 1, 1]
            send(("f2", a, r, 1), fold.at[i, 1, :, :, (y + 3) % 4], far_tok.at[i, 1], y_l)

    def f_r2(a, r):
        i = r - 1
        if a == 0:
            arrive(("f2", a, r, 0), far_out.at[i, 0])
            arrive(("f2", a, r, 1), far_out.at[i, 1])
            fold[i, 0, xh, 0] = fold[i, 0, xh, 0] + far_out[i, 0] + far_out[i, 1]
            send(("f3", a, r), fold.at[i, 0, xh, 0, (y + 2) % 4], last.at[i, a], y_s)
        else:
            arrive(("f2", a, r, 0), far_tok.at[i, 0])
            arrive(("f2", a, r, 1), far_tok.at[i, 1])
            fold[i, 1, :, :, y] = fold[i, 1, :, :, y] + far_tok[i, 0] + far_tok[i, 1]
            send(("f3", a, r), fold.at[i, 1, 1 - xh, 0, y], last.at[i, a], x_s)

    def f_r3(a, r):
        i = r - 1
        arrive(("f3", a, r), last.at[i, a])
        if a == 0:
            ys = (y + 1 + 2 * q) % 4
            fold[i, 0, xh, 0, ys] = fold[i, 0, xh, 0, ys] + last[i, 0]
            send(("f4", a, r, 0), fold.at[i, 0, xh, 0, (y + 1) % 4], ends.at[i, a, 0], y_r)
            send(("f4", a, r, 1), fold.at[i, 0, xh, 0, (y + 3) % 4], ends.at[i, a, 1], y_l)
        else:
            fold[i, 1, xh_s, 1, y] = fold[i, 1, xh_s, 1, y] + last[i, 1]
            send(("f4", a, r, 0), fold.at[i, 1, xh_r, 1, y], ends.at[i, a, 0], x_r)
            send(("f4", a, r, 1), fold.at[i, 1, xh_l, 1, y], ends.at[i, a, 1], x_l)

    def f_r4(a, r):
        i = r - 1
        arrive(("f4", a, r, 0), ends.at[i, a, 0])
        arrive(("f4", a, r, 1), ends.at[i, a, 1])
        result[a, i] = fold[i, a, xh, 0, y] + ends[i, a, 0] + ends[i, a, 1]

    def swap(a):
        dst = (output, grad_tokens)[a]
        first, second = result[a, :, :, 0:BLOCK], result[a, :, :, BLOCK:2 * BLOCK]
        lower = jnp.full(first.shape, q, jnp.int32) == 0
        give[a] = jnp.where(lower, second, first)
        send(("swap", a), give.at[a], take.at[a], sib)
        mine = jnp.where(lower, first, second)
        for r in range(1, 5):
            at = pl.ds(pl.multiple_of(round_chunk(r, q) * CHUNK, 8), CHUNK)
            dst[at, :] = mine[r - 1]

    def swapped(a):
        dst = (output, grad_tokens)[a]
        arrive(("swap", a), take.at[a])
        for r in range(1, 5):
            at = pl.ds(pl.multiple_of(round_chunk(r, 1 - q) * CHUNK, 8), CHUNK)
            dst[at, :] = take[a, r - 1]

    def grad(a, r):
        dst = (grad_down, grad_up)[a]
        chunks = (round_chunk(r, 0), round_chunk(r, 1))
        left = jnp.concatenate([spread[a, c].reshape(BLOCK, UNITS) for c in chunks], axis=0).T
        right = jnp.concatenate(
            [gathered[1 - a, :, :, pl.ds(pl.multiple_of(c * CHUNK, 8), CHUNK), :].reshape(BLOCK, WIDTH) for c in chunks], axis=0)
        l_high, l_low = halves(left)
        r_high, r_low = halves(right)
        term = jnp.dot(
            jnp.concatenate([l_high, l_low, l_high], axis=1), jnp.concatenate([r_high, r_high, r_low], axis=0),
            preferred_element_type=F32)
        dst[...] = term if r == 1 else dst[...] + term

    loads = [
        pltpu.make_async_copy(src, dst, local_sem.at[i])
        for i, (src, dst) in enumerate((
            (tokens, gathered.at[0, 0, y]), (cotangent, gathered.at[1, 0, y]),
            (up_weight, raw.at[0]), (down_weight, raw.at[1]),
        ))
    ]
    for load in loads:
        load.start()
    barrier = pltpu.get_barrier_semaphore()
    partners = (sib, y_r, y_l, x_r, x_l, z_r, z_l)
    for device in partners:
        pl.semaphore_signal(barrier, inc=1, device_id=device, device_id_type=pl.DeviceIdType.MESH)
    loads[0].wait()
    pl.semaphore_wait(barrier, len(partners))

    own(0)
    loads[2].wait()
    split_weights(0)
    get_y(0, 3)
    get_y(0, 1)
    loads[1].wait()
    own(1)
    loads[3].wait()
    split_weights(1)
    get_y2(0)
    get_x(0, 0)
    get_core(0, 0)
    first_product(0, 0)
    rs_start(0, 0)
    get_y(1, 3)
    get_y(1, 1)
    get_x(0, 1)
    get_x(0, 3)
    get_x(0, 2)
    get_y2(1)
    get_x(1, 0)
    get_core(0, 1)
    first_product(0, 1)
    rs_start(0, 1)
    rs_step(0, 2)
    get_x(1, 1)
    get_x(1, 3)
    get_x(1, 2)
    rs_step(0, 3)
    get_core(1, 0)
    first_product(1, 0)
    rs_start(1, 0)
    rs_step(0, 4)
    get_core(1, 1)
    first_product(1, 1)
    rs_start(1, 1)
    rs_step(1, 2)
    finish_hidden()
    rs_step(1, 3)
    ag_get(0, 1)
    rs_step(1, 4)
    ag_get(0, 2)
    finish_grad()
    f_mm(0, 1)
    ag_get(0, 3)
    f_sib(0, 1)
    grad(0, 1)
    ag_get(1, 1)
    f_r1(0, 1)
    f_mm(1, 1)
    f_mm(0, 2)
    f_r2(0, 1)
    ag_get(0, 4)
    f_sib(1, 1)
    f_sib(0, 2)
    ag_get(1, 2)
    f_r3(0, 1)
    f_r1(1, 1)
    f_r1(0, 2)
    f_mm(1, 2)
    f_mm(0, 3)
    f_r4(0, 1)
    f_r2(1, 1)
    f_r2(0, 2)
    f_sib(1, 2)
    f_sib(0, 3)
    grad(0, 2)
    ag_get(1, 3)
    f_r3(1, 1)
    f_r3(0, 2)
    f_r1(1, 2)
    f_r1(0, 3)
    f_mm(1, 3)
    f_mm(0, 4)
    f_r4(1, 1)
    f_r4(0, 2)
    f_r2(1, 2)
    f_r2(0, 3)
    f_sib(1, 3)
    f_sib(0, 4)
    grad(0, 3)
    ag_get(1, 4)
    f_mm(1, 4)
    f_r3(1, 2)
    f_r3(0, 3)
    f_r1(1, 3)
    f_r1(0, 4)
    f_sib(1, 4)
    grad(1, 1)
    f_r4(1, 2)
    f_r4(0, 3)
    f_r2(1, 3)
    f_r2(0, 4)
    f_r1(1, 4)
    grad(1, 2)
    f_r3(1, 3)
    f_r3(0, 4)
    f_r2(1, 4)
    grad(1, 3)
    f_r4(1, 3)
    f_r4(0, 4)
    f_r3(1, 4)
    swap(0)
    grad(1, 4)
    f_r4(1, 4)
    swap(1)
    grad(0, 4)
    swapped(0)
    swapped(1)
    for copy in pending:
        copy.wait_send()
    assert len(slots) <= SLOTS, len(slots)


def shards(tokens, up_weight, down_weight, cotangent):
    anywhere, vmem = pl.BlockSpec(memory_space=pl.ANY), pl.BlockSpec(memory_space=pltpu.VMEM)
    piece = (CHUNK, UNITS)
    return pl.pallas_call(
        kernel,
        out_shape=(
            jax.ShapeDtypeStruct((BLOCK, BLOCK), F32),
            jax.ShapeDtypeStruct((BLOCK, BLOCK), F32),
            jax.ShapeDtypeStruct((UNITS, WIDTH), F32),
            jax.ShapeDtypeStruct((UNITS, WIDTH), F32),
        ),
        in_specs=[anywhere] * 4,
        out_specs=(vmem,) * 4,
        scratch_shapes=[
            pltpu.VMEM((2, 2, 4, BLOCK, WIDTH), F32),
            pltpu.VMEM((2, UNITS, WIDTH), F32),
            pltpu.VMEM((2, 3 * UNITS, WIDTH), BF16),
            pltpu.VMEM((2, 8, 2, 4) + piece, F32),
            pltpu.VMEM((2, 2, 4, 2, 4) + piece, F32),
            pltpu.VMEM((2, 8, 2, 4) + piece, F32),
            pltpu.VMEM((2, 4) + piece, F32),
            pltpu.VMEM((4, 2, 2, 2, 4) + piece, F32),
            pltpu.VMEM((4, 2, 2, 2, 4) + piece, F32),
            pltpu.VMEM((4, 2, 2, 2, 4) + piece, F32),
            pltpu.VMEM((4, 2, 2, 2) + piece, F32),
            pltpu.VMEM((4, 2, 4) + piece, F32),
            pltpu.VMEM((4, 2, 2, 2) + piece, F32),
            pltpu.VMEM((4, 2) + piece, F32),
            pltpu.VMEM((4, 2, 2) + piece, F32),
            pltpu.VMEM((2, 4) + piece, F32),
            pltpu.VMEM((2, 4, CHUNK, BLOCK), F32),
            pltpu.VMEM((2, 4, CHUNK, BLOCK), F32),
            pltpu.SemaphoreType.DMA((SLOTS,)),
            pltpu.SemaphoreType.DMA((SLOTS,)),
            pltpu.SemaphoreType.DMA((4,)),
        ],
        compiler_params=pltpu.CompilerParams(
            collective_id=0, has_side_effects=True, vmem_limit_bytes=62 * 1024 * 1024),
        cost_estimate=pl.CostEstimate(flops=16_300_000_000, bytes_accessed=6_000_000, transcendentals=73728),
    )(tokens, up_weight, down_weight, cotangent)


def solution(mesh):
    return jax.shard_map(
        shards,
        mesh=mesh,
        in_specs=(
            P("row", "col"),
            P(("row", "depth"), "col"),
            P(("row", "depth"), "col"),
            P("row", "col"),
        ),
        out_specs=(
            P("row", ("col", "depth")),
            P("row", ("col", "depth")),
            P(("row", "depth"), "col"),
            P(("row", "depth"), "col"),
        ),
        check_vma=False,
    )
```

```python
import jax
import jax.numpy as jnp
from jax import lax
from jax.experimental import pallas as pl
from jax.experimental.pallas import tpu as pltpu
from jax.sharding import PartitionSpec as P

F32, BF16 = jnp.float32, jnp.bfloat16
root_two_pi = 0.7978845608028654
cubic_coef = 0.044715

SLOTS = 260
BLOCK, WIDTH, UNITS, CHUNK = 192, 768, 384, 24
PAIRS = (((0, 0), (1, 0)), ((0, 1), (0, 3)), ((1, 1), (1, 3)), ((0, 2), (1, 2)))
ORDER = (
    ("own", 0), ("split_weights", 0), ("split_weights", 1), ("gy", 0, 0, 0), ("gy", 0, 1, 1), ("gx", 0, 0, 0),
    ("gx", 0, 0, 1), ("prod", 0, 0), ("gy", 0, 0, 1), ("gy", 0, 1, 0), ("own", 1), ("gx", 0, 3, 0), ("gx", 0, 1, 1),
    ("prod", 0, 1), ("rs_hop", 0, 0, 0, 2), ("rs_hop", 0, 0, 1, 3), ("gf", 0, 0), ("gf", 0, 1), ("gx", 0, 3, 1),
    ("gx", 0, 1, 0), ("gy", 1, 0, 0), ("gy", 1, 1, 1), ("rs_hop", 0, 1, 1, 2), ("rs_hop", 0, 1, 0, 3), ("prod", 0, 2),
    ("rs_hop", 0, 0, 0, 3), ("rs_hop", 0, 0, 1, 4), ("gy", 1, 0, 1), ("gy", 1, 1, 0), ("rs_hop", 0, 1, 1, 3),
    ("rs_hop", 0, 1, 0, 4), ("gx", 1, 0, 0), ("gx", 1, 0, 1), ("gx", 0, 2, 1), ("gx", 0, 2, 0),
    ("rs_hop", 0, 2, 0, 2), ("rs_hop", 0, 2, 1, 3), ("gf", 1, 0), ("gf", 1, 1), ("prod", 0, 3),
    ("rs_hop", 0, 0, 0, 4), ("rs_hop", 0, 1, 1, 4), ("gx", 1, 1, 1), ("gx", 1, 3, 0), ("rs_hop", 0, 2, 0, 3),
    ("rs_hop", 0, 2, 1, 4), ("gx", 1, 3, 1), ("gx", 1, 1, 0), ("rs_hop", 0, 3, 1, 2), ("rs_hop", 0, 3, 0, 3),
    ("drain", 16), ("finish", 0, 0), ("finish", 0, 1), ("gx", 1, 2, 1), ("gx", 1, 2, 0), ("rs_hop", 0, 2, 0, 4),
    ("drain", 16), ("rs_hop", 0, 3, 0, 4), ("rs_hop", 0, 3, 1, 3), ("drain", 16), ("ag_get", 0, 0, 0, 1),
    ("ag_get", 0, 0, 1, 1), ("drain", 16), ("ag_get", 0, 1, 0, 1), ("ag_get", 0, 1, 1, 1), ("drain", 16),
    ("finish", 0, 2), ("rs_hop", 0, 3, 1, 4), ("prod", 1, 0), ("ag_get", 0, 0, 1, 2), ("prod", 1, 1),
    ("ag_get", 0, 0, 0, 2), ("ag_get", 0, 1, 1, 2), ("prod", 1, 2), ("ag_get", 0, 2, 0, 1), ("ag_get", 0, 2, 1, 1),
    ("ag_get", 0, 1, 0, 2), ("finish", 0, 3), ("prod", 1, 3), ("rs_hop", 1, 0, 1, 2), ("rs_hop", 1, 0, 0, 3),
    ("rs_hop", 1, 1, 0, 2), ("ag_get", 0, 0, 1, 3), ("drain", 16), ("ag_get", 0, 0, 0, 3), ("rs_hop", 1, 1, 1, 3),
    ("rs_hop", 1, 2, 0, 3), ("ag_get", 0, 1, 1, 3), ("ag_get", 0, 2, 0, 2), ("rs_hop", 1, 2, 1, 2),
    ("ag_get", 0, 1, 0, 3), ("ag_get", 0, 2, 1, 2), ("drain", 16), ("ag_get", 0, 3, 0, 1), ("ag_get", 0, 3, 1, 1),
    ("f_mm", 0, 1), ("rs_hop", 1, 3, 0, 2), ("rs_hop", 1, 3, 1, 3), ("grad", 0, 1), ("rs_hop", 1, 0, 1, 3),
    ("rs_hop", 1, 0, 0, 4), ("f_sib", 0, 1), ("rs_hop", 1, 1, 0, 3), ("rs_hop", 1, 1, 1, 4), ("ag_get", 0, 0, 0, 4),
    ("ag_get", 0, 1, 1, 4), ("rs_hop", 1, 2, 0, 4), ("rs_hop", 1, 2, 1, 3), ("f_r1", 0, 1), ("ag_get", 0, 2, 0, 3),
    ("ag_get", 0, 2, 1, 3), ("ag_get", 0, 3, 0, 2), ("ag_get", 0, 3, 1, 2), ("f_mm", 0, 2), ("rs_hop", 1, 3, 0, 3),
    ("rs_hop", 1, 3, 1, 4), ("f_r2", 0, 1), ("grad", 0, 2), ("rs_hop", 1, 0, 1, 4), ("rs_hop", 1, 1, 0, 4),
    ("f_r3", 0, 1), ("f_sib", 0, 2), ("rs_hop", 1, 2, 1, 4), ("f_r4", 0, 1), ("ag_get", 0, 2, 0, 4),
    ("ag_get", 0, 3, 1, 3), ("f_r1", 0, 2), ("ag_get", 0, 3, 0, 3), ("f_mm", 0, 3), ("rs_hop", 1, 3, 0, 4),
    ("finish", 1, 0), ("grad", 0, 3), ("finish", 1, 1), ("finish", 1, 2), ("finish", 1, 3), ("ag_get", 0, 3, 1, 4),
    ("f_r2", 0, 2), ("f_sib", 0, 3), ("ag_get", 1, 0, 0, 1), ("ag_get", 1, 0, 1, 1), ("f_mm", 0, 4),
    ("ag_get", 1, 1, 0, 1), ("ag_get", 1, 1, 1, 1), ("f_r3", 0, 2), ("grad", 0, 4), ("ag_get", 1, 2, 0, 1),
    ("ag_get", 1, 2, 1, 1), ("f_r4", 0, 2), ("ag_get", 1, 3, 0, 1), ("ag_get", 1, 3, 1, 1), ("f_r1", 0, 3),
    ("f_sib", 0, 4), ("f_mm", 1, 1), ("ag_get", 1, 0, 0, 2), ("ag_get", 1, 0, 1, 2), ("ag_get", 1, 1, 0, 2),
    ("ag_get", 1, 1, 1, 2), ("grad", 1, 1), ("ag_get", 1, 2, 0, 2), ("ag_get", 1, 2, 1, 2), ("f_sib", 1, 1),
    ("f_r2", 0, 3), ("ag_get", 1, 3, 0, 2), ("ag_get", 1, 3, 1, 2), ("f_r1", 0, 4), ("f_mm", 1, 2),
    ("ag_get", 1, 0, 1, 3), ("ag_get", 1, 0, 0, 3), ("f_r1", 1, 1), ("grad", 1, 2), ("ag_get", 1, 1, 0, 3),
    ("ag_get", 1, 2, 1, 3), ("ag_get", 1, 1, 1, 3), ("ag_get", 1, 2, 0, 3), ("f_sib", 1, 2), ("f_r3", 0, 3),
    ("ag_get", 1, 3, 0, 3), ("ag_get", 1, 3, 1, 3), ("f_r2", 0, 4), ("f_mm", 1, 3), ("ag_get", 1, 0, 1, 4),
    ("ag_get", 1, 1, 0, 4), ("f_r2", 1, 1), ("grad", 1, 3), ("ag_get", 1, 2, 1, 4), ("ag_get", 1, 3, 0, 4),
    ("f_r3", 1, 1), ("f_r1", 1, 2), ("f_r4", 0, 3), ("f_sib", 1, 3), ("f_r3", 0, 4), ("f_mm", 1, 4), ("f_r4", 1, 1),
    ("grad", 1, 4), ("f_r2", 1, 2), ("f_sib", 1, 4), ("f_r1", 1, 3), ("f_r4", 0, 4), ("f_r3", 1, 2), ("swap", 0),
    ("f_r1", 1, 4), ("swapped", 0), ("f_r4", 1, 2), ("drain", 16), ("drain", 16), ("f_r2", 1, 3), ("drain", 16),
    ("drain", 16), ("f_r3", 1, 3), ("f_r2", 1, 4), ("drain", 16), ("f_r4", 1, 3), ("f_r3", 1, 4), ("drain", 16),
    ("drain", 16), ("f_r4", 1, 4), ("swap", 1), ("swapped", 1),
)


def gelu_parts(hidden):
    inner_arg = root_two_pi * (hidden + cubic_coef * hidden * hidden * hidden)
    bent_value = jnp.tanh(inner_arg)
    result = 0.5 * hidden * (1.0 + bent_value)
    slopes = 0.5 * (1.0 + bent_value) + 0.5 * hidden * (
        1.0 - bent_value * bent_value
    ) * root_two_pi * (1.0 + 3.0 * cubic_coef * hidden * hidden)
    return (result, slopes)


def halves(value):
    high = value.astype(BF16)
    return high, (value - high.astype(F32)).astype(BF16)


def kernel(
    tokens, up_weight, down_weight, cotangent,
    output, grad_tokens, grad_up, grad_down,
    gathered, raw, weights, partial, summed, spread, slope, fold, to_sib, from_sib,
    near, far_out, far_tok, last, ends, result, give, take, widths, grads,
    send_sem, recv_sem, local_sem,
):
    row, z, depth = lax.axis_index("row"), lax.axis_index("col"), lax.axis_index("depth")
    y, xl, xh, q = row // 2, row % 2, depth // 2, depth % 2
    xh_r, xh_l, xh_s = (xh + xl) % 2, (xh + xl + 1) % 2, (xh + xl + q) % 2
    sib = (row, z, xh * 2 + 1 - q)
    y_r, y_l = (((y + 1) % 4) * 2 + xl, z, depth), (((y + 3) % 4) * 2 + xl, z, depth)
    x_r, x_l = (y * 2 + 1 - xl, z, xh_r * 2 + q), (y * 2 + 1 - xl, z, xh_l * 2 + q)
    z_r, z_l = (row, (z + 1) % 8, depth), (row, (z + 7) % 8, depth)
    y_s = (((y + 1 + 2 * q) % 4) * 2 + xl, z, depth)
    x_s = (y * 2 + 1 - xl, z, xh_s * 2 + q)
    z_dev, z_sgn = (z_r, z_l), (1, 7)

    slots, pending = {}, []

    def remote(name, src, dst, device):
        at = slots.setdefault(name, len(slots))
        return pltpu.make_async_remote_copy(
            src_ref=src, dst_ref=dst, send_sem=send_sem.at[at], recv_sem=recv_sem.at[at],
            device_id=device, device_id_type=pl.DeviceIdType.MESH,
        )

    def send(name, src, dst, device):
        copy = remote(name, src, dst, device)
        copy.start()
        pending.append(copy)

    def arrive(name, dst):
        remote(name, dst, dst, sib).wait_recv()

    def rows(core, half):
        return pl.ds(pl.multiple_of(core * 96 + half * 48, 8), 48)

    def own_piece(a, g, dy, half):
        return gathered.at[a, g, (y + dy) % 4, rows(q, half)]

    def across_x(a, dy, half):
        piece = rows(q, half)
        src, dst = (gathered.at[a, g, (y + dy) % 4, piece] for g in range(2))
        send(("x", a, dy, half), src, dst, (x_r, x_l)[half])

    def to_core(a, g, dy, half):
        piece = own_piece(a, g, dy, half)
        send(("s", a, g, dy, half), piece, piece, sib)

    def own(a):
        loads[a].wait()
        for first in range(2):
            for way in range(2):
                half = way if first == 0 else 1 - way
                piece = own_piece(a, 0, 0, half)
                send(("y", a, way, half), piece, piece, (y_r, y_l)[way])
            if first == 0:
                for half in range(2):
                    across_x(a, 0, half)

    def gy(a, way, half):
        dy = 3 if way == 0 else 1
        piece = own_piece(a, 0, dy, half)
        arrive(("y", a, way, half), piece)
        if half == way:
            send(("yf", a, way), piece, piece, (y_r, y_l)[way])
        across_x(a, dy, half)
        to_core(a, 0, dy, half)

    def gf(a, way):
        arrive(("yf", a, way), own_piece(a, 0, 2, way))
        across_x(a, 2, way)
        to_core(a, 0, 2, way)

    def gx(a, dy, half):
        arrive(("x", a, dy, half), own_piece(a, 1, dy, half))
        to_core(a, 1, dy, half)

    def split_weights(a):
        loads[2 + a].wait()
        high, low = halves(raw[a])
        weights[a, 0:UNITS] = high
        weights[a, UNITS:2 * UNITS] = high
        weights[a, 2 * UNITS:3 * UNITS] = low

    def prod(a, u):
        for g, dy in PAIRS[u]:
            if (g, dy) != (0, 0):
                for half in range(2):
                    arrive(("s", a, g, dy, half), gathered.at[a, g, (y + dy) % 4, rows(1 - q, half)])
        high, low = halves(jnp.concatenate([gathered[a, g, (y + dy) % 4] for g, dy in PAIRS[u]], axis=0))
        w_high, w_low = weights[a, 0:UNITS], weights[a, 2 * UNITS:3 * UNITS]

        def nt(left, right):
            return lax.dot_general(left, right, (((1,), (1,)), ((), ())), preferred_element_type=F32)

        total = nt(high, w_high) + (nt(low, w_high) + nt(high, w_low))
        for j in range(2):
            partial[a, :, u, j] = total[j * BLOCK:(j + 1) * BLOCK].reshape(8, CHUNK, UNITS)
        way = (a + u) % 2
        rs_send(a, u, way, 1)
        rs_send(a, u, 1 - way, 2)

    def z_chunk(way, distance):
        return (z + z_sgn[way] * distance) % 8

    def rs_send(a, u, way, step):
        src, dst = partial.at[a, z_chunk(way, 5 - step), u], summed.at[a, way, step - 1, u]
        send(("rs", a, u, way, step), src, dst, z_dev[way])

    def rs_hop(a, u, way, step):
        arrive(("rs", a, u, way, step - 1), summed.at[a, way, step - 2, u])
        c = z_chunk(way, 5 - step)
        partial[a, c, u] = partial[a, c, u] + summed[a, way, step - 2, u]
        rs_send(a, u, way, step)

    def ag_send(a, u, way, k):
        piece = spread.at[a, z_chunk(1 - way, k - 1), u]
        send(("ag", a, u, way, k), piece, piece, z_dev[way])

    def ag_get(a, u, way, k):
        arrive(("ag", a, u, way, k), spread.at[a, z_chunk(1 - way, k), u])
        if k < 3 or (k == 3 and way == (a + u) % 2):
            ag_send(a, u, way, k + 1)

    def finish(a, u):
        for way in range(2):
            arrive(("rs", a, u, way, 4), summed.at[a, way, 3, u])
        total = partial[a, z, u] + summed[a, 0, 3, u] + summed[a, 1, 3, u]
        if a == 0:
            spread[0, z, u], slope[u] = gelu_parts(total)
        else:
            spread[1, z, u] = total * slope[u]
        for way in range(2):
            ag_send(a, u, way, 1)

    def round_chunk(r, core):
        if r == 4:
            return (z + 4 * core) % 8
        return (z + r + (8 - 2 * r) * core) % 8

    def f_mm(a, r):
        chunks = (round_chunk(r, 1 - q), round_chunk(r, q))
        high, low = halves(jnp.concatenate([spread[a, c].reshape(BLOCK, UNITS) for c in chunks], axis=0))
        total = jnp.dot(jnp.concatenate([high, low, high], axis=1), weights[1 - a], preferred_element_type=F32)
        for i, dst in enumerate((to_sib, fold)):
            for u in range(4):
                for j, (g, dy) in enumerate(PAIRS[u]):
                    at = i * BLOCK + (u * 2 + j) * CHUNK
                    for side in range(2):
                        dst[r - 1, a, side, g, (y + dy) % 4] = total[at:at + CHUNK, side * UNITS:(side + 1) * UNITS]
            if i == 0:
                send(("fs", a, r), to_sib.at[r - 1, a], from_sib.at[r - 1, a], sib)

    def f_sib(a, r):
        i = r - 1
        arrive(("fs", a, r), from_sib.at[i, a])
        fold[i, a] = fold[i, a] + from_sib[i, a]
        if a == 0:
            send(("f1", a, r, 0), fold.at[i, 0, 1 - xh, 0, 0:2], near.at[i, a, 0], x_r)
            send(("f1", a, r, 1), fold.at[i, 0, 1 - xh, 0, 2:4], near.at[i, a, 1], x_l)
        else:
            send(("f1", a, r, 0), fold.at[i, 1, 0, :, (y + 2) % 4], near.at[i, a, 0], y_r)
            send(("f1", a, r, 1), fold.at[i, 1, 1, :, (y + 2) % 4], near.at[i, a, 1], y_l)

    def f_r1(a, r):
        i = r - 1
        arrive(("f1", a, r, 0), near.at[i, a, 0])
        if a == 0:
            fold[i, 0, xh_r, 1, 0:2] = fold[i, 0, xh_r, 1, 0:2] + near[i, 0, 0]
            send(("f2", a, r, 0), fold.at[i, 0, xh_r, 1], far_out.at[i, 0], x_r)
        else:
            fold[i, 1, 0, :, (y + 1) % 4] = fold[i, 1, 0, :, (y + 1) % 4] + near[i, 1, 0]
            send(("f2", a, r, 0), fold.at[i, 1, :, :, (y + 1) % 4], far_tok.at[i, 0], y_r)
        arrive(("f1", a, r, 1), near.at[i, a, 1])
        if a == 0:
            fold[i, 0, xh_l, 1, 2:4] = fold[i, 0, xh_l, 1, 2:4] + near[i, 0, 1]
            send(("f2", a, r, 1), fold.at[i, 0, xh_l, 1], far_out.at[i, 1], x_l)
        else:
            fold[i, 1, 1, :, (y + 3) % 4] = fold[i, 1, 1, :, (y + 3) % 4] + near[i, 1, 1]
            send(("f2", a, r, 1), fold.at[i, 1, :, :, (y + 3) % 4], far_tok.at[i, 1], y_l)

    def f_r2(a, r):
        i = r - 1
        if a == 0:
            arrive(("f2", a, r, 0), far_out.at[i, 0])
            arrive(("f2", a, r, 1), far_out.at[i, 1])
            fold[i, 0, xh, 0] = fold[i, 0, xh, 0] + far_out[i, 0] + far_out[i, 1]
            send(("f3", a, r), fold.at[i, 0, xh, 0, (y + 2) % 4], last.at[i, a], y_s)
        else:
            arrive(("f2", a, r, 0), far_tok.at[i, 0])
            arrive(("f2", a, r, 1), far_tok.at[i, 1])
            fold[i, 1, :, :, y] = fold[i, 1, :, :, y] + far_tok[i, 0] + far_tok[i, 1]
            send(("f3", a, r), fold.at[i, 1, 1 - xh, 0, y], last.at[i, a], x_s)

    def f_r3(a, r):
        i = r - 1
        arrive(("f3", a, r), last.at[i, a])
        if a == 0:
            ys = (y + 1 + 2 * q) % 4
            fold[i, 0, xh, 0, ys] = fold[i, 0, xh, 0, ys] + last[i, 0]
            send(("f4", a, r, 0), fold.at[i, 0, xh, 0, (y + 1) % 4], ends.at[i, a, 0], y_r)
            send(("f4", a, r, 1), fold.at[i, 0, xh, 0, (y + 3) % 4], ends.at[i, a, 1], y_l)
        else:
            fold[i, 1, xh_s, 1, y] = fold[i, 1, xh_s, 1, y] + last[i, 1]
            send(("f4", a, r, 0), fold.at[i, 1, xh_r, 1, y], ends.at[i, a, 0], x_r)
            send(("f4", a, r, 1), fold.at[i, 1, xh_l, 1, y], ends.at[i, a, 1], x_l)

    def f_r4(a, r):
        i = r - 1
        arrive(("f4", a, r, 0), ends.at[i, a, 0])
        arrive(("f4", a, r, 1), ends.at[i, a, 1])
        result[a, i] = fold[i, a, xh, 0, y] + ends[i, a, 0] + ends[i, a, 1]

    def swap(a):
        first, second = result[a, :, :, 0:BLOCK], result[a, :, :, BLOCK:2 * BLOCK]
        lower = jnp.full(first.shape, q, jnp.int32) == 0
        give[a] = jnp.where(lower, second, first)
        send(("swap", a), give.at[a], take.at[a], sib)
        mine = jnp.where(lower, first, second)
        for r in range(1, 5):
            at = pl.ds(pl.multiple_of(round_chunk(r, q) * CHUNK, 8), CHUNK)
            widths[a, at, :] = mine[r - 1]

    def swapped(a):
        arrive(("swap", a), take.at[a])
        for r in range(1, 5):
            at = pl.ds(pl.multiple_of(round_chunk(r, 1 - q) * CHUNK, 8), CHUNK)
            widths[a, at, :] = take[a, r - 1]
        stores[a].start()

    rounds_done = [0, 0]

    def grad(a, r):
        chunks = (round_chunk(r, 0), round_chunk(r, 1))
        left = jnp.concatenate([spread[a, c].reshape(BLOCK, UNITS) for c in chunks], axis=0).T
        right = jnp.concatenate([
            gathered[1 - a, g, (y + dy) % 4, pl.ds(pl.multiple_of(c * CHUNK, 8), CHUNK), :]
            for c in chunks for pair in PAIRS for g, dy in pair
        ], axis=0)
        l_high, l_low = halves(left)
        r_high, r_low = halves(right)
        term = jnp.dot(
            jnp.concatenate([l_high, l_low, l_high], axis=1), jnp.concatenate([r_high, r_high, r_low], axis=0),
            preferred_element_type=F32)
        grads[a] = term if rounds_done[a] == 0 else grads[a] + term
        rounds_done[a] += 1
        if rounds_done[a] == 4:
            stores[2 + a].start()

    def drain(count):
        for copy in pending[:count]:
            copy.wait_send()
        del pending[:count]

    loads = [
        pltpu.make_async_copy(src, dst, local_sem.at[i])
        for i, (src, dst) in enumerate((
            (tokens, gathered.at[0, 0, y]), (cotangent, gathered.at[1, 0, y]),
            (up_weight, raw.at[0]), (down_weight, raw.at[1]),
        ))
    ]
    stores = [
        pltpu.make_async_copy(src, dst, local_sem.at[4 + i])
        for i, (src, dst) in enumerate((
            (widths.at[0], output), (widths.at[1], grad_tokens), (grads.at[0], grad_down), (grads.at[1], grad_up),
        ))
    ]
    for load in loads:
        load.start()
    barrier = pltpu.get_barrier_semaphore()
    partners = (sib, y_r, y_l, x_r, x_l, z_r, z_l)
    for device in partners:
        pl.semaphore_signal(barrier, inc=1, device_id=device, device_id_type=pl.DeviceIdType.MESH)
    pl.semaphore_wait(barrier, len(partners))

    steps = {step.__name__: step for step in (
        own, gy, gf, gx, split_weights, prod, rs_hop, finish, ag_get,
        f_mm, f_sib, f_r1, f_r2, f_r3, f_r4, swap, swapped, grad, drain)}
    for name, *at in ORDER:
        steps[name](*at)
    drain(len(pending))
    for store in stores:
        store.wait()
    assert len(slots) <= SLOTS, len(slots)


def copy_kernel(*refs):
    sources, targets, sem = refs[:4], refs[4:8], refs[8]
    copies = []
    for src, dst in zip(sources, targets):
        parts = 4 if src.shape[0] == UNITS else 1
        size = src.shape[0] // parts
        for part in range(parts):
            at = pl.ds(part * size, size)
            copies.append(pltpu.make_async_copy(src.at[at], dst.at[at], sem.at[len(copies)]))
    for copy in copies:
        copy.start()
    for copy in copies:
        copy.wait()


def shards(tokens, up_weight, down_weight, cotangent):
    anywhere, piece = pl.BlockSpec(memory_space=pl.ANY), (CHUNK, UNITS)
    shapes = (
        jax.ShapeDtypeStruct((BLOCK, BLOCK), F32),
        jax.ShapeDtypeStruct((BLOCK, BLOCK), F32),
        jax.ShapeDtypeStruct((UNITS, WIDTH), F32),
        jax.ShapeDtypeStruct((UNITS, WIDTH), F32),
    )
    results = pl.pallas_call(
        kernel,
        out_shape=shapes,
        in_specs=[anywhere] * 4,
        out_specs=(anywhere,) * 4,
        scratch_shapes=[
            pltpu.VMEM((2, 2, 4, BLOCK, WIDTH), F32),
            pltpu.VMEM((2, UNITS, WIDTH), F32),
            pltpu.VMEM((2, 3 * UNITS, WIDTH), BF16),
            pltpu.VMEM((2, 8, 4, 2) + piece, F32),
            pltpu.VMEM((2, 2, 4, 4, 2) + piece, F32),
            pltpu.VMEM((2, 8, 4, 2) + piece, F32),
            pltpu.VMEM((4, 2) + piece, F32),
            pltpu.VMEM((4, 2, 2, 2, 4) + piece, F32),
            pltpu.VMEM((4, 2, 2, 2, 4) + piece, F32),
            pltpu.VMEM((4, 2, 2, 2, 4) + piece, F32),
            pltpu.VMEM((4, 2, 2, 2) + piece, F32),
            pltpu.VMEM((4, 2, 4) + piece, F32),
            pltpu.VMEM((4, 2, 2, 2) + piece, F32),
            pltpu.VMEM((4, 2) + piece, F32),
            pltpu.VMEM((4, 2, 2) + piece, F32),
            pltpu.VMEM((2, 4) + piece, F32),
            pltpu.VMEM((2, 4, CHUNK, BLOCK), F32),
            pltpu.VMEM((2, 4, CHUNK, BLOCK), F32),
            pltpu.VMEM((2, BLOCK, BLOCK), F32),
            pltpu.VMEM((2, UNITS, WIDTH), F32),
            pltpu.SemaphoreType.DMA((SLOTS,)),
            pltpu.SemaphoreType.DMA((SLOTS,)),
            pltpu.SemaphoreType.DMA((8,)),
        ],
        compiler_params=pltpu.CompilerParams(
            collective_id=0, has_side_effects=True, vmem_limit_bytes=62 * 1024 * 1024),
        cost_estimate=pl.CostEstimate(flops=16_300_000_000, bytes_accessed=6_000_000, transcendentals=73728),
    )(tokens, up_weight, down_weight, cotangent)
    return pl.pallas_call(
        copy_kernel,
        out_shape=shapes,
        in_specs=[anywhere] * 4,
        out_specs=(anywhere,) * 4,
        scratch_shapes=[pltpu.SemaphoreType.DMA((10,))],
    )(*results)


def solution(mesh):
    return jax.shard_map(
        shards,
        mesh=mesh,
        in_specs=(
            P("row", "col"),
            P(("row", "depth"), "col"),
            P(("row", "depth"), "col"),
            P("row", "col"),
        ),
        out_specs=(
            P("row", ("col", "depth")),
            P("row", ("col", "depth")),
            P(("row", "depth"), "col"),
            P(("row", "depth"), "col"),
        ),
        check_vma=False,
    )
```

```python
import jax
import jax.numpy as jnp
from jax import lax
from jax.experimental import pallas as pl
from jax.experimental.pallas import tpu as pltpu
from jax.sharding import PartitionSpec as P

F32, BF16 = jnp.float32, jnp.bfloat16
root_two_pi = 0.7978845608028654
cubic_coef = 0.044715

SLOTS = 260
BLOCK, WIDTH, UNITS, CHUNK = 192, 768, 384, 24
PAIRS = (
    ((0, 0, 0), (1, 0, 0)), ((0, 1, 0), (1, 1, 0)),
    ((0, 0, 1), (0, 0, 3)), ((0, 1, 1), (0, 1, 3)), ((0, 0, 2), (0, 1, 2)),
    ((1, 0, 1), (1, 0, 3)), ((1, 1, 1), (1, 1, 3)), ((1, 0, 2), (1, 1, 2)),
)
PLACE = {block: (u, j) for u, pair in enumerate(PAIRS) for j, block in enumerate(pair)}
BLOCKS = tuple((g, dy) for g in range(2) for dy in range(4))
Y_FIRST = ((0, 1, 0, 1), (0, 0, 0, 1))
(
    OWN_X, OWN_Y, GY, GF, GX, SPLIT_WEIGHTS, PROD, RS_HOP, FINISH, AG_GET, F_MM, F_SIB, F_R1, F_R2, F_R3, F_R4,
    SWAP, SWAPPED, GRAD, DRAIN,
) = range(20)
ORDER = (
    (OWN_Y, 0), (OWN_X, 0), (OWN_X, 1), (SPLIT_WEIGHTS, 0), (SPLIT_WEIGHTS, 1), (PROD, 0), (GY, 0, 0, 0),
    (GY, 0, 1, 1), (GX, 0, 0, 0), (GX, 0, 0, 1), (RS_HOP, 0, 0, 2), (RS_HOP, 0, 1, 3), (GY, 0, 0, 1), (GY, 0, 1, 0),
    (GX, 1, 0, 0), (GX, 1, 0, 1), (OWN_Y, 1), (RS_HOP, 0, 0, 3), (RS_HOP, 0, 1, 4), (PROD, 2), (PROD, 1),
    (GX, 0, 1, 1), (GF, 0, 1), (RS_HOP, 0, 0, 4), (GF, 0, 0), (GX, 0, 3, 0), (RS_HOP, 2, 0, 2), (RS_HOP, 2, 1, 3),
    (GY, 1, 0, 0), (GX, 0, 1, 0), (GY, 1, 1, 1), (GX, 0, 3, 1), (DRAIN, 16), (RS_HOP, 1, 1, 2), (RS_HOP, 1, 0, 3),
    (PROD, 3), (RS_HOP, 2, 1, 4), (FINISH, 0), (RS_HOP, 1, 1, 3), (GX, 0, 2, 0), (GX, 0, 2, 1), (RS_HOP, 2, 0, 3),
    (GY, 1, 1, 0), (GY, 1, 0, 1), (DRAIN, 16), (RS_HOP, 1, 0, 4), (PROD, 4), (GF, 1, 0), (RS_HOP, 3, 0, 3),
    (GF, 1, 1), (RS_HOP, 3, 1, 2), (GX, 1, 3, 0), (GX, 1, 1, 1), (AG_GET, 0, 0, 1), (AG_GET, 0, 1, 1), (GX, 1, 3, 1),
    (GX, 1, 1, 0), (DRAIN, 16), (RS_HOP, 2, 0, 4), (RS_HOP, 1, 1, 4), (DRAIN, 16), (RS_HOP, 4, 1, 3), (GX, 1, 2, 0),
    (GX, 1, 2, 1), (RS_HOP, 4, 0, 2), (RS_HOP, 3, 1, 3), (RS_HOP, 3, 0, 4), (AG_GET, 0, 1, 2), (DRAIN, 16),
    (AG_GET, 0, 0, 2), (FINISH, 1), (FINISH, 2), (RS_HOP, 4, 1, 4), (RS_HOP, 4, 0, 3), (RS_HOP, 3, 1, 4),
    (AG_GET, 0, 1, 3), (AG_GET, 0, 0, 3), (AG_GET, 1, 1, 1), (AG_GET, 1, 0, 1), (AG_GET, 2, 1, 1), (AG_GET, 2, 0, 1),
    (RS_HOP, 4, 0, 4), (FINISH, 3), (DRAIN, 16), (AG_GET, 0, 0, 4), (AG_GET, 1, 1, 2), (AG_GET, 1, 0, 2),
    (AG_GET, 2, 1, 2), (AG_GET, 2, 0, 2), (AG_GET, 3, 1, 1), (FINISH, 4), (AG_GET, 1, 1, 3), (PROD, 7),
    (AG_GET, 3, 0, 1), (PROD, 6), (AG_GET, 3, 1, 2), (AG_GET, 1, 0, 3), (PROD, 5), (AG_GET, 2, 0, 3),
    (AG_GET, 4, 1, 1), (AG_GET, 2, 1, 3), (AG_GET, 4, 0, 1), (F_MM, 0, 1), (RS_HOP, 7, 0, 3), (AG_GET, 1, 1, 4),
    (GRAD, 0, 1), (AG_GET, 3, 0, 2), (F_SIB, 0, 1), (RS_HOP, 7, 1, 2), (RS_HOP, 6, 1, 3), (RS_HOP, 6, 0, 2),
    (AG_GET, 3, 1, 3), (DRAIN, 16), (RS_HOP, 5, 0, 3), (RS_HOP, 5, 1, 2), (F_R1, 0, 1), (AG_GET, 2, 0, 4),
    (AG_GET, 4, 1, 2), (AG_GET, 4, 0, 2), (F_MM, 0, 2), (RS_HOP, 7, 1, 3), (RS_HOP, 7, 0, 4), (RS_HOP, 6, 1, 4),
    (GRAD, 0, 2), (AG_GET, 3, 0, 3), (AG_GET, 3, 1, 4), (F_R2, 0, 1), (F_SIB, 0, 2), (RS_HOP, 6, 0, 3),
    (RS_HOP, 5, 1, 3), (DRAIN, 16), (RS_HOP, 5, 0, 4), (F_R3, 0, 1), (AG_GET, 4, 1, 3), (AG_GET, 4, 0, 3),
    (F_MM, 0, 3), (RS_HOP, 7, 1, 4), (GRAD, 0, 3), (RS_HOP, 6, 0, 4), (RS_HOP, 5, 1, 4), (F_R4, 0, 1), (F_R1, 0, 2),
    (F_SIB, 0, 3), (FINISH, 7), (DRAIN, 16), (AG_GET, 4, 0, 4), (F_MM, 0, 4), (FINISH, 5), (FINISH, 6),
    (AG_GET, 7, 1, 1), (F_R2, 0, 2), (F_R1, 0, 3), (AG_GET, 7, 0, 1), (F_SIB, 0, 4), (GRAD, 0, 4), (F_R3, 0, 2),
    (AG_GET, 5, 1, 1), (AG_GET, 5, 0, 1), (AG_GET, 6, 0, 1), (AG_GET, 6, 1, 1), (F_MM, 1, 1), (AG_GET, 7, 0, 2),
    (AG_GET, 7, 1, 2), (F_R2, 0, 3), (F_R1, 0, 4), (F_R4, 0, 2), (GRAD, 1, 1), (AG_GET, 5, 1, 2), (AG_GET, 6, 0, 2),
    (AG_GET, 6, 1, 2), (AG_GET, 5, 0, 2), (F_SIB, 1, 1), (F_MM, 1, 2), (AG_GET, 7, 1, 3), (F_R3, 0, 3), (F_R2, 0, 4),
    (AG_GET, 7, 0, 3), (GRAD, 1, 2), (AG_GET, 5, 1, 3), (AG_GET, 6, 0, 3), (F_R4, 0, 3), (AG_GET, 5, 0, 3),
    (AG_GET, 6, 1, 3), (F_R1, 1, 1), (F_SIB, 1, 2), (F_R3, 0, 4), (AG_GET, 7, 1, 4), (F_MM, 1, 3), (AG_GET, 5, 1, 4),
    (AG_GET, 6, 0, 4), (F_MM, 1, 4), (F_SIB, 1, 3), (GRAD, 1, 3), (F_SIB, 1, 4), (F_R1, 1, 2), (F_R4, 0, 4),
    (F_R2, 1, 1), (SWAP, 0), (GRAD, 1, 4), (F_R1, 1, 4), (F_R1, 1, 3), (SWAPPED, 0), (F_R3, 1, 1), (DRAIN, 16),
    (F_R2, 1, 2), (DRAIN, 16), (DRAIN, 16), (DRAIN, 16), (F_R2, 1, 4), (F_R2, 1, 3), (F_R4, 1, 1), (F_R3, 1, 2),
    (F_R3, 1, 4), (F_R3, 1, 3), (DRAIN, 16), (F_R4, 1, 2), (F_R4, 1, 4), (F_R4, 1, 3), (SWAP, 1), (SWAPPED, 1),
)


def gelu_parts(hidden):
    inner_arg = root_two_pi * (hidden + cubic_coef * hidden * hidden * hidden)
    bent_value = jnp.tanh(inner_arg)
    result = 0.5 * hidden * (1.0 + bent_value)
    slopes = 0.5 * (1.0 + bent_value) + 0.5 * hidden * (
        1.0 - bent_value * bent_value
    ) * root_two_pi * (1.0 + 3.0 * cubic_coef * hidden * hidden)
    return (result, slopes)


def halves(value):
    high = value.astype(BF16)
    return high, (value - high.astype(F32)).astype(BF16)


def kernel(
    tokens, up_weight, down_weight, cotangent,
    output, grad_tokens, grad_up, grad_down,
    gathered, raw, weights, partial, summed, spread, slope, fold, to_sib, from_sib,
    near, far_x, far_y, last, ends, result, give, take, widths, grads,
    send_sem, recv_sem, local_sem,
):
    row, z, depth = lax.axis_index("row"), lax.axis_index("col"), lax.axis_index("depth")
    y, xl, xh, q = row // 2, row % 2, depth // 2, depth % 2
    xh_r, xh_l, xh_s = (xh + xl) % 2, (xh + xl + 1) % 2, (xh + xl + q) % 2
    sib = (row, z, xh * 2 + 1 - q)
    y_r, y_l = (((y + 1) % 4) * 2 + xl, z, depth), (((y + 3) % 4) * 2 + xl, z, depth)
    x_r, x_l = (y * 2 + 1 - xl, z, xh_r * 2 + q), (y * 2 + 1 - xl, z, xh_l * 2 + q)
    z_r, z_l = (row, (z + 1) % 8, depth), (row, (z + 7) % 8, depth)
    y_s = (((y + 1 + 2 * q) % 4) * 2 + xl, z, depth)
    x_s = (y * 2 + 1 - xl, z, xh_s * 2 + q)
    z_dev, z_sgn = (z_r, z_l), (1, 7)

    slots, pending = {}, []

    def remote(name, src, dst, device):
        at = slots.setdefault(name, len(slots))
        return pltpu.make_async_remote_copy(
            src_ref=src, dst_ref=dst, send_sem=send_sem.at[at], recv_sem=recv_sem.at[at],
            device_id=device, device_id_type=pl.DeviceIdType.MESH,
        )

    def send(name, src, dst, device):
        copy = remote(name, src, dst, device)
        copy.start()
        pending.append(copy)

    def arrive(name, dst):
        remote(name, dst, dst, sib).wait_recv()

    def rows(core, half):
        return pl.ds(pl.multiple_of(core * 96 + half * 48, 8), 48)

    def own_piece(a, g, dy, half):
        return gathered.at[a, g, (y + dy) % 4, rows(q, half)]

    def across_x(a, dy, half):
        piece = rows(q, half)
        src, dst = (gathered.at[a, g, (y + dy) % 4, piece] for g in range(2))
        send(("x", a, dy, half), src, dst, (x_r, x_l)[half])

    def to_core(a, g, dy, half):
        piece = own_piece(a, g, dy, half)
        send(("s", a, g, dy, half), piece, piece, sib)

    def own_x(a):
        if a == 1:
            loads[a].wait()
        for half in range(2):
            across_x(a, 0, half)

    def own_y(a):
        if a == 0:
            loads[a].wait()
        for halves_of in ((0, 1), (1, 0)):
            for way in range(2):
                piece = own_piece(a, 0, 0, halves_of[way])
                send(("y", a, way, halves_of[way]), piece, piece, (y_r, y_l)[way])

    def gy(a, way, half):
        dy = 3 if way == 0 else 1
        piece = own_piece(a, 0, dy, half)
        arrive(("y", a, way, half), piece)
        if half == way:
            send(("yf", a, way), piece, piece, (y_r, y_l)[way])
        across_x(a, dy, half)
        to_core(a, 0, dy, half)

    def gf(a, way):
        arrive(("yf", a, way), own_piece(a, 0, 2, way))
        across_x(a, 2, way)
        to_core(a, 0, 2, way)

    def gx(a, dy, half):
        arrive(("x", a, dy, half), own_piece(a, 1, dy, half))
        to_core(a, 1, dy, half)

    def split_weights(a):
        loads[2 + a].wait()
        high, low = halves(raw[a])
        weights[a, 0:UNITS] = high
        weights[a, UNITS:2 * UNITS] = high
        weights[a, 2 * UNITS:3 * UNITS] = low

    def prod(u):
        def nt(left, right):
            return lax.dot_general(left, right, (((1,), (1,)), ((), ())), preferred_element_type=F32)

        def product(a, blocks):
            high, low = halves(jnp.concatenate([gathered[a, g, (y + dy) % 4] for g, dy in blocks], axis=0))
            w_high, w_low = weights[a, 0:UNITS], weights[a, 2 * UNITS:3 * UNITS]
            return nt(high, w_high) + (nt(low, w_high) + nt(high, w_low))

        for a, g, dy in PAIRS[u]:
            if (g, dy) != (0, 0):
                for half in range(2):
                    arrive(("s", a, g, dy, half), gathered.at[a, g, (y + dy) % 4, rows(1 - q, half)])
        (a, *first), (b, *second) = PAIRS[u]
        if a == b:
            total = product(a, (first, second))
            parts = total[0:BLOCK], total[BLOCK:2 * BLOCK]
        else:
            parts = product(a, (first,)), product(b, (second,))
        for j, part in enumerate(parts):
            partial[:, u, j] = part.reshape(8, CHUNK, UNITS)
        rs_send(u, u % 2, 1)
        rs_send(u, 1 - u % 2, 2)

    def z_chunk(way, distance):
        return (z + z_sgn[way] * distance) % 8

    def rs_send(u, way, step):
        src, dst = partial.at[z_chunk(way, 5 - step), u], summed.at[way, step - 1, u]
        send(("rs", u, way, step), src, dst, z_dev[way])

    def rs_hop(u, way, step):
        arrive(("rs", u, way, step - 1), summed.at[way, step - 2, u])
        c = z_chunk(way, 5 - step)
        partial[c, u] = partial[c, u] + summed[way, step - 2, u]
        rs_send(u, way, step)

    def ag_send(u, way, k):
        piece = spread.at[z_chunk(1 - way, k - 1), u]
        send(("ag", u, way, k), piece, piece, z_dev[way])

    def ag_get(u, way, k):
        arrive(("ag", u, way, k), spread.at[z_chunk(1 - way, k), u])
        if k < 3 or (k == 3 and way == u % 2):
            ag_send(u, way, k + 1)

    def finish(u):
        for way in range(2):
            arrive(("rs", u, way, 4), summed.at[way, 3, u])
        for j, (a, g, dy) in enumerate(PAIRS[u]):
            total = partial[z, u, j] + summed[0, 3, u, j] + summed[1, 3, u, j]
            if a == 0:
                spread[z, u, j], slope[g, dy] = gelu_parts(total)
            else:
                spread[z, u, j] = total * slope[g, dy]
        for way in range(2):
            ag_send(u, way, 1)

    def spread_rows(a, chunks):
        places = [PLACE[(a, g, dy)] for g, dy in BLOCKS]
        return jnp.concatenate([spread[c, u, j] for c in chunks for u, j in places], axis=0)

    def round_chunk(r, core):
        if r == 4:
            return (z + 4 * core) % 8
        return (z + r + (8 - 2 * r) * core) % 8

    def f_mm(a, r):
        high, low = halves(spread_rows(a, (round_chunk(r, 1 - q), round_chunk(r, q))))
        total = jnp.dot(jnp.concatenate([high, low, high], axis=1), weights[1 - a], preferred_element_type=F32)
        for i, dst in enumerate((to_sib, fold)):
            for n, (g, dy) in enumerate(BLOCKS):
                at = i * BLOCK + n * CHUNK
                for side in range(2):
                    dst[r - 1, a, side, g, (y + dy) % 4] = total[at:at + CHUNK, side * UNITS:(side + 1) * UNITS]
            if i == 0:
                send(("fs", a, r), to_sib.at[r - 1, a], from_sib.at[r - 1, a], sib)

    def f_sib(a, r):
        i = r - 1
        arrive(("fs", a, r), from_sib.at[i, a])
        fold[i, a] = fold[i, a] + from_sib[i, a]
        if Y_FIRST[a][i]:
            send(("f1", a, r, 0), fold.at[i, a, 0, :, (y + 2) % 4], near.at[i, a, 0], y_r)
            send(("f1", a, r, 1), fold.at[i, a, 1, :, (y + 2) % 4], near.at[i, a, 1], y_l)
        else:
            send(("f1", a, r, 0), fold.at[i, a, 1 - xh, 0, 0:2], near.at[i, a, 0], x_r)
            send(("f1", a, r, 1), fold.at[i, a, 1 - xh, 0, 2:4], near.at[i, a, 1], x_l)

    def f_r1(a, r):
        i = r - 1
        for way, yy, xx in ((0, (y + 1) % 4, xh_r), (1, (y + 3) % 4, xh_l)):
            arrive(("f1", a, r, way), near.at[i, a, way])
            if Y_FIRST[a][i]:
                fold[i, a, way, :, yy] = fold[i, a, way, :, yy] + near[i, a, way]
                send(("f2", a, r, way), fold.at[i, a, :, :, yy], far_y.at[i, a, way], (y_r, y_l)[way])
            else:
                half = slice(2 * way, 2 * way + 2)
                fold[i, a, xx, 1, half] = fold[i, a, xx, 1, half] + near[i, a, way]
                send(("f2", a, r, way), fold.at[i, a, xx, 1], far_x.at[i, a, way], (x_r, x_l)[way])

    def f_r2(a, r):
        i = r - 1
        far = (far_x, far_y)[Y_FIRST[a][i]]
        for way in range(2):
            arrive(("f2", a, r, way), far.at[i, a, way])
        if Y_FIRST[a][i]:
            fold[i, a, :, :, y] = fold[i, a, :, :, y] + far[i, a, 0] + far[i, a, 1]
            send(("f3", a, r), fold.at[i, a, 1 - xh, 0, y], last.at[i, a], x_s)
        else:
            fold[i, a, xh, 0] = fold[i, a, xh, 0] + far[i, a, 0] + far[i, a, 1]
            send(("f3", a, r), fold.at[i, a, xh, 0, (y + 2) % 4], last.at[i, a], y_s)

    def f_r3(a, r):
        i = r - 1
        arrive(("f3", a, r), last.at[i, a])
        if Y_FIRST[a][i]:
            fold[i, a, xh_s, 1, y] = fold[i, a, xh_s, 1, y] + last[i, a]
            send(("f4", a, r, 0), fold.at[i, a, xh_r, 1, y], ends.at[i, a, 0], x_r)
            send(("f4", a, r, 1), fold.at[i, a, xh_l, 1, y], ends.at[i, a, 1], x_l)
        else:
            ys = (y + 1 + 2 * q) % 4
            fold[i, a, xh, 0, ys] = fold[i, a, xh, 0, ys] + last[i, a]
            send(("f4", a, r, 0), fold.at[i, a, xh, 0, (y + 1) % 4], ends.at[i, a, 0], y_r)
            send(("f4", a, r, 1), fold.at[i, a, xh, 0, (y + 3) % 4], ends.at[i, a, 1], y_l)

    def f_r4(a, r):
        i = r - 1
        arrive(("f4", a, r, 0), ends.at[i, a, 0])
        arrive(("f4", a, r, 1), ends.at[i, a, 1])
        result[a, i] = fold[i, a, xh, 0, y] + ends[i, a, 0] + ends[i, a, 1]

    def swap(a):
        first, second = result[a, :, :, 0:BLOCK], result[a, :, :, BLOCK:2 * BLOCK]
        lower = jnp.full(first.shape, q, jnp.int32) == 0
        give[a] = jnp.where(lower, second, first)
        send(("swap", a), give.at[a], take.at[a], sib)
        mine = jnp.where(lower, first, second)
        for r in range(1, 5):
            at = pl.ds(pl.multiple_of(round_chunk(r, q) * CHUNK, 8), CHUNK)
            widths[a, at, :] = mine[r - 1]

    def swapped(a):
        arrive(("swap", a), take.at[a])
        for r in range(1, 5):
            at = pl.ds(pl.multiple_of(round_chunk(r, 1 - q) * CHUNK, 8), CHUNK)
            widths[a, at, :] = take[a, r - 1]
        stores[a].start()

    rounds_done = [0, 0]

    def grad(a, r):
        chunks = (round_chunk(r, 0), round_chunk(r, 1))
        left = spread_rows(a, chunks).T
        right = jnp.concatenate([
            gathered[1 - a, g, (y + dy) % 4, pl.ds(pl.multiple_of(c * CHUNK, 8), CHUNK), :]
            for c in chunks for g, dy in BLOCKS
        ], axis=0)
        l_high, l_low = halves(left)
        r_high, r_low = halves(right)
        term = jnp.dot(
            jnp.concatenate([l_high, l_low, l_high], axis=1), jnp.concatenate([r_high, r_high, r_low], axis=0),
            preferred_element_type=F32)
        grads[a] = term if rounds_done[a] == 0 else grads[a] + term
        rounds_done[a] += 1
        if rounds_done[a] == 4:
            stores[2 + a].start()

    def drain(count):
        for copy in pending[:count]:
            copy.wait_send()
        del pending[:count]

    loads = [
        pltpu.make_async_copy(src, dst, local_sem.at[i])
        for i, (src, dst) in enumerate((
            (tokens, gathered.at[0, 0, y]), (cotangent, gathered.at[1, 0, y]),
            (up_weight, raw.at[0]), (down_weight, raw.at[1]),
        ))
    ]
    stores = [
        pltpu.make_async_copy(src, dst, local_sem.at[4 + i])
        for i, (src, dst) in enumerate((
            (widths.at[0], output), (widths.at[1], grad_tokens), (grads.at[0], grad_down), (grads.at[1], grad_up),
        ))
    ]
    for load in loads:
        load.start()
    barrier = pltpu.get_barrier_semaphore()
    partners = (sib, y_r, y_l, x_r, x_l, z_r, z_l)
    for device in partners:
        pl.semaphore_signal(barrier, inc=1, device_id=device, device_id_type=pl.DeviceIdType.MESH)
    pl.semaphore_wait(barrier, len(partners))

    steps = (
        own_x, own_y, gy, gf, gx, split_weights, prod, rs_hop, finish, ag_get,
        f_mm, f_sib, f_r1, f_r2, f_r3, f_r4, swap, swapped, grad, drain,
    )
    for step, *at in ORDER:
        steps[step](*at)
    drain(len(pending))
    for store in stores:
        store.wait()
    assert len(slots) <= SLOTS, len(slots)


def copy_kernel(*refs):
    sources, targets, held, sem = refs[:4], refs[4:8], refs[8:12], refs[12]
    loads, stores = [], []
    for src, dst, hold in zip(sources, targets, held):
        parts = 4 if src.shape[0] == UNITS else 1
        size = src.shape[0] // parts
        for part in range(parts):
            at, n = pl.ds(part * size, size), len(loads)
            loads.append(pltpu.make_async_copy(src.at[at], hold.at[at], sem.at[0, n]))
            stores.append(pltpu.make_async_copy(hold.at[at], dst.at[at], sem.at[1, n]))
    for load in loads:
        load.start()
    for load, store in zip(loads, stores):
        load.wait()
        store.start()
    for store in stores:
        store.wait()


def shards(tokens, up_weight, down_weight, cotangent):
    anywhere, piece = pl.BlockSpec(memory_space=pl.ANY), (CHUNK, UNITS)
    shapes = (
        jax.ShapeDtypeStruct((BLOCK, BLOCK), F32),
        jax.ShapeDtypeStruct((BLOCK, BLOCK), F32),
        jax.ShapeDtypeStruct((UNITS, WIDTH), F32),
        jax.ShapeDtypeStruct((UNITS, WIDTH), F32),
    )
    results = pl.pallas_call(
        kernel,
        out_shape=shapes,
        in_specs=[anywhere] * 4,
        out_specs=(anywhere,) * 4,
        scratch_shapes=[
            pltpu.VMEM((2, 2, 4, BLOCK, WIDTH), F32),
            pltpu.VMEM((2, UNITS, WIDTH), F32),
            pltpu.VMEM((2, 3 * UNITS, WIDTH), BF16),
            pltpu.VMEM((8, 8, 2) + piece, F32),
            pltpu.VMEM((2, 4, 8, 2) + piece, F32),
            pltpu.VMEM((8, 8, 2) + piece, F32),
            pltpu.VMEM((2, 4) + piece, F32),
            pltpu.VMEM((4, 2, 2, 2, 4) + piece, F32),
            pltpu.VMEM((4, 2, 2, 2, 4) + piece, F32),
            pltpu.VMEM((4, 2, 2, 2, 4) + piece, F32),
            pltpu.VMEM((4, 2, 2, 2) + piece, F32),
            pltpu.VMEM((4, 2, 2, 4) + piece, F32),
            pltpu.VMEM((4, 2, 2, 2, 2) + piece, F32),
            pltpu.VMEM((4, 2) + piece, F32),
            pltpu.VMEM((4, 2, 2) + piece, F32),
            pltpu.VMEM((2, 4) + piece, F32),
            pltpu.VMEM((2, 4, CHUNK, BLOCK), F32),
            pltpu.VMEM((2, 4, CHUNK, BLOCK), F32),
            pltpu.VMEM((2, BLOCK, BLOCK), F32),
            pltpu.VMEM((2, UNITS, WIDTH), F32),
            pltpu.SemaphoreType.DMA((SLOTS,)),
            pltpu.SemaphoreType.DMA((SLOTS,)),
            pltpu.SemaphoreType.DMA((8,)),
        ],
        compiler_params=pltpu.CompilerParams(
            collective_id=0, has_side_effects=True, vmem_limit_bytes=62 * 1024 * 1024),
        cost_estimate=pl.CostEstimate(flops=16_300_000_000, bytes_accessed=6_000_000, transcendentals=73728),
    )(tokens, up_weight, down_weight, cotangent)
    return pl.pallas_call(
        copy_kernel,
        out_shape=shapes,
        in_specs=[anywhere] * 4,
        out_specs=(anywhere,) * 4,
        scratch_shapes=[pltpu.VMEM(shape.shape, F32) for shape in shapes] + [pltpu.SemaphoreType.DMA((2, 10))],
    )(*results)


def solution(mesh):
    return jax.shard_map(
        shards,
        mesh=mesh,
        in_specs=(
            P("row", "col"),
            P(("row", "depth"), "col"),
            P(("row", "depth"), "col"),
            P("row", "col"),
        ),
        out_specs=(
            P("row", ("col", "depth")),
            P("row", ("col", "depth")),
            P(("row", "depth"), "col"),
            P(("row", "depth"), "col"),
        ),
        check_vma=False,
    )
```

```python
import jax
import jax.numpy as jnp
from jax import lax
from jax.experimental import pallas as pl
from jax.experimental.pallas import tpu as pltpu
from jax.sharding import PartitionSpec as P

F32, BF16 = jnp.float32, jnp.bfloat16
root_two_pi = 0.7978845608028654
cubic_coef = 0.044715

SLOTS = 260
BLOCK, WIDTH, UNITS, CHUNK = 192, 768, 384, 24
PAIRS = (
    ((0, 0, 0), (1, 0, 0)), ((0, 1, 0), (1, 1, 0)),
    ((0, 0, 1), (0, 0, 3)), ((0, 1, 1), (0, 1, 3)), ((0, 0, 2), (0, 1, 2)),
    ((1, 0, 1), (1, 0, 3)), ((1, 1, 1), (1, 1, 3)), ((1, 0, 2), (1, 1, 2)),
)
PLACE = {block: (u, j) for u, pair in enumerate(PAIRS) for j, block in enumerate(pair)}
BLOCKS = tuple((g, dy) for g in range(2) for dy in range(4))
(
    OWN_X, OWN_Y, GY, GF, GX, SPLIT_WEIGHTS, PROD, RS_HOP, FINISH, AG_GET, F_MM, F_SIB, F_R1, F_R2, F_R3, SWAP,
    SWAPPED, GRAD, DRAIN,
) = range(19)
ORDER = (
    (OWN_Y, 0), (OWN_X, 0), (OWN_X, 1), (SPLIT_WEIGHTS, 1), (SPLIT_WEIGHTS, 0), (PROD, 0), (GY, 0, 0, 0),
    (GX, 0, 0, 0), (GX, 0, 0, 1), (GY, 0, 1, 1), (RS_HOP, 0, 0, 2), (RS_HOP, 0, 1, 3), (GY, 0, 0, 1), (GY, 0, 1, 0),
    (OWN_Y, 1), (GX, 1, 0, 0), (GX, 1, 0, 1), (RS_HOP, 0, 0, 3), (RS_HOP, 0, 1, 4), (PROD, 2), (PROD, 1),
    (RS_HOP, 0, 0, 4), (GF, 0, 1), (GX, 0, 1, 1), (GX, 0, 3, 0), (GF, 0, 0), (RS_HOP, 2, 0, 2), (RS_HOP, 2, 1, 3),
    (GY, 1, 0, 0), (GX, 0, 1, 0), (GX, 0, 3, 1), (GY, 1, 1, 1), (DRAIN, 16), (RS_HOP, 1, 1, 2), (RS_HOP, 1, 0, 3),
    (PROD, 3), (RS_HOP, 2, 1, 4), (GX, 0, 2, 0), (FINISH, 0), (GX, 0, 2, 1), (RS_HOP, 2, 0, 3), (RS_HOP, 1, 1, 3),
    (GY, 1, 1, 0), (GY, 1, 0, 1), (PROD, 4), (GX, 1, 3, 0), (GF, 1, 1), (GF, 1, 0), (RS_HOP, 3, 0, 3), (GX, 1, 1, 1),
    (RS_HOP, 1, 0, 4), (RS_HOP, 3, 1, 2), (DRAIN, 16), (AG_GET, 0, 0, 1), (AG_GET, 0, 1, 1), (GX, 1, 3, 1),
    (GX, 1, 1, 0), (DRAIN, 16), (RS_HOP, 2, 0, 4), (RS_HOP, 1, 1, 4), (DRAIN, 16), (RS_HOP, 4, 0, 2),
    (RS_HOP, 4, 1, 3), (GX, 1, 2, 1), (GX, 1, 2, 0), (RS_HOP, 3, 0, 4), (RS_HOP, 3, 1, 3), (AG_GET, 0, 1, 2),
    (DRAIN, 16), (AG_GET, 0, 0, 2), (FINISH, 1), (FINISH, 2), (RS_HOP, 4, 1, 4), (RS_HOP, 4, 0, 3), (RS_HOP, 3, 1, 4),
    (AG_GET, 0, 1, 3), (AG_GET, 0, 0, 3), (AG_GET, 1, 1, 1), (AG_GET, 1, 0, 1), (AG_GET, 2, 1, 1), (AG_GET, 2, 0, 1),
    (RS_HOP, 4, 0, 4), (FINISH, 3), (DRAIN, 16), (AG_GET, 0, 0, 4), (AG_GET, 1, 1, 2), (AG_GET, 1, 0, 2),
    (AG_GET, 2, 1, 2), (AG_GET, 2, 0, 2), (AG_GET, 3, 1, 1), (FINISH, 4), (PROD, 5), (AG_GET, 1, 1, 3),
    (AG_GET, 3, 0, 1), (PROD, 6), (AG_GET, 3, 1, 2), (PROD, 7), (AG_GET, 4, 1, 1), (AG_GET, 2, 0, 3),
    (AG_GET, 2, 1, 3), (AG_GET, 1, 0, 3), (F_MM, 0, 4, 0), (RS_HOP, 5, 1, 2), (AG_GET, 4, 0, 1), (F_MM, 0, 1, 0, 1),
    (AG_GET, 1, 1, 4), (RS_HOP, 5, 0, 3), (GRAD, 0, 1), (AG_GET, 3, 0, 2), (F_SIB, 0, 1), (RS_HOP, 6, 0, 2),
    (RS_HOP, 6, 1, 3), (AG_GET, 3, 1, 3), (DRAIN, 16), (RS_HOP, 7, 0, 3), (RS_HOP, 7, 1, 2), (F_R1, 0, 1),
    (AG_GET, 2, 0, 4), (AG_GET, 4, 1, 2), (AG_GET, 4, 0, 2), (GRAD, 0, 2), (F_R2, 0, 1), (RS_HOP, 5, 1, 3),
    (RS_HOP, 6, 1, 4), (RS_HOP, 5, 0, 4), (F_MM, 0, 2, 0, 1), (AG_GET, 3, 1, 4), (AG_GET, 3, 0, 3), (F_R3, 0, 1),
    (RS_HOP, 7, 1, 3), (RS_HOP, 6, 0, 3), (DRAIN, 16), (RS_HOP, 7, 0, 4), (F_SIB, 0, 2), (AG_GET, 4, 1, 3),
    (AG_GET, 4, 0, 3), (F_MM, 0, 3, 0, 1), (RS_HOP, 5, 1, 4), (F_R1, 0, 2), (GRAD, 0, 3), (RS_HOP, 7, 1, 4),
    (RS_HOP, 6, 0, 4), (F_SIB, 0, 3), (F_R2, 0, 2), (FINISH, 5), (DRAIN, 16), (AG_GET, 4, 0, 4), (F_MM, 0, 4, 1),
    (FINISH, 7), (F_R1, 0, 3), (F_R3, 0, 2), (FINISH, 6), (AG_GET, 5, 1, 1), (F_MM, 1, 4, 0), (AG_GET, 5, 0, 1),
    (GRAD, 0, 4), (AG_GET, 7, 0, 1), (F_R2, 0, 3), (AG_GET, 6, 1, 1), (AG_GET, 7, 1, 1), (F_SIB, 0, 4),
    (AG_GET, 6, 0, 1), (F_MM, 1, 1, 0, 1), (AG_GET, 5, 1, 2), (AG_GET, 5, 0, 2), (F_R3, 0, 3), (GRAD, 1, 1),
    (F_R1, 0, 4), (AG_GET, 7, 1, 2), (AG_GET, 6, 0, 2), (AG_GET, 7, 0, 2), (AG_GET, 6, 1, 2), (GRAD, 1, 2),
    (AG_GET, 5, 1, 3), (F_SIB, 1, 1), (AG_GET, 7, 1, 3), (F_R2, 0, 4), (AG_GET, 6, 0, 3), (F_MM, 1, 2, 0, 1),
    (AG_GET, 7, 0, 3), (AG_GET, 6, 1, 3), (F_R1, 1, 1), (AG_GET, 5, 0, 3), (F_MM, 1, 3, 0, 1), (AG_GET, 6, 0, 4),
    (F_SIB, 1, 2), (AG_GET, 5, 1, 4), (F_R3, 0, 4), (SWAP, 0), (AG_GET, 7, 1, 4), (F_MM, 1, 4, 1), (F_R2, 1, 1),
    (F_SIB, 1, 3), (F_R1, 1, 2), (SWAPPED, 0), (GRAD, 1, 4), (F_R3, 1, 1), (F_SIB, 1, 4), (F_R1, 1, 3), (GRAD, 1, 3),
    (F_R1, 1, 4), (F_R2, 1, 2), (DRAIN, 16), (F_R2, 1, 3), (DRAIN, 16), (DRAIN, 16), (F_R2, 1, 4), (DRAIN, 16),
    (F_R3, 1, 2), (F_R3, 1, 3), (DRAIN, 16), (F_R3, 1, 4), (SWAP, 1), (SWAPPED, 1),
)


def gelu_parts(hidden):
    inner_arg = root_two_pi * (hidden + cubic_coef * hidden * hidden * hidden)
    bent_value = jnp.tanh(inner_arg)
    result = 0.5 * hidden * (1.0 + bent_value)
    slopes = 0.5 * (1.0 + bent_value) + 0.5 * hidden * (
        1.0 - bent_value * bent_value
    ) * root_two_pi * (1.0 + 3.0 * cubic_coef * hidden * hidden)
    return (result, slopes)


def halves(value):
    high = value.astype(BF16)
    return high, (value - high.astype(F32)).astype(BF16)


def kernel(
    tokens, up_weight, down_weight, cotangent,
    output, grad_tokens, grad_up, grad_down,
    gathered, raw, weights, partial, summed, spread, slope, sums, from_sib,
    near, far, last, result, give, take,
    send_sem, recv_sem, local_sem,
):
    row, z, depth = lax.axis_index("row"), lax.axis_index("col"), lax.axis_index("depth")
    y, xl, xh, q = row // 2, row % 2, depth // 2, depth % 2
    xh_r, xh_l = (xh + xl) % 2, (xh + xl + 1) % 2
    sib = (row, z, xh * 2 + 1 - q)
    y_r, y_l = (((y + 1) % 4) * 2 + xl, z, depth), (((y + 3) % 4) * 2 + xl, z, depth)
    x_r, x_l = (y * 2 + 1 - xl, z, xh_r * 2 + q), (y * 2 + 1 - xl, z, xh_l * 2 + q)
    z_r, z_l = (row, (z + 1) % 8, depth), (row, (z + 7) % 8, depth)
    y_2, x_2 = (((y + 2) % 4) * 2 + xl, z, depth), (row, z, (1 - xh) * 2 + q)

    def by_core(zero, one):
        return tuple(i + q * (j - i) for i, j in zip(zero, one))

    ring_1 = (by_core(x_r, y_r), by_core(x_l, y_l))
    ring_2 = (by_core(y_r, x_r), by_core(y_l, x_l), by_core(y_2, x_2))
    z_dev, z_sgn = (z_r, z_l), (1, 7)

    slots, pending = {}, []

    def remote(name, src, dst, device):
        at = slots.setdefault(name, len(slots))
        return pltpu.make_async_remote_copy(
            src_ref=src, dst_ref=dst, send_sem=send_sem.at[at], recv_sem=recv_sem.at[at],
            device_id=device, device_id_type=pl.DeviceIdType.MESH,
        )

    def send(name, src, dst, device):
        copy = remote(name, src, dst, device)
        copy.start()
        pending.append(copy)

    def arrive(name, dst):
        remote(name, dst, dst, sib).wait_recv()

    def rows(core, half):
        return pl.ds(pl.multiple_of(core * 96 + half * 48, 8), 48)

    def own_piece(a, g, dy, half):
        return gathered.at[a, g, (y + dy) % 4, rows(q, half)]

    def across_x(a, dy, half):
        piece = rows(q, half)
        src, dst = (gathered.at[a, g, (y + dy) % 4, piece] for g in range(2))
        send(("x", a, dy, half), src, dst, (x_r, x_l)[half])

    def to_core(a, g, dy, half):
        piece = own_piece(a, g, dy, half)
        send(("s", a, g, dy, half), piece, piece, sib)

    def own_x(a):
        if a == 1:
            loads[a].wait()
        for half in range(2):
            across_x(a, 0, half)

    def own_y(a):
        if a == 0:
            loads[a].wait()
        for halves_of in ((0, 1), (1, 0)):
            for way in range(2):
                piece = own_piece(a, 0, 0, halves_of[way])
                send(("y", a, way, halves_of[way]), piece, piece, (y_r, y_l)[way])

    def gy(a, way, half):
        dy = 3 if way == 0 else 1
        piece = own_piece(a, 0, dy, half)
        arrive(("y", a, way, half), piece)
        if half == way:
            send(("yf", a, way), piece, piece, (y_r, y_l)[way])
        across_x(a, dy, half)
        to_core(a, 0, dy, half)

    def gf(a, way):
        arrive(("yf", a, way), own_piece(a, 0, 2, way))
        across_x(a, 2, way)
        to_core(a, 0, 2, way)

    def gx(a, dy, half):
        arrive(("x", a, dy, half), own_piece(a, 1, dy, half))
        to_core(a, 1, dy, half)

    def split_weights(a):
        loads[2 + a].wait()
        high, low = halves(raw[a])
        weights[a, 0:UNITS] = high
        weights[a, UNITS:2 * UNITS] = high
        weights[a, 2 * UNITS:3 * UNITS] = low

    def prod(u):
        def nt(left, right):
            return lax.dot_general(left, right, (((1,), (1,)), ((), ())), preferred_element_type=F32)

        def product(a, blocks):
            high, low = halves(jnp.concatenate([gathered[a, g, (y + dy) % 4] for g, dy in blocks], axis=0))
            w_high, w_low = weights[a, 0:UNITS], weights[a, 2 * UNITS:3 * UNITS]
            return nt(high, w_high) + (nt(low, w_high) + nt(high, w_low))

        for a, g, dy in PAIRS[u]:
            if (g, dy) != (0, 0):
                for half in range(2):
                    arrive(("s", a, g, dy, half), gathered.at[a, g, (y + dy) % 4, rows(1 - q, half)])
        (a, *first), (b, *second) = PAIRS[u]
        if a == b:
            total = product(a, (first, second))
            parts = total[0:BLOCK], total[BLOCK:2 * BLOCK]
        else:
            parts = product(a, (first,)), product(b, (second,))
        for j, part in enumerate(parts):
            partial[:, u, j] = part.reshape(8, CHUNK, UNITS)
        rs_send(u, u % 2, 1)
        rs_send(u, 1 - u % 2, 2)

    def z_chunk(way, distance):
        return (z + z_sgn[way] * distance) % 8

    def rs_send(u, way, step):
        src, dst = partial.at[z_chunk(way, 5 - step), u], summed.at[way, step - 1, u]
        send(("rs", u, way, step), src, dst, z_dev[way])

    def rs_hop(u, way, step):
        arrive(("rs", u, way, step - 1), summed.at[way, step - 2, u])
        c = z_chunk(way, 5 - step)
        partial[c, u] = partial[c, u] + summed[way, step - 2, u]
        rs_send(u, way, step)

    def ag_send(u, way, k):
        piece = spread.at[z_chunk(1 - way, k - 1), u]
        send(("ag", u, way, k), piece, piece, z_dev[way])

    def ag_get(u, way, k):
        arrive(("ag", u, way, k), spread.at[z_chunk(1 - way, k), u])
        if k < 3 or (k == 3 and way == u % 2):
            ag_send(u, way, k + 1)

    def finish(u):
        for way in range(2):
            arrive(("rs", u, way, 4), summed.at[way, 3, u])
        for j, (a, g, dy) in enumerate(PAIRS[u]):
            total = partial[z, u, j] + summed[0, 3, u, j] + summed[1, 3, u, j]
            if a == 0:
                spread[z, u, j], slope[g, dy] = gelu_parts(total)
            else:
                spread[z, u, j] = total * slope[g, dy]
        for way in range(2):
            ag_send(u, way, 1)

    def spread_rows(a, chunks):
        places = [PLACE[(a, g, dy)] for g, dy in BLOCKS]
        return jnp.concatenate([spread[c, u, j] for c in chunks for u, j in places], axis=0)

    def round_chunk(r, core):
        if r == 4:
            return (z + 4 * core) % 8
        return (z + r + (8 - 2 * r) * core) % 8

    def f_mm(a, r, *cores):
        high, low = halves(spread_rows(a, [round_chunk(r, core) for core in cores]))
        total = jnp.dot(jnp.concatenate([high, low, high], axis=1), weights[1 - a], preferred_element_type=F32)
        for i, core in enumerate(cores):
            for n, (g, dy) in enumerate(BLOCKS):
                at = i * BLOCK + n * CHUNK
                for side in range(2):
                    dx = 2 * ((side + xh) % 2) if g == 0 else 1 + 2 * ((side + xh_r) % 2)
                    place = (dx, dy) if core == 0 else (dy, dx)
                    sums[r - 1, a, core, *place] = total[at:at + CHUNK, side * UNITS:(side + 1) * UNITS]
        if 1 in cores:
            send(("fs", a, r), sums.at[r - 1, a, 1 - q], from_sib.at[r - 1, a], sib)

    def f_sib(a, r):
        i = r - 1
        arrive(("fs", a, r), from_sib.at[i, a])
        sums[i, a, q] = sums[i, a, q] + from_sib[i, a]
        for way in range(2):
            piece = sums.at[i, a, q, 2, 2 * way:2 * way + 2]
            send(("f1", a, r, way), piece, near.at[i, a, way], ring_1[way])

    def f_r1(a, r):
        i = r - 1
        for way, at in ((0, 1), (1, 3)):
            half = slice(2 * way, 2 * way + 2)
            arrive(("f1", a, r, way), near.at[i, a, way])
            sums[i, a, q, at, half] = sums[i, a, q, at, half] + near[i, a, way]
            send(("f2", a, r, way), sums.at[i, a, q, at], far.at[i, a, way], ring_1[way])

    def f_r2(a, r):
        i = r - 1
        for way in range(2):
            arrive(("f2", a, r, way), far.at[i, a, way])
        sums[i, a, q, 0] = sums[i, a, q, 0] + far[i, a, 0] + far[i, a, 1]
        for way, at in ((2, 2), (0, 1), (1, 3)):
            send(("f3", a, r, way), sums.at[i, a, q, 0, at], last.at[i, a, way], ring_2[way])

    def f_r3(a, r):
        i = r - 1
        for way in range(3):
            arrive(("f3", a, r, way), last.at[i, a, way])
        result[a, i] = (sums[i, a, q, 0, 0] + last[i, a, 2]) + (last[i, a, 0] + last[i, a, 1])

    def swap(a):
        first, second = result[a, :, :, 0:BLOCK], result[a, :, :, BLOCK:2 * BLOCK]
        lower = jnp.full(first.shape, q, jnp.int32) == 0
        give[a] = jnp.where(lower, second, first)
        send(("swap", a), give.at[a], take.at[a], sib)
        mine = jnp.where(lower, first, second)
        for r in range(1, 5):
            at = pl.ds(pl.multiple_of(round_chunk(r, q) * CHUNK, 8), CHUNK)
            (output, grad_tokens)[a][at, :] = mine[r - 1]

    def swapped(a):
        arrive(("swap", a), take.at[a])
        for r in range(1, 5):
            at = pl.ds(pl.multiple_of(round_chunk(r, 1 - q) * CHUNK, 8), CHUNK)
            (output, grad_tokens)[a][at, :] = take[a, r - 1]

    rounds_done = [0, 0]

    def grad(a, r):
        dst = (grad_down, grad_up)[a]
        chunks = (round_chunk(r, 0), round_chunk(r, 1))
        left = spread_rows(a, chunks).T
        right = jnp.concatenate([
            gathered[1 - a, g, (y + dy) % 4, pl.ds(pl.multiple_of(c * CHUNK, 8), CHUNK), :]
            for c in chunks for g, dy in BLOCKS
        ], axis=0)
        l_high, l_low = halves(left)
        r_high, r_low = halves(right)
        term = jnp.dot(
            jnp.concatenate([l_high, l_low, l_high], axis=1), jnp.concatenate([r_high, r_high, r_low], axis=0),
            preferred_element_type=F32)
        dst[...] = term if rounds_done[a] == 0 else dst[...] + term
        rounds_done[a] += 1

    def drain(count):
        for copy in pending[:count]:
            copy.wait_send()
        del pending[:count]

    loads = [
        pltpu.make_async_copy(src, dst, local_sem.at[i])
        for i, (src, dst) in enumerate((
            (tokens, gathered.at[0, 0, y]), (cotangent, gathered.at[1, 0, y]),
            (up_weight, raw.at[0]), (down_weight, raw.at[1]),
        ))
    ]
    for load in loads:
        load.start()
    barrier = pltpu.get_barrier_semaphore()
    partners = (sib, y_r, y_l, x_r, x_l, z_r, z_l, ring_2[2])
    for device in partners:
        pl.semaphore_signal(barrier, inc=1, device_id=device, device_id_type=pl.DeviceIdType.MESH)
    pl.semaphore_wait(barrier, len(partners))

    steps = (
        own_x, own_y, gy, gf, gx, split_weights, prod, rs_hop, finish, ag_get,
        f_mm, f_sib, f_r1, f_r2, f_r3, swap, swapped, grad, drain,
    )
    for step, *at in ORDER:
        steps[step](*at)
    drain(len(pending))
    assert len(slots) <= SLOTS, len(slots)


def store_kernel(*refs):
    sources, targets, sem = refs[:4], refs[4:8], refs[8]
    stores = [pltpu.make_async_copy(src, dst, sem.at[i]) for i, (src, dst) in enumerate(zip(sources, targets))]
    for store in stores:
        store.start()
    for store in stores:
        store.wait()


def shards(tokens, up_weight, down_weight, cotangent):
    anywhere, vmem = pl.BlockSpec(memory_space=pl.ANY), pl.BlockSpec(memory_space=pltpu.VMEM)
    piece = (CHUNK, UNITS)
    shapes = (
        jax.ShapeDtypeStruct((BLOCK, BLOCK), F32),
        jax.ShapeDtypeStruct((BLOCK, BLOCK), F32),
        jax.ShapeDtypeStruct((UNITS, WIDTH), F32),
        jax.ShapeDtypeStruct((UNITS, WIDTH), F32),
    )
    results = pl.pallas_call(
        kernel,
        out_shape=tuple(pltpu.VMEM(shape.shape, F32) for shape in shapes),
        in_specs=[anywhere] * 4,
        out_specs=(vmem,) * 4,
        scratch_shapes=[
            pltpu.VMEM((2, 2, 4, BLOCK, WIDTH), F32),
            pltpu.VMEM((2, UNITS, WIDTH), F32),
            pltpu.VMEM((2, 3 * UNITS, WIDTH), BF16),
            pltpu.VMEM((8, 8, 2) + piece, F32),
            pltpu.VMEM((2, 4, 8, 2) + piece, F32),
            pltpu.VMEM((8, 8, 2) + piece, F32),
            pltpu.VMEM((2, 4) + piece, F32),
            pltpu.VMEM((4, 2, 2, 4, 4) + piece, F32),
            pltpu.VMEM((4, 2, 4, 4) + piece, F32),
            pltpu.VMEM((4, 2, 2, 2) + piece, F32),
            pltpu.VMEM((4, 2, 2, 4) + piece, F32),
            pltpu.VMEM((4, 2, 3) + piece, F32),
            pltpu.VMEM((2, 4) + piece, F32),
            pltpu.VMEM((2, 4, CHUNK, BLOCK), F32),
            pltpu.VMEM((2, 4, CHUNK, BLOCK), F32),
            pltpu.SemaphoreType.DMA((SLOTS,)),
            pltpu.SemaphoreType.DMA((SLOTS,)),
            pltpu.SemaphoreType.DMA((4,)),
        ],
        compiler_params=pltpu.CompilerParams(
            collective_id=0, has_side_effects=True, vmem_limit_bytes=58 * 1024 * 1024),
        cost_estimate=pl.CostEstimate(flops=16_300_000_000, bytes_accessed=6_000_000, transcendentals=73728),
    )(tokens, up_weight, down_weight, cotangent)
    return pl.pallas_call(
        store_kernel,
        out_shape=shapes,
        in_specs=[vmem] * 4,
        out_specs=(anywhere,) * 4,
        scratch_shapes=[pltpu.SemaphoreType.DMA((4,))],
    )(*results)


def solution(mesh):
    return jax.shard_map(
        shards,
        mesh=mesh,
        in_specs=(
            P("row", "col"),
            P(("row", "depth"), "col"),
            P(("row", "depth"), "col"),
            P("row", "col"),
        ),
        out_specs=(
            P("row", ("col", "depth")),
            P("row", ("col", "depth")),
            P(("row", "depth"), "col"),
            P(("row", "depth"), "col"),
        ),
        check_vma=False,
    )
```

```python
import jax
import jax.numpy as jnp
from jax import lax
from jax.experimental import pallas as pl
from jax.experimental.pallas import tpu as pltpu
from jax.sharding import PartitionSpec as P

F32, BF16 = jnp.float32, jnp.bfloat16
root_two_pi = 0.7978845608028654
cubic_coef = 0.044715

SLOTS = 260
BLOCK, WIDTH, UNITS, CHUNK = 192, 768, 384, 24
PAIRS = (
    ((0, 0, 0), (1, 0, 0)), ((0, 1, 0), (1, 1, 0)),
    ((0, 0, 1), (0, 0, 3)), ((0, 1, 1), (0, 1, 3)), ((0, 0, 2), (0, 1, 2)),
    ((1, 0, 1), (1, 0, 3)), ((1, 1, 1), (1, 1, 3)), ((1, 0, 2), (1, 1, 2)),
)
PLACE = {block: (u, j) for u, pair in enumerate(PAIRS) for j, block in enumerate(pair)}
BLOCKS = tuple((g, dy) for g in range(2) for dy in range(4))
Y_FIRST = ((0, 1, 0, 1), (0, 1, 1, 0))
(
    OWN_X, OWN_Y, GY, GF, GX, SPLIT_WEIGHTS, PROD, RS_HOP, FINISH, AG_GET, F_MM, F_SIB, F_R1, F_R2, F_R3, F_R4,
    SWAP, SWAPPED, GRAD, DRAIN,
) = range(20)
ORDER = (
    (OWN_Y, 0), (OWN_X, 0), (OWN_X, 1), (SPLIT_WEIGHTS, 1), (SPLIT_WEIGHTS, 0), (PROD, 0), (GY, 0, 0, 0),
    (GX, 0, 0, 0), (GX, 0, 0, 1), (GY, 0, 1, 1), (RS_HOP, 0, 0, 2), (RS_HOP, 0, 1, 3), (GY, 0, 0, 1), (GY, 0, 1, 0),
    (GX, 1, 0, 1), (GX, 1, 0, 0), (OWN_Y, 1), (RS_HOP, 0, 0, 3), (RS_HOP, 0, 1, 4), (PROD, 2), (GF, 0, 0), (GF, 0, 1),
    (RS_HOP, 0, 0, 4), (PROD, 1), (GX, 0, 1, 0), (RS_HOP, 2, 0, 2), (RS_HOP, 2, 1, 3), (GY, 1, 0, 0), (GX, 0, 3, 0),
    (GX, 0, 1, 1), (GX, 0, 3, 1), (FINISH, 0), (GY, 1, 0, 1), (GX, 0, 2, 1), (GY, 1, 1, 0), (RS_HOP, 1, 1, 2),
    (RS_HOP, 1, 0, 3), (GX, 0, 2, 0), (GY, 1, 1, 1), (RS_HOP, 2, 1, 4), (RS_HOP, 2, 0, 3), (PROD, 3), (GF, 1, 0),
    (GX, 1, 3, 0), (AG_GET, 0, 1, 1), (RS_HOP, 1, 1, 3), (RS_HOP, 1, 0, 4), (GX, 1, 3, 1), (PROD, 4),
    (RS_HOP, 2, 0, 4), (GX, 1, 1, 0), (RS_HOP, 3, 1, 2), (GF, 1, 1), (GX, 1, 1, 1), (RS_HOP, 3, 0, 3), (GX, 1, 2, 0),
    (DRAIN, 16), (RS_HOP, 1, 1, 4), (RS_HOP, 4, 0, 2), (DRAIN, 16), (RS_HOP, 4, 1, 3), (FINISH, 2), (GX, 1, 2, 1),
    (RS_HOP, 3, 1, 3), (RS_HOP, 3, 0, 4), (DRAIN, 16), (RS_HOP, 4, 0, 3), (DRAIN, 16), (RS_HOP, 4, 1, 4), (FINISH, 1),
    (AG_GET, 2, 0, 1), (AG_GET, 2, 1, 1), (DRAIN, 16), (RS_HOP, 3, 1, 4), (RS_HOP, 4, 0, 4), (AG_GET, 1, 0, 1),
    (AG_GET, 1, 1, 1), (AG_GET, 2, 0, 2), (AG_GET, 2, 1, 2), (FINISH, 4), (PROD, 6), (FINISH, 3), (AG_GET, 1, 0, 2),
    (AG_GET, 2, 0, 3), (PROD, 5), (AG_GET, 0, 0, 1), (AG_GET, 4, 0, 1), (AG_GET, 1, 1, 2), (RS_HOP, 6, 0, 2),
    (AG_GET, 4, 1, 1), (PROD, 7), (RS_HOP, 6, 1, 3), (AG_GET, 3, 0, 1), (AG_GET, 3, 1, 1), (F_MM, 0, 1, 0, 1),
    (GRAD, 0, 1), (RS_HOP, 5, 0, 3), (RS_HOP, 5, 1, 2), (AG_GET, 0, 1, 2), (F_SIB, 0, 1), (AG_GET, 4, 1, 2),
    (AG_GET, 1, 1, 3), (F_MM, 0, 4, 0), (RS_HOP, 7, 1, 2), (AG_GET, 4, 0, 2), (RS_HOP, 6, 1, 4), (AG_GET, 2, 1, 3),
    (AG_GET, 0, 0, 2), (RS_HOP, 6, 0, 3), (F_R1, 0, 1), (RS_HOP, 7, 0, 3), (AG_GET, 3, 1, 2), (RS_HOP, 5, 1, 3),
    (AG_GET, 3, 0, 2), (F_MM, 0, 2, 0, 1), (RS_HOP, 5, 0, 4), (GRAD, 0, 2), (F_R2, 0, 1), (AG_GET, 4, 0, 3),
    (AG_GET, 0, 0, 3), (F_SIB, 0, 2), (RS_HOP, 7, 1, 3), (RS_HOP, 6, 0, 4), (AG_GET, 4, 1, 3), (F_R3, 0, 1),
    (RS_HOP, 7, 0, 4), (AG_GET, 2, 0, 4), (AG_GET, 1, 1, 4), (AG_GET, 1, 0, 3), (AG_GET, 0, 1, 3), (F_R1, 0, 2),
    (AG_GET, 3, 1, 3), (AG_GET, 3, 0, 3), (F_MM, 0, 3, 0, 1), (F_R4, 0, 1), (RS_HOP, 5, 1, 4), (GRAD, 0, 3),
    (RS_HOP, 7, 1, 4), (F_R2, 0, 2), (AG_GET, 0, 0, 4), (AG_GET, 4, 0, 4), (F_SIB, 0, 3), (FINISH, 5), (FINISH, 6),
    (AG_GET, 3, 1, 4), (F_MM, 0, 4, 1), (FINISH, 7), (F_R3, 0, 2), (F_R1, 0, 3), (AG_GET, 5, 1, 1), (AG_GET, 5, 0, 1),
    (F_MM, 1, 4, 0), (AG_GET, 6, 0, 1), (F_SIB, 0, 4), (AG_GET, 6, 1, 1), (F_R4, 0, 2), (GRAD, 0, 4),
    (AG_GET, 7, 0, 1), (AG_GET, 7, 1, 1), (F_R2, 0, 3), (F_R1, 0, 4), (AG_GET, 5, 0, 2), (AG_GET, 5, 1, 2),
    (AG_GET, 6, 0, 2), (AG_GET, 6, 1, 2), (F_MM, 1, 1, 0, 1), (AG_GET, 7, 0, 2), (F_R3, 0, 3), (AG_GET, 7, 1, 2),
    (F_MM, 1, 2, 0, 1), (AG_GET, 5, 1, 3), (GRAD, 1, 1), (F_SIB, 1, 1), (AG_GET, 7, 1, 3), (AG_GET, 6, 0, 3),
    (AG_GET, 7, 0, 3), (F_SIB, 1, 2), (F_R2, 0, 4), (AG_GET, 5, 0, 3), (AG_GET, 5, 1, 4), (AG_GET, 6, 1, 3),
    (F_MM, 1, 3, 0, 1), (F_R1, 1, 1), (AG_GET, 6, 0, 4), (AG_GET, 7, 1, 4), (F_MM, 1, 4, 1), (F_R1, 1, 2),
    (GRAD, 1, 4), (F_SIB, 1, 3), (F_SIB, 1, 4), (F_R2, 1, 1), (F_R3, 0, 4), (GRAD, 1, 2), (F_R1, 1, 3), (F_R1, 1, 4),
    (F_R3, 1, 1), (F_R4, 0, 4), (F_R2, 1, 2), (GRAD, 1, 3), (F_R4, 0, 3), (SWAP, 0), (F_R2, 1, 3), (F_R2, 1, 4),
    (F_R4, 1, 1), (F_R3, 1, 2), (SWAPPED, 0), (DRAIN, 16), (F_R3, 1, 3), (F_R3, 1, 4), (F_R4, 1, 2), (DRAIN, 16),
    (F_R4, 1, 3), (F_R4, 1, 4), (SWAP, 1), (DRAIN, 16), (DRAIN, 16), (SWAPPED, 1),
)


def gelu_parts(hidden):
    inner_arg = root_two_pi * (hidden + cubic_coef * hidden * hidden * hidden)
    bent_value = jnp.tanh(inner_arg)
    result = 0.5 * hidden * (1.0 + bent_value)
    slopes = 0.5 * (1.0 + bent_value) + 0.5 * hidden * (
        1.0 - bent_value * bent_value
    ) * root_two_pi * (1.0 + 3.0 * cubic_coef * hidden * hidden)
    return (result, slopes)


def halves(value):
    high = value.astype(BF16)
    return high, (value - high.astype(F32)).astype(BF16)


def kernel(
    tokens, up_weight, down_weight, cotangent,
    output, grad_tokens, grad_up, grad_down,
    gathered, raw, weights, partial, summed, spread, slope, fold, from_sib,
    near, far_x, far_y, last, ends, result, give, take, widths, grads,
    send_sem, recv_sem, local_sem,
):
    row, z, depth = lax.axis_index("row"), lax.axis_index("col"), lax.axis_index("depth")
    y, xl, xh, q = row // 2, row % 2, depth // 2, depth % 2
    xh_r, xh_l, xh_s = (xh + xl) % 2, (xh + xl + 1) % 2, (xh + xl + q) % 2
    sib = (row, z, xh * 2 + 1 - q)
    y_r, y_l = (((y + 1) % 4) * 2 + xl, z, depth), (((y + 3) % 4) * 2 + xl, z, depth)
    x_r, x_l = (y * 2 + 1 - xl, z, xh_r * 2 + q), (y * 2 + 1 - xl, z, xh_l * 2 + q)
    z_r, z_l = (row, (z + 1) % 8, depth), (row, (z + 7) % 8, depth)
    y_s = (((y + 1 + 2 * q) % 4) * 2 + xl, z, depth)
    x_s = (y * 2 + 1 - xl, z, xh_s * 2 + q)
    z_dev, z_sgn = (z_r, z_l), (1, 7)

    slots, pending = {}, []

    def remote(name, src, dst, device):
        at = slots.setdefault(name, len(slots))
        return pltpu.make_async_remote_copy(
            src_ref=src, dst_ref=dst, send_sem=send_sem.at[at], recv_sem=recv_sem.at[at],
            device_id=device, device_id_type=pl.DeviceIdType.MESH,
        )

    def send(name, src, dst, device):
        copy = remote(name, src, dst, device)
        copy.start()
        pending.append(copy)

    def arrive(name, dst):
        remote(name, dst, dst, sib).wait_recv()

    def rows(core, half):
        return pl.ds(pl.multiple_of(core * 96 + half * 48, 8), 48)

    def own_piece(a, g, dy, half):
        return gathered.at[a, g, (y + dy) % 4, rows(q, half)]

    def across_x(a, dy, half):
        piece = rows(q, half)
        src, dst = (gathered.at[a, g, (y + dy) % 4, piece] for g in range(2))
        send(("x", a, dy, half), src, dst, (x_r, x_l)[half])

    def to_core(a, g, dy, half):
        piece = own_piece(a, g, dy, half)
        send(("s", a, g, dy, half), piece, piece, sib)

    def own_x(a):
        if a == 1:
            loads[a].wait()
        for half in range(2):
            across_x(a, 0, half)

    def own_y(a):
        if a == 0:
            loads[a].wait()
        for halves_of in ((0, 1), (1, 0)):
            for way in range(2):
                piece = own_piece(a, 0, 0, halves_of[way])
                send(("y", a, way, halves_of[way]), piece, piece, (y_r, y_l)[way])

    def gy(a, way, half):
        dy = 3 if way == 0 else 1
        piece = own_piece(a, 0, dy, half)
        arrive(("y", a, way, half), piece)
        if half == way:
            send(("yf", a, way), piece, piece, (y_r, y_l)[way])
        across_x(a, dy, half)
        to_core(a, 0, dy, half)

    def gf(a, way):
        arrive(("yf", a, way), own_piece(a, 0, 2, way))
        across_x(a, 2, way)
        to_core(a, 0, 2, way)

    def gx(a, dy, half):
        arrive(("x", a, dy, half), own_piece(a, 1, dy, half))
        to_core(a, 1, dy, half)

    def split_weights(a):
        loads[2 + a].wait()
        high, low = halves(raw[a])
        weights[a, 0:UNITS] = high
        weights[a, UNITS:2 * UNITS] = high
        weights[a, 2 * UNITS:3 * UNITS] = low

    def prod(u):
        def nt(left, right):
            return lax.dot_general(left, right, (((1,), (1,)), ((), ())), preferred_element_type=F32)

        def product(a, blocks):
            high, low = halves(jnp.concatenate([gathered[a, g, (y + dy) % 4] for g, dy in blocks], axis=0))
            w_high, w_low = weights[a, 0:UNITS], weights[a, 2 * UNITS:3 * UNITS]
            return nt(high, w_high) + (nt(low, w_high) + nt(high, w_low))

        for a, g, dy in PAIRS[u]:
            if (g, dy) != (0, 0):
                for half in range(2):
                    arrive(("s", a, g, dy, half), gathered.at[a, g, (y + dy) % 4, rows(1 - q, half)])
        (a, *first), (b, *second) = PAIRS[u]
        if a == b:
            total = product(a, (first, second))
            parts = total[0:BLOCK], total[BLOCK:2 * BLOCK]
        else:
            parts = product(a, (first,)), product(b, (second,))
        for j, part in enumerate(parts):
            partial[:, u, j] = part.reshape(8, CHUNK, UNITS)
        rs_send(u, u % 2, 1)
        rs_send(u, 1 - u % 2, 2)

    def z_chunk(way, distance):
        return (z + z_sgn[way] * distance) % 8

    def rs_send(u, way, step):
        src, dst = partial.at[z_chunk(way, 5 - step), u], summed.at[way, step - 1, u]
        send(("rs", u, way, step), src, dst, z_dev[way])

    def rs_hop(u, way, step):
        arrive(("rs", u, way, step - 1), summed.at[way, step - 2, u])
        c = z_chunk(way, 5 - step)
        partial[c, u] = partial[c, u] + summed[way, step - 2, u]
        rs_send(u, way, step)

    def ag_send(u, way, k):
        piece = spread.at[z_chunk(1 - way, k - 1), u]
        send(("ag", u, way, k), piece, piece, z_dev[way])

    def ag_get(u, way, k):
        arrive(("ag", u, way, k), spread.at[z_chunk(1 - way, k), u])
        if k < 3 or (k == 3 and way == u % 2):
            ag_send(u, way, k + 1)

    def finish(u):
        for way in range(2):
            arrive(("rs", u, way, 4), summed.at[way, 3, u])
        for j, (a, g, dy) in enumerate(PAIRS[u]):
            total = partial[z, u, j] + summed[0, 3, u, j] + summed[1, 3, u, j]
            if a == 0:
                spread[z, u, j], slope[g, dy] = gelu_parts(total)
            else:
                spread[z, u, j] = total * slope[g, dy]
        for way in range(2):
            ag_send(u, way, 1)

    def spread_rows(a, chunks):
        places = [PLACE[(a, g, dy)] for g, dy in BLOCKS]
        return jnp.concatenate([spread[c, u, j] for c in chunks for u, j in places], axis=0)

    def round_chunk(r, core):
        if r == 4:
            return (z + 4 * core) % 8
        return (z + r + (8 - 2 * r) * core) % 8

    def f_mm(a, r, *cores):
        high, low = halves(spread_rows(a, [round_chunk(r, core) for core in cores]))
        total = jnp.dot(jnp.concatenate([high, low, high], axis=1), weights[1 - a], preferred_element_type=F32)
        for i, core in enumerate(cores):
            for n, (g, dy) in enumerate(BLOCKS):
                at = i * BLOCK + n * CHUNK
                for side in range(2):
                    fold[r - 1, a, core, side, g, (y + dy) % 4] = total[at:at + CHUNK, side * UNITS:(side + 1) * UNITS]
        if 1 in cores:
            send(("fs", a, r), fold.at[r - 1, a, 1 - q], from_sib.at[r - 1, a], sib)

    def f_sib(a, r):
        i = r - 1
        arrive(("fs", a, r), from_sib.at[i, a])
        fold[i, a, q] = fold[i, a, q] + from_sib[i, a]
        if Y_FIRST[a][i]:
            send(("f1", a, r, 0), fold.at[i, a, q, 0, :, (y + 2) % 4], near.at[i, a, 0], y_r)
            send(("f1", a, r, 1), fold.at[i, a, q, 1, :, (y + 2) % 4], near.at[i, a, 1], y_l)
        else:
            send(("f1", a, r, 0), fold.at[i, a, q, 1 - xh, 0, 0:2], near.at[i, a, 0], x_r)
            send(("f1", a, r, 1), fold.at[i, a, q, 1 - xh, 0, 2:4], near.at[i, a, 1], x_l)

    def f_r1(a, r):
        i = r - 1
        for way, yy, xx in ((0, (y + 1) % 4, xh_r), (1, (y + 3) % 4, xh_l)):
            arrive(("f1", a, r, way), near.at[i, a, way])
            if Y_FIRST[a][i]:
                fold[i, a, q, way, :, yy] = fold[i, a, q, way, :, yy] + near[i, a, way]
                send(("f2", a, r, way), fold.at[i, a, q, :, :, yy], far_y.at[i, a, way], (y_r, y_l)[way])
            else:
                half = slice(2 * way, 2 * way + 2)
                fold[i, a, q, xx, 1, half] = fold[i, a, q, xx, 1, half] + near[i, a, way]
                send(("f2", a, r, way), fold.at[i, a, q, xx, 1], far_x.at[i, a, way], (x_r, x_l)[way])

    def f_r2(a, r):
        i = r - 1
        far = (far_x, far_y)[Y_FIRST[a][i]]
        for way in range(2):
            arrive(("f2", a, r, way), far.at[i, a, way])
        if Y_FIRST[a][i]:
            fold[i, a, q, :, :, y] = fold[i, a, q, :, :, y] + far[i, a, 0] + far[i, a, 1]
            send(("f3", a, r), fold.at[i, a, q, 1 - xh, 0, y], last.at[i, a], x_s)
        else:
            fold[i, a, q, xh, 0] = fold[i, a, q, xh, 0] + far[i, a, 0] + far[i, a, 1]
            send(("f3", a, r), fold.at[i, a, q, xh, 0, (y + 2) % 4], last.at[i, a], y_s)

    def f_r3(a, r):
        i = r - 1
        arrive(("f3", a, r), last.at[i, a])
        if Y_FIRST[a][i]:
            fold[i, a, q, xh_s, 1, y] = fold[i, a, q, xh_s, 1, y] + last[i, a]
            send(("f4", a, r, 0), fold.at[i, a, q, xh_r, 1, y], ends.at[i, a, 0], x_r)
            send(("f4", a, r, 1), fold.at[i, a, q, xh_l, 1, y], ends.at[i, a, 1], x_l)
        else:
            ys = (y + 1 + 2 * q) % 4
            fold[i, a, q, xh, 0, ys] = fold[i, a, q, xh, 0, ys] + last[i, a]
            send(("f4", a, r, 0), fold.at[i, a, q, xh, 0, (y + 1) % 4], ends.at[i, a, 0], y_r)
            send(("f4", a, r, 1), fold.at[i, a, q, xh, 0, (y + 3) % 4], ends.at[i, a, 1], y_l)

    def f_r4(a, r):
        i = r - 1
        arrive(("f4", a, r, 0), ends.at[i, a, 0])
        arrive(("f4", a, r, 1), ends.at[i, a, 1])
        result[a, i] = fold[i, a, q, xh, 0, y] + ends[i, a, 0] + ends[i, a, 1]

    def swap(a):
        first, second = result[a, :, :, 0:BLOCK], result[a, :, :, BLOCK:2 * BLOCK]
        lower = jnp.full(first.shape, q, jnp.int32) == 0
        give[a] = jnp.where(lower, second, first)
        send(("swap", a), give.at[a], take.at[a], sib)
        mine = jnp.where(lower, first, second)
        for r in range(1, 5):
            at = pl.ds(pl.multiple_of(round_chunk(r, q) * CHUNK, 8), CHUNK)
            widths[a, at, :] = mine[r - 1]

    def swapped(a):
        arrive(("swap", a), take.at[a])
        for r in range(1, 5):
            at = pl.ds(pl.multiple_of(round_chunk(r, 1 - q) * CHUNK, 8), CHUNK)
            widths[a, at, :] = take[a, r - 1]
        stores[a].start()

    rounds_done = [0, 0]

    def grad(a, r):
        chunks = (round_chunk(r, 0), round_chunk(r, 1))
        left = spread_rows(a, chunks).T
        right = jnp.concatenate([
            gathered[1 - a, g, (y + dy) % 4, pl.ds(pl.multiple_of(c * CHUNK, 8), CHUNK), :]
            for c in chunks for g, dy in BLOCKS
        ], axis=0)
        l_high, l_low = halves(left)
        r_high, r_low = halves(right)
        term = jnp.dot(
            jnp.concatenate([l_high, l_low, l_high], axis=1), jnp.concatenate([r_high, r_high, r_low], axis=0),
            preferred_element_type=F32)
        grads[a] = term if rounds_done[a] == 0 else grads[a] + term
        rounds_done[a] += 1
        if rounds_done[a] == 4:
            stores[2 + a].start()

    def drain(count):
        for copy in pending[:count]:
            copy.wait_send()
        del pending[:count]

    loads = [
        pltpu.make_async_copy(src, dst, local_sem.at[i])
        for i, (src, dst) in enumerate((
            (tokens, gathered.at[0, 0, y]), (cotangent, gathered.at[1, 0, y]),
            (up_weight, raw.at[0]), (down_weight, raw.at[1]),
        ))
    ]
    stores = [
        pltpu.make_async_copy(src, dst, local_sem.at[4 + i])
        for i, (src, dst) in enumerate((
            (widths.at[0], output), (widths.at[1], grad_tokens), (grads.at[0], grad_down), (grads.at[1], grad_up),
        ))
    ]
    for load in loads:
        load.start()
    barrier = pltpu.get_barrier_semaphore()
    partners = (sib, y_r, y_l, x_r, x_l, z_r, z_l)
    for device in partners:
        pl.semaphore_signal(barrier, inc=1, device_id=device, device_id_type=pl.DeviceIdType.MESH)
    pl.semaphore_wait(barrier, len(partners))

    steps = (
        own_x, own_y, gy, gf, gx, split_weights, prod, rs_hop, finish, ag_get,
        f_mm, f_sib, f_r1, f_r2, f_r3, f_r4, swap, swapped, grad, drain,
    )
    for step, *at in ORDER:
        steps[step](*at)
    drain(len(pending))
    for store in stores:
        store.wait()
    assert len(slots) <= SLOTS, len(slots)


def copy_kernel(*refs):
    sources, targets, held, sem = refs[:4], refs[4:8], refs[8:12], refs[12]
    loads, stores = [], []
    for src, dst, hold in zip(sources, targets, held):
        parts = 4 if src.shape[0] == UNITS else 1
        size = src.shape[0] // parts
        for part in range(parts):
            at, n = pl.ds(part * size, size), len(loads)
            loads.append(pltpu.make_async_copy(src.at[at], hold.at[at], sem.at[0, n]))
            stores.append(pltpu.make_async_copy(hold.at[at], dst.at[at], sem.at[1, n]))
    for load in loads:
        load.start()
    for load, store in zip(loads, stores):
        load.wait()
        store.start()
    for store in stores:
        store.wait()


def shards(tokens, up_weight, down_weight, cotangent):
    anywhere, piece = pl.BlockSpec(memory_space=pl.ANY), (CHUNK, UNITS)
    shapes = (
        jax.ShapeDtypeStruct((BLOCK, BLOCK), F32),
        jax.ShapeDtypeStruct((BLOCK, BLOCK), F32),
        jax.ShapeDtypeStruct((UNITS, WIDTH), F32),
        jax.ShapeDtypeStruct((UNITS, WIDTH), F32),
    )
    results = pl.pallas_call(
        kernel,
        out_shape=shapes,
        in_specs=[anywhere] * 4,
        out_specs=(anywhere,) * 4,
        scratch_shapes=[
            pltpu.VMEM((2, 2, 4, BLOCK, WIDTH), F32),
            pltpu.VMEM((2, UNITS, WIDTH), F32),
            pltpu.VMEM((2, 3 * UNITS, WIDTH), BF16),
            pltpu.VMEM((8, 8, 2) + piece, F32),
            pltpu.VMEM((2, 4, 8, 2) + piece, F32),
            pltpu.VMEM((8, 8, 2) + piece, F32),
            pltpu.VMEM((2, 4) + piece, F32),
            pltpu.VMEM((4, 2, 2, 2, 2, 4) + piece, F32),
            pltpu.VMEM((4, 2, 2, 2, 4) + piece, F32),
            pltpu.VMEM((4, 2, 2, 2) + piece, F32),
            pltpu.VMEM((4, 2, 2, 4) + piece, F32),
            pltpu.VMEM((4, 2, 2, 2, 2) + piece, F32),
            pltpu.VMEM((4, 2) + piece, F32),
            pltpu.VMEM((4, 2, 2) + piece, F32),
            pltpu.VMEM((2, 4) + piece, F32),
            pltpu.VMEM((2, 4, CHUNK, BLOCK), F32),
            pltpu.VMEM((2, 4, CHUNK, BLOCK), F32),
            pltpu.VMEM((2, BLOCK, BLOCK), F32),
            pltpu.VMEM((2, UNITS, WIDTH), F32),
            pltpu.SemaphoreType.DMA((SLOTS,)),
            pltpu.SemaphoreType.DMA((SLOTS,)),
            pltpu.SemaphoreType.DMA((8,)),
        ],
        compiler_params=pltpu.CompilerParams(
            collective_id=0, has_side_effects=True, vmem_limit_bytes=62 * 1024 * 1024),
        cost_estimate=pl.CostEstimate(flops=16_300_000_000, bytes_accessed=6_000_000, transcendentals=73728),
    )(tokens, up_weight, down_weight, cotangent)
    return pl.pallas_call(
        copy_kernel,
        out_shape=shapes,
        in_specs=[anywhere] * 4,
        out_specs=(anywhere,) * 4,
        scratch_shapes=[pltpu.VMEM(shape.shape, F32) for shape in shapes] + [pltpu.SemaphoreType.DMA((2, 10))],
    )(*results)


def solution(mesh):
    return jax.shard_map(
        shards,
        mesh=mesh,
        in_specs=(
            P("row", "col"),
            P(("row", "depth"), "col"),
            P(("row", "depth"), "col"),
            P("row", "col"),
        ),
        out_specs=(
            P("row", ("col", "depth")),
            P("row", ("col", "depth")),
            P(("row", "depth"), "col"),
            P(("row", "depth"), "col"),
        ),
        check_vma=False,
    )
```

```python
import jax
import jax.numpy as jnp
from jax import lax
from jax.experimental import pallas as pl
from jax.experimental.pallas import tpu as pltpu
from jax.sharding import PartitionSpec as P

F32, BF16 = jnp.float32, jnp.bfloat16
root_two_pi = 0.7978845608028654
cubic_coef = 0.044715

SLOTS = 260
BLOCK, WIDTH, UNITS, CHUNK = 192, 768, 384, 24
GROUPS = (
    ((0, 0, 0), (1, 0, 0)),
    ((0, 1, 0), (1, 1, 0)),
    ((0, 0, 1), (0, 0, 3)),
    ((0, 1, 1), (0, 1, 3), (0, 0, 2), (0, 1, 2)),
    ((1, 0, 1), (1, 0, 3)),
    ((1, 1, 1), (1, 1, 3), (1, 0, 2), (1, 1, 2)),
)
FIRST_WAY = (0, 1, 0, 1, 1, 0)
PLACE = {block: at for at, block in enumerate(block for group in GROUPS for block in group)}
SPAN = tuple(slice(PLACE[group[0]], PLACE[group[0]] + len(group)) for group in GROUPS)
BLOCKS = tuple((g, dy) for g in range(2) for dy in range(4))
Y_FIRST = ((0, 1, 0, 1), (1, 0, 1, 0))
(
    OWN_X, OWN_Y, GY, GF, GX, SPLIT_WEIGHTS, PROD, RS_HOP, FINISH, AG_GET, F_MM, F_SIB, F_R1, F_R2, F_R3, F_R4,
    SWAP, SWAPPED, GRAD, DRAIN,
) = range(20)
ORDER = (
    (OWN_Y, 0), (OWN_X, 1), (SPLIT_WEIGHTS, 0), (SPLIT_WEIGHTS, 1), (PROD, 0), (OWN_X, 0), (GY, 0, 0, 0),
    (GY, 0, 1, 1), (GX, 1, 0, 0), (GX, 1, 0, 1), (RS_HOP, 0, 0, 2), (RS_HOP, 0, 1, 3), (GY, 0, 0, 1), (GY, 0, 1, 0),
    (OWN_Y, 1), (GX, 0, 0, 1), (GX, 0, 0, 0), (RS_HOP, 0, 0, 3), (RS_HOP, 0, 1, 4), (PROD, 2), (GF, 0, 1), (GF, 0, 0),
    (PROD, 1), (GX, 0, 1, 1), (GX, 0, 3, 0), (RS_HOP, 0, 0, 4), (DRAIN, 16), (GY, 1, 0, 0), (GY, 1, 1, 1),
    (GX, 0, 3, 1), (GX, 0, 1, 0), (RS_HOP, 2, 0, 2), (RS_HOP, 2, 1, 3), (RS_HOP, 1, 0, 3), (RS_HOP, 1, 1, 2),
    (DRAIN, 16), (GY, 1, 0, 1), (GX, 0, 2, 0), (GX, 0, 2, 1), (GY, 1, 1, 0), (FINISH, 0), (RS_HOP, 2, 1, 4),
    (PROD, 3), (GX, 1, 3, 0), (GF, 1, 0), (GF, 1, 1), (RS_HOP, 1, 1, 3), (AG_GET, 0, 1, 1), (RS_HOP, 2, 0, 3),
    (RS_HOP, 1, 0, 4), (GX, 1, 1, 1), (DRAIN, 16), (GX, 1, 1, 0), (GX, 1, 3, 1), (GX, 1, 2, 0), (GX, 1, 2, 1),
    (RS_HOP, 3, 0, 3), (RS_HOP, 3, 1, 2), (DRAIN, 16), (RS_HOP, 2, 0, 4), (RS_HOP, 1, 1, 4), (AG_GET, 0, 1, 2),
    (RS_HOP, 3, 0, 4), (RS_HOP, 3, 1, 3), (DRAIN, 16), (FINISH, 2), (PROD, 4), (PROD, 5), (FINISH, 1),
    (RS_HOP, 3, 1, 4), (AG_GET, 2, 0, 1), (AG_GET, 0, 1, 3), (AG_GET, 2, 1, 1), (RS_HOP, 4, 0, 3), (RS_HOP, 4, 1, 2),
    (RS_HOP, 5, 0, 2), (RS_HOP, 5, 1, 3), (AG_GET, 1, 0, 1), (AG_GET, 2, 0, 2), (RS_HOP, 4, 0, 4), (DRAIN, 16),
    (FINISH, 3), (F_MM, 0, 4, 0), (RS_HOP, 5, 0, 3), (AG_GET, 1, 1, 1), (RS_HOP, 4, 1, 3), (AG_GET, 1, 0, 2),
    (RS_HOP, 5, 1, 4), (AG_GET, 3, 1, 1), (AG_GET, 3, 0, 1), (AG_GET, 0, 0, 1), (F_MM, 0, 1, 0, 1), (AG_GET, 1, 1, 2),
    (GRAD, 0, 1), (RS_HOP, 4, 1, 4), (RS_HOP, 5, 0, 4), (F_SIB, 0, 1), (AG_GET, 1, 0, 3), (F_R1, 0, 1), (DRAIN, 16),
    (AG_GET, 3, 0, 2), (AG_GET, 2, 1, 2), (AG_GET, 3, 1, 2), (AG_GET, 0, 0, 2), (GRAD, 0, 2), (F_MM, 0, 2, 0, 1),
    (FINISH, 4), (F_R2, 0, 1), (FINISH, 5), (F_MM, 1, 4, 0), (F_SIB, 0, 2), (AG_GET, 1, 1, 3), (AG_GET, 2, 0, 3),
    (AG_GET, 2, 1, 3), (F_R3, 0, 1), (AG_GET, 3, 0, 3), (AG_GET, 3, 1, 3), (AG_GET, 0, 0, 3), (GRAD, 0, 3),
    (F_R1, 0, 2), (AG_GET, 4, 1, 1), (F_R4, 0, 1), (AG_GET, 4, 0, 1), (F_MM, 0, 3, 0, 1), (DRAIN, 16),
    (AG_GET, 5, 1, 1), (AG_GET, 5, 0, 1), (F_MM, 1, 1, 0, 1), (GRAD, 1, 1), (AG_GET, 2, 0, 4), (AG_GET, 0, 0, 4),
    (F_R2, 0, 2), (F_SIB, 1, 1), (AG_GET, 1, 1, 4), (F_SIB, 0, 3), (AG_GET, 3, 1, 4), (F_MM, 0, 4, 1),
    (AG_GET, 4, 0, 2), (GRAD, 0, 4), (F_R1, 1, 1), (AG_GET, 4, 1, 2), (F_SIB, 0, 4), (AG_GET, 5, 0, 2), (F_R1, 0, 3),
    (F_R3, 0, 2), (DRAIN, 16), (AG_GET, 5, 1, 2), (F_MM, 1, 2, 0, 1), (AG_GET, 4, 0, 3), (GRAD, 1, 2),
    (AG_GET, 4, 1, 3), (F_R2, 1, 1), (AG_GET, 5, 0, 3), (F_SIB, 1, 2), (F_R2, 0, 3), (F_R1, 0, 4), (F_R4, 0, 2),
    (AG_GET, 5, 1, 3), (F_MM, 1, 3, 0, 1), (F_R3, 1, 1), (GRAD, 1, 3), (F_R1, 1, 2), (F_R3, 0, 3), (F_SIB, 1, 3),
    (F_R4, 1, 1), (AG_GET, 5, 0, 4), (AG_GET, 4, 1, 4), (F_MM, 1, 4, 1), (F_R2, 0, 4), (GRAD, 1, 4), (F_R4, 0, 3),
    (F_SIB, 1, 4), (F_R1, 1, 3), (DRAIN, 16), (DRAIN, 16), (F_R2, 1, 2), (F_R3, 0, 4), (F_R1, 1, 4), (F_R4, 0, 4),
    (SWAP, 0), (F_R2, 1, 3), (SWAPPED, 0), (F_R3, 1, 2), (F_R2, 1, 4), (F_R4, 1, 2), (DRAIN, 16), (F_R3, 1, 3),
    (F_R3, 1, 4), (F_R4, 1, 3), (SWAP, 1), (SWAPPED, 1), (F_R4, 1, 4),
)


def gelu_parts(hidden):
    inner_arg = root_two_pi * (hidden + cubic_coef * hidden * hidden * hidden)
    bent_value = jnp.tanh(inner_arg)
    result = 0.5 * hidden * (1.0 + bent_value)
    slopes = 0.5 * (1.0 + bent_value) + 0.5 * hidden * (
        1.0 - bent_value * bent_value
    ) * root_two_pi * (1.0 + 3.0 * cubic_coef * hidden * hidden)
    return (result, slopes)


def halves(value):
    high = value.astype(BF16)
    return high, (value - high.astype(F32)).astype(BF16)


def kernel(
    tokens, up_weight, down_weight, cotangent,
    output, grad_tokens, grad_up, grad_down,
    gathered, raw, weights, partial, summed, spread, slope, fold, from_sib,
    near, far_x, far_y, last, ends, result, give, take, owed, paid, widths, grads,
    send_sem, recv_sem, local_sem,
):
    row, z, depth = lax.axis_index("row"), lax.axis_index("col"), lax.axis_index("depth")
    y, xl, xh, q = row // 2, row % 2, depth // 2, depth % 2
    xh_r, xh_l, xh_s = (xh + xl) % 2, (xh + xl + 1) % 2, (xh + xl + q) % 2
    sib = (row, z, xh * 2 + 1 - q)
    y_r, y_l = (((y + 1) % 4) * 2 + xl, z, depth), (((y + 3) % 4) * 2 + xl, z, depth)
    x_r, x_l = (y * 2 + 1 - xl, z, xh_r * 2 + q), (y * 2 + 1 - xl, z, xh_l * 2 + q)
    z_r, z_l = (row, (z + 1) % 8, depth), (row, (z + 7) % 8, depth)
    y_s = (((y + 1 + 2 * q) % 4) * 2 + xl, z, depth)
    x_s = (y * 2 + 1 - xl, z, xh_s * 2 + q)
    if Y_FIRST[1][3]:
        ring_ends = tuple((device, device[:2] + (device[2] + 1 - 2 * q,)) for device in (x_r, x_l))
    else:
        ring_ends = tuple((device, device[:2] + (device[2] + 1 - 2 * q,)) for device in (y_r, y_l))
    z_dev, z_sgn = (z_r, z_l), (1, 7)

    slots, pending = {}, []

    def remote(name, src, dst, device):
        at = slots.setdefault(name, len(slots))
        return pltpu.make_async_remote_copy(
            src_ref=src, dst_ref=dst, send_sem=send_sem.at[at], recv_sem=recv_sem.at[at],
            device_id=device, device_id_type=pl.DeviceIdType.MESH,
        )

    def send(name, src, dst, device):
        copy = remote(name, src, dst, device)
        copy.start()
        pending.append(copy)

    def arrive(name, dst):
        remote(name, dst, dst, sib).wait_recv()

    def rows(core, half):
        return pl.ds(pl.multiple_of(core * 96 + half * 48, 8), 48)

    def own_piece(a, g, dy, half):
        return gathered.at[a, g, (y + dy) % 4, rows(q, half)]

    def across_x(a, dy, half):
        piece = rows(q, half)
        src, dst = (gathered.at[a, g, (y + dy) % 4, piece] for g in range(2))
        send(("x", a, dy, half), src, dst, (x_r, x_l)[half])

    def to_core(a, g, dy, half):
        piece = own_piece(a, g, dy, half)
        send(("s", a, g, dy, half), piece, piece, sib)

    def own_x(a):
        if a == 1:
            loads[a].wait()
        for half in range(2):
            across_x(a, 0, half)

    def own_y(a):
        if a == 0:
            loads[a].wait()
        for halves_of in ((0, 1), (1, 0)):
            for way in range(2):
                piece = own_piece(a, 0, 0, halves_of[way])
                send(("y", a, way, halves_of[way]), piece, piece, (y_r, y_l)[way])

    def gy(a, way, half):
        dy = 3 if way == 0 else 1
        piece = own_piece(a, 0, dy, half)
        arrive(("y", a, way, half), piece)
        if half == way:
            send(("yf", a, way), piece, piece, (y_r, y_l)[way])
        across_x(a, dy, half)
        to_core(a, 0, dy, half)

    def gf(a, way):
        arrive(("yf", a, way), own_piece(a, 0, 2, way))
        across_x(a, 2, way)
        to_core(a, 0, 2, way)

    def gx(a, dy, half):
        arrive(("x", a, dy, half), own_piece(a, 1, dy, half))
        to_core(a, 1, dy, half)

    def split_weights(a):
        loads[2 + a].wait()
        high, low = halves(raw[a])
        weights[a, 0:UNITS] = high
        weights[a, UNITS:2 * UNITS] = high
        weights[a, 2 * UNITS:3 * UNITS] = low

    def prod(u):
        def nt(left, right):
            return lax.dot_general(left, right, (((1,), (1,)), ((), ())), preferred_element_type=F32)

        def product(a, blocks):
            high, low = halves(jnp.concatenate([gathered[a, g, (y + dy) % 4] for g, dy in blocks], axis=0))
            w_high, w_low = weights[a, 0:UNITS], weights[a, 2 * UNITS:3 * UNITS]
            return nt(high, w_high) + (nt(low, w_high) + nt(high, w_low))

        for a, g, dy in GROUPS[u]:
            if (g, dy) != (0, 0):
                for half in range(2):
                    arrive(("s", a, g, dy, half), gathered.at[a, g, (y + dy) % 4, rows(1 - q, half)])
        for a in range(2):
            blocks = [block for block in GROUPS[u] if block[0] == a]
            if blocks:
                total = product(a, [block[1:] for block in blocks])
                for n, block in enumerate(blocks):
                    partial[:, PLACE[block]] = total[n * BLOCK:(n + 1) * BLOCK].reshape(8, CHUNK, UNITS)
        rs_send(u, FIRST_WAY[u], 1)
        rs_send(u, 1 - FIRST_WAY[u], 2)

    def z_chunk(way, distance):
        return (z + z_sgn[way] * distance) % 8

    def rs_send(u, way, step):
        src, dst = partial.at[z_chunk(way, 5 - step), SPAN[u]], summed.at[way, step - 1, SPAN[u]]
        send(("rs", u, way, step), src, dst, z_dev[way])

    def rs_hop(u, way, step):
        arrive(("rs", u, way, step - 1), summed.at[way, step - 2, SPAN[u]])
        c = z_chunk(way, 5 - step)
        partial[c, SPAN[u]] = partial[c, SPAN[u]] + summed[way, step - 2, SPAN[u]]
        rs_send(u, way, step)

    def ag_send(u, way, k):
        piece = spread.at[z_chunk(1 - way, k - 1), SPAN[u]]
        send(("ag", u, way, k), piece, piece, z_dev[way])

    def ag_get(u, way, k):
        arrive(("ag", u, way, k), spread.at[z_chunk(1 - way, k), SPAN[u]])
        if k < 3 or (k == 3 and way == FIRST_WAY[u]):
            ag_send(u, way, k + 1)

    def finish(u):
        for way in range(2):
            arrive(("rs", u, way, 4), summed.at[way, 3, SPAN[u]])
        for a, g, dy in GROUPS[u]:
            at = PLACE[(a, g, dy)]
            total = partial[z, at] + summed[0, 3, at] + summed[1, 3, at]
            if a == 0:
                spread[z, at], slope[g, dy] = gelu_parts(total)
            else:
                spread[z, at] = total * slope[g, dy]
        for way in range(2):
            ag_send(u, way, 1)

    def spread_rows(a, chunks):
        return jnp.concatenate([spread[c, PLACE[(a, g, dy)]] for c in chunks for g, dy in BLOCKS], axis=0)

    def round_chunk(r, core):
        if r == 4:
            return (z + 4 * core) % 8
        return (z + r + (8 - 2 * r) * core) % 8

    def f_mm(a, r, *cores):
        high, low = halves(spread_rows(a, [round_chunk(r, core) for core in cores]))
        total = jnp.dot(jnp.concatenate([high, low, high], axis=1), weights[1 - a], preferred_element_type=F32)
        for i, core in enumerate(cores):
            for n, (g, dy) in enumerate(BLOCKS):
                at = i * BLOCK + n * CHUNK
                for side in range(2):
                    fold[r - 1, a, core, side, g, (y + dy) % 4] = total[at:at + CHUNK, side * UNITS:(side + 1) * UNITS]
        if 1 in cores:
            send(("fs", a, r), fold.at[r - 1, a, 1 - q], from_sib.at[r - 1, a], sib)

    def f_sib(a, r):
        i = r - 1
        arrive(("fs", a, r), from_sib.at[i, a])
        fold[i, a, q] = fold[i, a, q] + from_sib[i, a]
        if Y_FIRST[a][i]:
            send(("f1", a, r, 0), fold.at[i, a, q, 0, :, (y + 2) % 4], near.at[i, a, 0], y_r)
            send(("f1", a, r, 1), fold.at[i, a, q, 1, :, (y + 2) % 4], near.at[i, a, 1], y_l)
        else:
            send(("f1", a, r, 0), fold.at[i, a, q, 1 - xh, 0, 0:2], near.at[i, a, 0], x_r)
            send(("f1", a, r, 1), fold.at[i, a, q, 1 - xh, 0, 2:4], near.at[i, a, 1], x_l)

    def f_r1(a, r):
        i = r - 1
        for way, yy, xx in ((0, (y + 1) % 4, xh_r), (1, (y + 3) % 4, xh_l)):
            arrive(("f1", a, r, way), near.at[i, a, way])
            if Y_FIRST[a][i]:
                fold[i, a, q, way, :, yy] = fold[i, a, q, way, :, yy] + near[i, a, way]
                send(("f2", a, r, way), fold.at[i, a, q, :, :, yy], far_y.at[i, a, way], (y_r, y_l)[way])
            else:
                half = slice(2 * way, 2 * way + 2)
                fold[i, a, q, xx, 1, half] = fold[i, a, q, xx, 1, half] + near[i, a, way]
                send(("f2", a, r, way), fold.at[i, a, q, xx, 1], far_x.at[i, a, way], (x_r, x_l)[way])

    def f_r2(a, r):
        i = r - 1
        far = (far_x, far_y)[Y_FIRST[a][i]]
        for way in range(2):
            arrive(("f2", a, r, way), far.at[i, a, way])
        if Y_FIRST[a][i]:
            fold[i, a, q, :, :, y] = fold[i, a, q, :, :, y] + far[i, a, 0] + far[i, a, 1]
            send(("f3", a, r), fold.at[i, a, q, 1 - xh, 0, y], last.at[i, a], x_s)
        else:
            fold[i, a, q, xh, 0] = fold[i, a, q, xh, 0] + far[i, a, 0] + far[i, a, 1]
            send(("f3", a, r), fold.at[i, a, q, xh, 0, (y + 2) % 4], last.at[i, a], y_s)

    def columns(value, core):
        first, second = value[..., 0:BLOCK], value[..., BLOCK:2 * BLOCK]
        return jnp.where(jnp.full(first.shape, core, jnp.int32) == 0, first, second)

    def f_r3(a, r):
        i = r - 1
        arrive(("f3", a, r), last.at[i, a])
        if (a, r) == (1, 4):
            last_hop()
            return
        if Y_FIRST[a][i]:
            fold[i, a, q, xh_s, 1, y] = fold[i, a, q, xh_s, 1, y] + last[i, a]
            send(("f4", a, r, 0), fold.at[i, a, q, xh_r, 1, y], ends.at[i, a, 0], x_r)
            send(("f4", a, r, 1), fold.at[i, a, q, xh_l, 1, y], ends.at[i, a, 1], x_l)
        else:
            ys = (y + 1 + 2 * q) % 4
            fold[i, a, q, xh, 0, ys] = fold[i, a, q, xh, 0, ys] + last[i, a]
            send(("f4", a, r, 0), fold.at[i, a, q, xh, 0, (y + 1) % 4], ends.at[i, a, 0], y_r)
            send(("f4", a, r, 1), fold.at[i, a, q, xh, 0, (y + 3) % 4], ends.at[i, a, 1], y_l)

    def last_hop():
        if Y_FIRST[1][3]:
            fold[3, 1, q, xh_s, 1, y] = fold[3, 1, q, xh_s, 1, y] + last[3, 1]
            pieces = fold[3, 1, q, xh_r, 1, y], fold[3, 1, q, xh_l, 1, y]
        else:
            ys = (y + 1 + 2 * q) % 4
            fold[3, 1, q, xh, 0, ys] = fold[3, 1, q, xh, 0, ys] + last[3, 1]
            pieces = fold[3, 1, q, xh, 0, (y + 1) % 4], fold[3, 1, q, xh, 0, (y + 3) % 4]
        for way in range(2):
            for kind in range(2):
                owed[way, kind] = columns(pieces[way], (1 - q) if kind else q)
                send(("f4", way, kind), owed.at[way, kind], paid.at[way, kind], ring_ends[way][kind])
        owed[2, 0] = columns(fold[3, 1, q, xh, 0, y], 1 - q)
        send(("f5",), owed.at[2, 0], paid.at[2, 0], sib)

    def last_sum():
        for way in range(2):
            for kind in range(2):
                arrive(("f4", way, kind), paid.at[way, kind])
        arrive(("f5",), paid.at[2, 0])
        for kind, base in ((0, columns(fold[3, 1, q, xh, 0, y], q)), (1, paid[2, 0])):
            at = pl.ds(pl.multiple_of(round_chunk(4, (1 - q) if kind else q) * CHUNK, 8), CHUNK)
            widths[1, at, :] = base + paid[0, kind] + paid[1, kind]
        stores[1].start()

    def f_r4(a, r):
        i = r - 1
        if (a, r) == (1, 4):
            last_sum()
            return
        arrive(("f4", a, r, 0), ends.at[i, a, 0])
        arrive(("f4", a, r, 1), ends.at[i, a, 1])
        result[a, i] = fold[i, a, q, xh, 0, y] + ends[i, a, 0] + ends[i, a, 1]

    def swap(a):
        rounds = 4 - a
        for i in range(rounds):
            give[a, i] = columns(result[a, i], 1 - q)
        send(("swap", a), give.at[a, 0:rounds], take.at[a, 0:rounds], sib)
        for i in range(rounds):
            at = pl.ds(pl.multiple_of(round_chunk(i + 1, q) * CHUNK, 8), CHUNK)
            widths[a, at, :] = columns(result[a, i], q)

    def swapped(a):
        rounds = 4 - a
        arrive(("swap", a), take.at[a, 0:rounds])
        for i in range(rounds):
            at = pl.ds(pl.multiple_of(round_chunk(i + 1, 1 - q) * CHUNK, 8), CHUNK)
            widths[a, at, :] = take[a, i]
        if a == 0:
            stores[0].start()

    rounds_done = [0, 0]

    def grad(a, r):
        chunks = (round_chunk(r, 0), round_chunk(r, 1))
        left = spread_rows(a, chunks).T
        right = jnp.concatenate([
            gathered[1 - a, g, (y + dy) % 4, pl.ds(pl.multiple_of(c * CHUNK, 8), CHUNK), :]
            for c in chunks for g, dy in BLOCKS
        ], axis=0)
        l_high, l_low = halves(left)
        r_high, r_low = halves(right)
        term = jnp.dot(
            jnp.concatenate([l_high, l_low, l_high], axis=1), jnp.concatenate([r_high, r_high, r_low], axis=0),
            preferred_element_type=F32)
        grads[a] = term if rounds_done[a] == 0 else grads[a] + term
        rounds_done[a] += 1
        if rounds_done[a] == 4:
            stores[2 + a].start()

    def drain(count):
        for copy in pending[:count]:
            copy.wait_send()
        del pending[:count]

    loads = [
        pltpu.make_async_copy(src, dst, local_sem.at[i])
        for i, (src, dst) in enumerate((
            (tokens, gathered.at[0, 0, y]), (cotangent, gathered.at[1, 0, y]),
            (up_weight, raw.at[0]), (down_weight, raw.at[1]),
        ))
    ]
    stores = [
        pltpu.make_async_copy(src, dst, local_sem.at[4 + i])
        for i, (src, dst) in enumerate((
            (widths.at[0], output), (widths.at[1], grad_tokens), (grads.at[0], grad_down), (grads.at[1], grad_up),
        ))
    ]
    for load in loads:
        load.start()
    barrier = pltpu.get_barrier_semaphore()
    partners = (sib, y_r, y_l, x_r, x_l, z_r, z_l, ring_ends[0][1], ring_ends[1][1])
    for device in partners:
        pl.semaphore_signal(barrier, inc=1, device_id=device, device_id_type=pl.DeviceIdType.MESH)
    pl.semaphore_wait(barrier, len(partners))

    steps = (
        own_x, own_y, gy, gf, gx, split_weights, prod, rs_hop, finish, ag_get,
        f_mm, f_sib, f_r1, f_r2, f_r3, f_r4, swap, swapped, grad, drain,
    )
    for step, *at in ORDER:
        steps[step](*at)
    drain(len(pending))
    for store in stores:
        store.wait()
    assert len(slots) <= SLOTS, len(slots)


def copy_kernel(*refs):
    sources, targets, held, sem = refs[:4], refs[4:8], refs[8:12], refs[12]
    loads, stores = [], []
    for src, dst, hold in zip(sources, targets, held):
        parts = 4 if src.shape[0] == UNITS else 1
        size = src.shape[0] // parts
        for part in range(parts):
            at, n = pl.ds(part * size, size), len(loads)
            loads.append(pltpu.make_async_copy(src.at[at], hold.at[at], sem.at[0, n]))
            stores.append(pltpu.make_async_copy(hold.at[at], dst.at[at], sem.at[1, n]))
    for load in loads:
        load.start()
    for load, store in zip(loads, stores):
        load.wait()
        store.start()
    for store in stores:
        store.wait()


def shards(tokens, up_weight, down_weight, cotangent):
    anywhere, piece = pl.BlockSpec(memory_space=pl.ANY), (CHUNK, UNITS)
    shapes = (
        jax.ShapeDtypeStruct((BLOCK, BLOCK), F32),
        jax.ShapeDtypeStruct((BLOCK, BLOCK), F32),
        jax.ShapeDtypeStruct((UNITS, WIDTH), F32),
        jax.ShapeDtypeStruct((UNITS, WIDTH), F32),
    )
    results = pl.pallas_call(
        kernel,
        out_shape=shapes,
        in_specs=[anywhere] * 4,
        out_specs=(anywhere,) * 4,
        scratch_shapes=[
            pltpu.VMEM((2, 2, 4, BLOCK, WIDTH), F32),
            pltpu.VMEM((2, UNITS, WIDTH), F32),
            pltpu.VMEM((2, 3 * UNITS, WIDTH), BF16),
            pltpu.VMEM((8, 16) + piece, F32),
            pltpu.VMEM((2, 4, 16) + piece, F32),
            pltpu.VMEM((8, 16) + piece, F32),
            pltpu.VMEM((2, 4) + piece, F32),
            pltpu.VMEM((4, 2, 2, 2, 2, 4) + piece, F32),
            pltpu.VMEM((4, 2, 2, 2, 4) + piece, F32),
            pltpu.VMEM((4, 2, 2, 2) + piece, F32),
            pltpu.VMEM((4, 2, 2, 4) + piece, F32),
            pltpu.VMEM((4, 2, 2, 2, 2) + piece, F32),
            pltpu.VMEM((4, 2) + piece, F32),
            pltpu.VMEM((4, 2, 2) + piece, F32),
            pltpu.VMEM((2, 4) + piece, F32),
            pltpu.VMEM((2, 4, CHUNK, BLOCK), F32),
            pltpu.VMEM((2, 4, CHUNK, BLOCK), F32),
            pltpu.VMEM((3, 2, CHUNK, BLOCK), F32),
            pltpu.VMEM((3, 2, CHUNK, BLOCK), F32),
            pltpu.VMEM((2, BLOCK, BLOCK), F32),
            pltpu.VMEM((2, UNITS, WIDTH), F32),
            pltpu.SemaphoreType.DMA((SLOTS,)),
            pltpu.SemaphoreType.DMA((SLOTS,)),
            pltpu.SemaphoreType.DMA((8,)),
        ],
        compiler_params=pltpu.CompilerParams(
            collective_id=0, has_side_effects=True, vmem_limit_bytes=62 * 1024 * 1024),
        cost_estimate=pl.CostEstimate(flops=16_300_000_000, bytes_accessed=6_000_000, transcendentals=73728),
    )(tokens, up_weight, down_weight, cotangent)
    return pl.pallas_call(
        copy_kernel,
        out_shape=shapes,
        in_specs=[anywhere] * 4,
        out_specs=(anywhere,) * 4,
        scratch_shapes=[pltpu.VMEM(shape.shape, F32) for shape in shapes] + [pltpu.SemaphoreType.DMA((2, 10))],
    )(*results)


def solution(mesh):
    return jax.shard_map(
        shards,
        mesh=mesh,
        in_specs=(
            P("row", "col"),
            P(("row", "depth"), "col"),
            P(("row", "depth"), "col"),
            P("row", "col"),
        ),
        out_specs=(
            P("row", ("col", "depth")),
            P("row", ("col", "depth")),
            P(("row", "depth"), "col"),
            P(("row", "depth"), "col"),
        ),
        check_vma=False,
    )
```

```python
import jax
import jax.numpy as jnp
from jax import lax
from jax.experimental import pallas as pl
from jax.experimental.pallas import tpu as pltpu
from jax.sharding import PartitionSpec as P

F32, BF16 = jnp.float32, jnp.bfloat16
root_two_pi = 0.7978845608028654
cubic_coef = 0.044715

SLOTS = 260
BLOCK, WIDTH, UNITS, CHUNK = 192, 768, 384, 24
GROUPS = (
    ((0, 0, 0), (1, 0, 0)),
    ((0, 1, 0), (1, 1, 0)),
    ((0, 0, 1), (0, 0, 3)),
    ((0, 1, 1), (0, 1, 3)),
    ((0, 0, 2), (0, 1, 2)),
    ((1, 0, 1), (1, 0, 3)),
    ((1, 1, 1), (1, 1, 3)),
    ((1, 0, 2), (1, 1, 2)),
)
FIRST_WAY = (0, 1, 0, 1, 0, 1, 0, 1)
PLACE = {block: at for at, block in enumerate(block for group in GROUPS for block in group)}
SPAN = tuple(slice(PLACE[group[0]], PLACE[group[0]] + len(group)) for group in GROUPS)
BLOCKS = tuple((g, dy) for g in range(2) for dy in range(4))
Y_FIRST = ((0, 1, 0, 1), (0, 1, 0, 1))
SPLIT = ((1, 3), (1, 4))
(
    OWN_X, OWN_Y, GY, GF, GX, SPLIT_WEIGHTS, PROD, RS_HOP, FINISH, AG_GET, F_MM, F_SIB, F_R1, F_R2, F_R3, F_R4,
    SWAP, SWAPPED, GRAD, DRAIN,
) = range(20)
ORDER = (
    (OWN_Y, 0), (OWN_X, 1), (SPLIT_WEIGHTS, 1), (SPLIT_WEIGHTS, 0), (PROD, 0), (OWN_X, 0), (DRAIN, 16), (GX, 1, 0, 1),
    (GY, 0, 1, 1), (GX, 1, 0, 0), (RS_HOP, 0, 0, 2), (RS_HOP, 0, 1, 3), (GY, 0, 0, 0), (DRAIN, 16), (GY, 0, 1, 0),
    (GY, 0, 0, 1), (GX, 0, 0, 0), (OWN_Y, 1), (GX, 0, 0, 1), (RS_HOP, 0, 0, 3), (RS_HOP, 0, 1, 4), (PROD, 2),
    (PROD, 1), (GX, 0, 3, 0), (RS_HOP, 0, 0, 4), (GF, 0, 1), (RS_HOP, 2, 0, 2), (RS_HOP, 2, 1, 3), (DRAIN, 16),
    (GF, 0, 0), (GX, 0, 1, 1), (GX, 0, 3, 1), (GX, 0, 1, 0), (RS_HOP, 1, 0, 3), (GY, 1, 0, 0), (DRAIN, 16),
    (RS_HOP, 1, 1, 2), (GY, 1, 1, 1), (FINISH, 0), (PROD, 3), (GY, 1, 0, 1), (RS_HOP, 2, 0, 3), (GX, 0, 2, 0),
    (RS_HOP, 2, 1, 4), (GX, 0, 2, 1), (PROD, 4), (GF, 1, 1), (GX, 1, 3, 1), (GX, 1, 1, 1), (RS_HOP, 3, 1, 2),
    (RS_HOP, 1, 1, 3), (RS_HOP, 1, 0, 4), (GY, 1, 1, 0), (AG_GET, 0, 0, 1), (AG_GET, 0, 1, 1), (RS_HOP, 4, 0, 2),
    (RS_HOP, 4, 1, 3), (RS_HOP, 2, 0, 4), (RS_HOP, 1, 1, 4), (GF, 1, 0), (PROD, 5), (RS_HOP, 3, 1, 3), (GX, 1, 3, 0),
    (DRAIN, 16), (DRAIN, 16), (RS_HOP, 4, 0, 3), (GX, 1, 2, 1), (GX, 1, 1, 0), (PROD, 6), (AG_GET, 0, 1, 2),
    (AG_GET, 0, 0, 2), (GX, 1, 2, 0), (RS_HOP, 3, 0, 3), (RS_HOP, 4, 0, 4), (RS_HOP, 6, 1, 3), (RS_HOP, 3, 1, 4),
    (FINISH, 1), (PROD, 7), (RS_HOP, 3, 0, 4), (RS_HOP, 4, 1, 4), (FINISH, 2), (AG_GET, 1, 1, 1), (AG_GET, 1, 0, 1),
    (RS_HOP, 6, 0, 2), (FINISH, 4), (AG_GET, 0, 0, 3), (FINISH, 3), (DRAIN, 16), (RS_HOP, 5, 1, 2), (AG_GET, 4, 1, 1),
    (AG_GET, 4, 0, 1), (AG_GET, 2, 1, 1), (AG_GET, 2, 0, 1), (AG_GET, 3, 1, 1), (AG_GET, 3, 0, 1), (F_MM, 0, 1, 0, 1),
    (RS_HOP, 7, 0, 3), (DRAIN, 16), (RS_HOP, 5, 0, 3), (RS_HOP, 6, 0, 3), (AG_GET, 2, 1, 2), (AG_GET, 1, 0, 2),
    (RS_HOP, 7, 1, 2), (F_SIB, 0, 1), (RS_HOP, 5, 1, 3), (GRAD, 0, 1), (AG_GET, 4, 0, 2), (AG_GET, 3, 0, 2),
    (DRAIN, 16), (AG_GET, 3, 1, 2), (F_R1, 0, 1), (RS_HOP, 7, 1, 3), (AG_GET, 4, 1, 2), (AG_GET, 2, 0, 2),
    (AG_GET, 1, 1, 2), (F_MM, 0, 2, 0, 1), (F_MM, 0, 4, 0), (RS_HOP, 5, 0, 4), (F_SIB, 0, 2), (RS_HOP, 7, 0, 4),
    (F_R2, 0, 1), (RS_HOP, 6, 1, 4), (AG_GET, 1, 0, 3), (RS_HOP, 7, 1, 4), (GRAD, 0, 2), (RS_HOP, 5, 1, 4),
    (AG_GET, 1, 1, 3), (AG_GET, 3, 0, 3), (AG_GET, 0, 1, 3), (AG_GET, 0, 0, 4), (AG_GET, 2, 1, 3), (RS_HOP, 6, 0, 4),
    (AG_GET, 4, 0, 3), (AG_GET, 4, 1, 3), (AG_GET, 3, 1, 3), (F_R1, 0, 2), (F_R3, 0, 1), (AG_GET, 2, 0, 3),
    (F_MM, 0, 3, 0, 1), (GRAD, 0, 3), (FINISH, 5), (F_R4, 0, 1), (F_R2, 0, 2), (AG_GET, 1, 1, 4), (FINISH, 6),
    (F_SIB, 0, 3), (FINISH, 7), (F_MM, 1, 4, 0), (F_R3, 0, 2), (AG_GET, 3, 1, 4), (AG_GET, 2, 0, 4),
    (AG_GET, 5, 1, 1), (AG_GET, 4, 0, 4), (F_MM, 0, 4, 1), (F_R1, 0, 3), (AG_GET, 5, 0, 1), (GRAD, 0, 4),
    (AG_GET, 6, 1, 1), (F_SIB, 0, 4), (AG_GET, 7, 1, 1), (AG_GET, 6, 0, 1), (AG_GET, 7, 0, 1), (F_MM, 1, 1, 0, 1),
    (F_R2, 0, 3), (AG_GET, 5, 0, 2), (AG_GET, 5, 1, 2), (GRAD, 1, 1), (F_R1, 0, 4), (AG_GET, 7, 1, 2),
    (AG_GET, 6, 1, 2), (F_SIB, 1, 1), (F_R3, 0, 3), (AG_GET, 6, 0, 2), (AG_GET, 7, 0, 2), (F_MM, 1, 2, 0, 1),
    (AG_GET, 5, 1, 3), (GRAD, 1, 2), (AG_GET, 7, 1, 3), (F_SIB, 1, 2), (AG_GET, 5, 0, 3), (F_R1, 1, 1),
    (AG_GET, 6, 0, 3), (AG_GET, 6, 1, 3), (AG_GET, 7, 0, 3), (F_MM, 1, 3, 0, 1), (F_R2, 0, 4), (F_R1, 1, 2),
    (AG_GET, 5, 1, 4), (AG_GET, 6, 0, 4), (AG_GET, 7, 1, 4), (F_MM, 1, 4, 1), (F_SIB, 1, 3), (GRAD, 1, 4),
    (F_SIB, 1, 4), (DRAIN, 16), (F_R2, 1, 2), (F_R2, 1, 1), (F_R4, 0, 2), (F_R1, 1, 3), (F_R1, 1, 4), (F_R4, 0, 3),
    (F_R3, 0, 4), (GRAD, 1, 3), (F_R2, 1, 3), (F_R3, 1, 2), (F_R3, 1, 1), (F_R2, 1, 4), (DRAIN, 16), (F_R4, 0, 4),
    (SWAP, 0), (F_R3, 1, 3), (DRAIN, 16), (F_R4, 1, 2), (F_R4, 1, 1), (F_R3, 1, 4), (F_R4, 1, 3), (SWAP, 1),
    (SWAPPED, 0), (DRAIN, 16), (DRAIN, 16), (SWAPPED, 1), (F_R4, 1, 4),
)


def gelu_parts(hidden):
    inner_arg = root_two_pi * (hidden + cubic_coef * hidden * hidden * hidden)
    bent_value = jnp.tanh(inner_arg)
    result = 0.5 * hidden * (1.0 + bent_value)
    slopes = 0.5 * (1.0 + bent_value) + 0.5 * hidden * (
        1.0 - bent_value * bent_value
    ) * root_two_pi * (1.0 + 3.0 * cubic_coef * hidden * hidden)
    return (result, slopes)


def halves(value):
    high = value.astype(BF16)
    return high, (value - high.astype(F32)).astype(BF16)


def kernel(
    tokens, up_weight, down_weight, cotangent,
    output, grad_tokens, grad_up, grad_down,
    gathered, raw, weights, partial, summed, spread, slope, fold, from_sib,
    near, far_x, far_y, last, ends, result, give, take, owed, paid, widths, grads,
    send_sem, recv_sem, local_sem,
):
    row, z, depth = lax.axis_index("row"), lax.axis_index("col"), lax.axis_index("depth")
    y, xl, xh, q = row // 2, row % 2, depth // 2, depth % 2
    xh_r, xh_l, xh_s = (xh + xl) % 2, (xh + xl + 1) % 2, (xh + xl + q) % 2
    sib = (row, z, xh * 2 + 1 - q)
    y_r, y_l = (((y + 1) % 4) * 2 + xl, z, depth), (((y + 3) % 4) * 2 + xl, z, depth)
    x_r, x_l = (y * 2 + 1 - xl, z, xh_r * 2 + q), (y * 2 + 1 - xl, z, xh_l * 2 + q)
    z_r, z_l = (row, (z + 1) % 8, depth), (row, (z + 7) % 8, depth)
    y_s = (((y + 1 + 2 * q) % 4) * 2 + xl, z, depth)
    x_s = (y * 2 + 1 - xl, z, xh_s * 2 + q)
    across = tuple(device[:2] + (device[2] + 1 - 2 * q,) for device in (x_r, x_l, y_r, y_l))
    z_dev, z_sgn = (z_r, z_l), (1, 7)

    slots, pending = {}, []

    def remote(name, src, dst, device):
        at = slots.setdefault(name, len(slots))
        return pltpu.make_async_remote_copy(
            src_ref=src, dst_ref=dst, send_sem=send_sem.at[at], recv_sem=recv_sem.at[at],
            device_id=device, device_id_type=pl.DeviceIdType.MESH,
        )

    def send(name, src, dst, device):
        copy = remote(name, src, dst, device)
        copy.start()
        pending.append(copy)

    def arrive(name, dst):
        remote(name, dst, dst, sib).wait_recv()

    def rows(core, half):
        return pl.ds(pl.multiple_of(core * 96 + half * 48, 8), 48)

    def own_piece(a, g, dy, half):
        return gathered.at[a, g, (y + dy) % 4, rows(q, half)]

    def across_x(a, dy, half):
        piece = rows(q, half)
        src, dst = (gathered.at[a, g, (y + dy) % 4, piece] for g in range(2))
        send(("x", a, dy, half), src, dst, (x_r, x_l)[half])

    def to_core(a, g, dy, half):
        piece = own_piece(a, g, dy, half)
        send(("s", a, g, dy, half), piece, piece, sib)

    def own_x(a):
        if a == 1:
            loads[a].wait()
        for half in range(2):
            across_x(a, 0, half)

    def own_y(a):
        if a == 0:
            loads[a].wait()
        for halves_of in ((0, 1), (1, 0)):
            for way in range(2):
                piece = own_piece(a, 0, 0, halves_of[way])
                send(("y", a, way, halves_of[way]), piece, piece, (y_r, y_l)[way])

    def gy(a, way, half):
        dy = 3 if way == 0 else 1
        piece = own_piece(a, 0, dy, half)
        arrive(("y", a, way, half), piece)
        if half == way:
            send(("yf", a, way), piece, piece, (y_r, y_l)[way])
        across_x(a, dy, half)
        to_core(a, 0, dy, half)

    def gf(a, way):
        arrive(("yf", a, way), own_piece(a, 0, 2, way))
        across_x(a, 2, way)
        to_core(a, 0, 2, way)

    def gx(a, dy, half):
        arrive(("x", a, dy, half), own_piece(a, 1, dy, half))
        to_core(a, 1, dy, half)

    def split_weights(a):
        loads[2 + a].wait()
        high, low = halves(raw[a])
        weights[a, 0:UNITS] = high
        weights[a, UNITS:2 * UNITS] = high
        weights[a, 2 * UNITS:3 * UNITS] = low

    def prod(u):
        def nt(left, right):
            return lax.dot_general(left, right, (((1,), (1,)), ((), ())), preferred_element_type=F32)

        def product(a, blocks):
            high, low = halves(jnp.concatenate([gathered[a, g, (y + dy) % 4] for g, dy in blocks], axis=0))
            w_high, w_low = weights[a, 0:UNITS], weights[a, 2 * UNITS:3 * UNITS]
            return nt(high, w_high) + (nt(low, w_high) + nt(high, w_low))

        for a, g, dy in GROUPS[u]:
            if (g, dy) != (0, 0):
                for half in range(2):
                    arrive(("s", a, g, dy, half), gathered.at[a, g, (y + dy) % 4, rows(1 - q, half)])
        for a in range(2):
            blocks = [block for block in GROUPS[u] if block[0] == a]
            if blocks:
                total = product(a, [block[1:] for block in blocks])
                for n, block in enumerate(blocks):
                    partial[:, PLACE[block]] = total[n * BLOCK:(n + 1) * BLOCK].reshape(8, CHUNK, UNITS)
        rs_send(u, FIRST_WAY[u], 1)
        rs_send(u, 1 - FIRST_WAY[u], 2)

    def z_chunk(way, distance):
        return (z + z_sgn[way] * distance) % 8

    def rs_send(u, way, step):
        src, dst = partial.at[z_chunk(way, 5 - step), SPAN[u]], summed.at[way, step - 1, SPAN[u]]
        send(("rs", u, way, step), src, dst, z_dev[way])

    def rs_hop(u, way, step):
        arrive(("rs", u, way, step - 1), summed.at[way, step - 2, SPAN[u]])
        c = z_chunk(way, 5 - step)
        partial[c, SPAN[u]] = partial[c, SPAN[u]] + summed[way, step - 2, SPAN[u]]
        rs_send(u, way, step)

    def ag_send(u, way, k):
        piece = spread.at[z_chunk(1 - way, k - 1), SPAN[u]]
        send(("ag", u, way, k), piece, piece, z_dev[way])

    def ag_get(u, way, k):
        arrive(("ag", u, way, k), spread.at[z_chunk(1 - way, k), SPAN[u]])
        if k < 3 or (k == 3 and way == FIRST_WAY[u]):
            ag_send(u, way, k + 1)

    def finish(u):
        for way in range(2):
            arrive(("rs", u, way, 4), summed.at[way, 3, SPAN[u]])
        for a, g, dy in GROUPS[u]:
            at = PLACE[(a, g, dy)]
            total = partial[z, at] + summed[0, 3, at] + summed[1, 3, at]
            if a == 0:
                spread[z, at], slope[g, dy] = gelu_parts(total)
            else:
                spread[z, at] = total * slope[g, dy]
        for way in range(2):
            ag_send(u, way, 1)

    def spread_rows(a, chunks):
        return jnp.concatenate([spread[c, PLACE[(a, g, dy)]] for c in chunks for g, dy in BLOCKS], axis=0)

    def round_chunk(r, core):
        if r == 4:
            return (z + 4 * core) % 8
        return (z + r + (8 - 2 * r) * core) % 8

    def f_mm(a, r, *cores):
        high, low = halves(spread_rows(a, [round_chunk(r, core) for core in cores]))
        total = jnp.dot(jnp.concatenate([high, low, high], axis=1), weights[1 - a], preferred_element_type=F32)
        for i, core in enumerate(cores):
            for n, (g, dy) in enumerate(BLOCKS):
                at = i * BLOCK + n * CHUNK
                for side in range(2):
                    fold[r - 1, a, core, side, g, (y + dy) % 4] = total[at:at + CHUNK, side * UNITS:(side + 1) * UNITS]
        if 1 in cores:
            send(("fs", a, r), fold.at[r - 1, a, 1 - q], from_sib.at[r - 1, a], sib)

    def parts(a, r):
        y_first = Y_FIRST[a][r - 1]
        if (a, r) in SPLIT:
            return (slice(0, 16), y_first), (slice(16, CHUNK), 1 - y_first)
        return ((slice(0, CHUNK), y_first),)

    def f_sib(a, r):
        i = r - 1
        arrive(("fs", a, r), from_sib.at[i, a])
        fold[i, a, q] = fold[i, a, q] + from_sib[i, a]
        for at, y_first in parts(a, r):
            for way in range(2):
                if y_first:
                    piece, device = fold.at[i, a, q, way, :, (y + 2) % 4, at], (y_r, y_l)[way]
                else:
                    piece, device = fold.at[i, a, q, 1 - xh, 0, 2 * way:2 * way + 2, at], (x_r, x_l)[way]
                send(("f1", a, r, way, y_first), piece, near.at[i, a, way, :, at], device)

    def f_r1(a, r):
        i = r - 1
        for at, y_first in parts(a, r):
            for way, yy, xx in ((0, (y + 1) % 4, xh_r), (1, (y + 3) % 4, xh_l)):
                arrive(("f1", a, r, way, y_first), near.at[i, a, way, :, at])
                if y_first:
                    fold[i, a, q, way, :, yy, at] = fold[i, a, q, way, :, yy, at] + near[i, a, way, :, at]
                    piece, dst, device = fold.at[i, a, q, :, :, yy, at], far_y.at[i, a, way, :, :, at], (y_r, y_l)[way]
                else:
                    half = slice(2 * way, 2 * way + 2)
                    fold[i, a, q, xx, 1, half, at] = fold[i, a, q, xx, 1, half, at] + near[i, a, way, :, at]
                    piece, dst, device = fold.at[i, a, q, xx, 1, :, at], far_x.at[i, a, way, :, at], (x_r, x_l)[way]
                send(("f2", a, r, way, y_first), piece, dst, device)

    def f_r2(a, r):
        i = r - 1
        for at, y_first in parts(a, r):
            if y_first:
                for way in range(2):
                    arrive(("f2", a, r, way, y_first), far_y.at[i, a, way, :, :, at])
                fold[i, a, q, :, :, y, at] = fold[i, a, q, :, :, y, at] + far_y[i, a, 0, :, :, at] + far_y[i, a, 1, :, :, at]
                piece, device = fold.at[i, a, q, 1 - xh, 0, y, at], x_s
            else:
                for way in range(2):
                    arrive(("f2", a, r, way, y_first), far_x.at[i, a, way, :, at])
                fold[i, a, q, xh, 0, :, at] = fold[i, a, q, xh, 0, :, at] + far_x[i, a, 0, :, at] + far_x[i, a, 1, :, at]
                piece, device = fold.at[i, a, q, xh, 0, (y + 2) % 4, at], y_s
            send(("f3", a, r, y_first), piece, last.at[i, a, at], device)

    def columns(value, core):
        first, second = value[..., 0:BLOCK], value[..., BLOCK:2 * BLOCK]
        return jnp.where(jnp.full(first.shape, core, jnp.int32) == 0, first, second)

    def ends_from(a, r, at, y_first):
        i = r - 1
        arrive(("f3", a, r, y_first), last.at[i, a, at])
        if y_first:
            fold[i, a, q, xh_s, 1, y, at] = fold[i, a, q, xh_s, 1, y, at] + last[i, a, at]
            return tuple(fold.at[i, a, q, xx, 1, y, at] for xx in (xh_r, xh_l)), (x_r, x_l)
        ys = (y + 1 + 2 * q) % 4
        fold[i, a, q, xh, 0, ys, at] = fold[i, a, q, xh, 0, ys, at] + last[i, a, at]
        return tuple(fold.at[i, a, q, xh, 0, (y + dy) % 4, at] for dy in (1, 3)), (y_r, y_l)

    def f_r3(a, r):
        i = r - 1
        for at, y_first in parts(a, r):
            pieces, devices = ends_from(a, r, at, y_first)
            for way in range(2):
                if (a, r) != (1, 4):
                    send(("f4", a, r, way, y_first), pieces[way], ends.at[i, a, way, at], devices[way])
                    continue
                for kind in range(2):
                    owed[way, kind, at] = columns(pieces[way][...], (1 - q) if kind else q)
                    device = devices[way][:2] + (devices[way][2] + kind * (1 - 2 * q),)
                    send(("f4", way, kind, y_first), owed.at[way, kind, at], paid.at[way, kind, at], device)
        if (a, r) == (1, 4):
            owed[2, 0] = columns(fold[3, 1, q, xh, 0, y], 1 - q)
            send(("f5",), owed.at[2, 0], paid.at[2, 0], sib)

    def f_r4(a, r):
        i = r - 1
        if (a, r) != (1, 4):
            for at, y_first in parts(a, r):
                for way in range(2):
                    arrive(("f4", a, r, way, y_first), ends.at[i, a, way, at])
            result[a, i] = fold[i, a, q, xh, 0, y] + ends[i, a, 0] + ends[i, a, 1]
            return
        for at, y_first in parts(a, r):
            for way in range(2):
                for kind in range(2):
                    arrive(("f4", way, kind, y_first), paid.at[way, kind, at])
        arrive(("f5",), paid.at[2, 0])
        for kind, base in ((0, columns(fold[3, 1, q, xh, 0, y], q)), (1, paid[2, 0])):
            at = pl.ds(pl.multiple_of(round_chunk(4, (1 - q) if kind else q) * CHUNK, 8), CHUNK)
            widths[1, at, :] = base + paid[0, kind] + paid[1, kind]
        stores[1].start()

    def swap(a):
        rounds = 4 - a
        for i in range(rounds):
            give[a, i] = columns(result[a, i], 1 - q)
        send(("swap", a), give.at[a, 0:rounds], take.at[a, 0:rounds], sib)
        for i in range(rounds):
            at = pl.ds(pl.multiple_of(round_chunk(i + 1, q) * CHUNK, 8), CHUNK)
            widths[a, at, :] = columns(result[a, i], q)

    def swapped(a):
        rounds = 4 - a
        arrive(("swap", a), take.at[a, 0:rounds])
        for i in range(rounds):
            at = pl.ds(pl.multiple_of(round_chunk(i + 1, 1 - q) * CHUNK, 8), CHUNK)
            widths[a, at, :] = take[a, i]
        if a == 0:
            stores[0].start()

    rounds_done = [0, 0]

    def grad(a, r):
        chunks = (round_chunk(r, 0), round_chunk(r, 1))
        left = spread_rows(a, chunks).T
        right = jnp.concatenate([
            gathered[1 - a, g, (y + dy) % 4, pl.ds(pl.multiple_of(c * CHUNK, 8), CHUNK), :]
            for c in chunks for g, dy in BLOCKS
        ], axis=0)
        l_high, l_low = halves(left)
        r_high, r_low = halves(right)
        term = jnp.dot(
            jnp.concatenate([l_high, l_low, l_high], axis=1), jnp.concatenate([r_high, r_high, r_low], axis=0),
            preferred_element_type=F32)
        grads[a] = term if rounds_done[a] == 0 else grads[a] + term
        rounds_done[a] += 1
        if rounds_done[a] == 4:
            stores[2 + a].start()

    def drain(count):
        for copy in pending[:count]:
            copy.wait_send()
        del pending[:count]

    loads = [
        pltpu.make_async_copy(src, dst, local_sem.at[i])
        for i, (src, dst) in enumerate((
            (tokens, gathered.at[0, 0, y]), (cotangent, gathered.at[1, 0, y]),
            (up_weight, raw.at[0]), (down_weight, raw.at[1]),
        ))
    ]
    stores = [
        pltpu.make_async_copy(src, dst, local_sem.at[4 + i])
        for i, (src, dst) in enumerate((
            (widths.at[0], output), (widths.at[1], grad_tokens), (grads.at[0], grad_down), (grads.at[1], grad_up),
        ))
    ]
    for load in loads:
        load.start()
    barrier = pltpu.get_barrier_semaphore()
    partners = (sib, y_r, y_l, x_r, x_l, z_r, z_l) + across
    for device in partners:
        pl.semaphore_signal(barrier, inc=1, device_id=device, device_id_type=pl.DeviceIdType.MESH)
    pl.semaphore_wait(barrier, len(partners))

    steps = (
        own_x, own_y, gy, gf, gx, split_weights, prod, rs_hop, finish, ag_get,
        f_mm, f_sib, f_r1, f_r2, f_r3, f_r4, swap, swapped, grad, drain,
    )
    for step, *at in ORDER:
        steps[step](*at)
    drain(len(pending))
    for store in stores:
        store.wait()
    assert len(slots) <= SLOTS, len(slots)


def copy_kernel(*refs):
    sources, targets, held, sem = refs[:4], refs[4:8], refs[8:12], refs[12]
    loads, stores = [], []
    for src, dst, hold in zip(sources, targets, held):
        parts = 4 if src.shape[0] == UNITS else 1
        size = src.shape[0] // parts
        for part in range(parts):
            at, n = pl.ds(part * size, size), len(loads)
            loads.append(pltpu.make_async_copy(src.at[at], hold.at[at], sem.at[0, n]))
            stores.append(pltpu.make_async_copy(hold.at[at], dst.at[at], sem.at[1, n]))
    for load in loads:
        load.start()
    for load, store in zip(loads, stores):
        load.wait()
        store.start()
    for store in stores:
        store.wait()


def shards(tokens, up_weight, down_weight, cotangent):
    anywhere, piece = pl.BlockSpec(memory_space=pl.ANY), (CHUNK, UNITS)
    shapes = (
        jax.ShapeDtypeStruct((BLOCK, BLOCK), F32),
        jax.ShapeDtypeStruct((BLOCK, BLOCK), F32),
        jax.ShapeDtypeStruct((UNITS, WIDTH), F32),
        jax.ShapeDtypeStruct((UNITS, WIDTH), F32),
    )
    results = pl.pallas_call(
        kernel,
        out_shape=shapes,
        in_specs=[anywhere] * 4,
        out_specs=(anywhere,) * 4,
        scratch_shapes=[
            pltpu.VMEM((2, 2, 4, BLOCK, WIDTH), F32),
            pltpu.VMEM((2, UNITS, WIDTH), F32),
            pltpu.VMEM((2, 3 * UNITS, WIDTH), BF16),
            pltpu.VMEM((8, 16) + piece, F32),
            pltpu.VMEM((2, 4, 16) + piece, F32),
            pltpu.VMEM((8, 16) + piece, F32),
            pltpu.VMEM((2, 4) + piece, F32),
            pltpu.VMEM((4, 2, 2, 2, 2, 4) + piece, F32),
            pltpu.VMEM((4, 2, 2, 2, 4) + piece, F32),
            pltpu.VMEM((4, 2, 2, 2) + piece, F32),
            pltpu.VMEM((4, 2, 2, 4) + piece, F32),
            pltpu.VMEM((4, 2, 2, 2, 2) + piece, F32),
            pltpu.VMEM((4, 2) + piece, F32),
            pltpu.VMEM((4, 2, 2) + piece, F32),
            pltpu.VMEM((2, 4) + piece, F32),
            pltpu.VMEM((2, 4, CHUNK, BLOCK), F32),
            pltpu.VMEM((2, 4, CHUNK, BLOCK), F32),
            pltpu.VMEM((3, 2, CHUNK, BLOCK), F32),
            pltpu.VMEM((3, 2, CHUNK, BLOCK), F32),
            pltpu.VMEM((2, BLOCK, BLOCK), F32),
            pltpu.VMEM((2, UNITS, WIDTH), F32),
            pltpu.SemaphoreType.DMA((SLOTS,)),
            pltpu.SemaphoreType.DMA((SLOTS,)),
            pltpu.SemaphoreType.DMA((8,)),
        ],
        compiler_params=pltpu.CompilerParams(
            collective_id=0, has_side_effects=True, vmem_limit_bytes=62 * 1024 * 1024),
        cost_estimate=pl.CostEstimate(flops=16_300_000_000, bytes_accessed=6_000_000, transcendentals=73728),
    )(tokens, up_weight, down_weight, cotangent)
    return pl.pallas_call(
        copy_kernel,
        out_shape=shapes,
        in_specs=[anywhere] * 4,
        out_specs=(anywhere,) * 4,
        scratch_shapes=[pltpu.VMEM(shape.shape, F32) for shape in shapes] + [pltpu.SemaphoreType.DMA((2, 10))],
    )(*results)


def solution(mesh):
    return jax.shard_map(
        shards,
        mesh=mesh,
        in_specs=(
            P("row", "col"),
            P(("row", "depth"), "col"),
            P(("row", "depth"), "col"),
            P("row", "col"),
        ),
        out_specs=(
            P("row", ("col", "depth")),
            P("row", ("col", "depth")),
            P(("row", "depth"), "col"),
            P(("row", "depth"), "col"),
        ),
        check_vma=False,
    )
```

```python
import jax
import jax.numpy as jnp
from jax import lax
from jax.experimental import pallas as pl
from jax.experimental.pallas import tpu as pltpu
from jax.sharding import PartitionSpec as P

F32, BF16 = jnp.float32, jnp.bfloat16
root_two_pi = 0.7978845608028654
cubic_coef = 0.044715

SLOTS = 260
BLOCK, WIDTH, UNITS, CHUNK = 192, 768, 384, 24
GROUPS = (
    ((0, 0, 0), (1, 0, 0)),
    ((0, 1, 0), (1, 1, 0)),
    ((0, 0, 1), (0, 0, 3)),
    ((0, 1, 1), (0, 1, 3)),
    ((0, 0, 2), (0, 1, 2)),
    ((1, 0, 1), (1, 0, 3)),
    ((1, 1, 1), (1, 1, 3)),
    ((1, 0, 2), (1, 1, 2)),
)
FIRST_WAY = (0, 1, 0, 1, 0, 1, 0, 1)
PLACE = {block: at for at, block in enumerate(block for group in GROUPS for block in group)}
SPAN = tuple(slice(PLACE[group[0]], PLACE[group[0]] + len(group)) for group in GROUPS)
BLOCKS = tuple((g, dy) for g in range(2) for dy in range(4))
Y_FIRST = ((0, 1, 0, 1), (0, 1, 1, 0))
(
    OWN_X, OWN_Y, GY, GF, GX, SPLIT_WEIGHTS, PROD, RS_HOP, FINISH, AG_GET, F_MM, F_SIB, F_R1, F_R2, F_R3, F_R4,
    SWAP, SWAPPED, GRAD, DRAIN,
) = range(20)
ORDER = (
    (OWN_Y, 0), (OWN_X, 0), (OWN_X, 1), (SPLIT_WEIGHTS, 1), (SPLIT_WEIGHTS, 0), (PROD, 0), (GY, 0, 0, 0),
    (GX, 0, 0, 0), (GX, 0, 0, 1), (GY, 0, 1, 1), (RS_HOP, 0, 0, 2), (RS_HOP, 0, 1, 3), (GY, 0, 0, 1), (GY, 0, 1, 0),
    (GX, 1, 0, 1), (GX, 1, 0, 0), (OWN_Y, 1), (RS_HOP, 0, 0, 3), (RS_HOP, 0, 1, 4), (PROD, 2), (GF, 0, 0), (GF, 0, 1),
    (RS_HOP, 0, 0, 4), (PROD, 1), (GX, 0, 1, 0), (RS_HOP, 2, 0, 2), (RS_HOP, 2, 1, 3), (GY, 1, 0, 0), (GX, 0, 3, 0),
    (GX, 0, 1, 1), (GX, 0, 3, 1), (FINISH, 0), (GY, 1, 0, 1), (GX, 0, 2, 1), (GY, 1, 1, 0), (RS_HOP, 1, 1, 2),
    (RS_HOP, 1, 0, 3), (GX, 0, 2, 0), (GY, 1, 1, 1), (DRAIN, 16), (RS_HOP, 2, 1, 4), (RS_HOP, 2, 0, 3), (PROD, 3),
    (GF, 1, 0), (GX, 1, 3, 0), (AG_GET, 0, 1, 1), (RS_HOP, 1, 1, 3), (DRAIN, 16), (RS_HOP, 1, 0, 4), (GX, 1, 3, 1),
    (PROD, 4), (DRAIN, 16), (GX, 1, 1, 0), (DRAIN, 16), (RS_HOP, 2, 0, 4), (RS_HOP, 3, 0, 3), (RS_HOP, 3, 1, 2),
    (RS_HOP, 1, 1, 4), (RS_HOP, 4, 0, 2), (GX, 1, 2, 0), (GF, 1, 1), (RS_HOP, 4, 1, 3), (FINISH, 2), (GX, 1, 1, 1),
    (RS_HOP, 3, 0, 4), (RS_HOP, 3, 1, 3), (RS_HOP, 4, 0, 3), (FINISH, 1), (AG_GET, 2, 0, 1), (RS_HOP, 4, 1, 4),
    (AG_GET, 2, 1, 1), (RS_HOP, 3, 1, 4), (RS_HOP, 4, 0, 4), (AG_GET, 1, 0, 1), (PROD, 6), (AG_GET, 1, 1, 1),
    (GX, 1, 2, 1), (AG_GET, 2, 0, 2), (FINISH, 4), (FINISH, 3), (PROD, 5), (RS_HOP, 6, 0, 2), (AG_GET, 0, 0, 1),
    (AG_GET, 2, 0, 3), (PROD, 7), (AG_GET, 4, 0, 1), (AG_GET, 1, 1, 2), (AG_GET, 2, 1, 2), (AG_GET, 3, 1, 1),
    (AG_GET, 4, 1, 1), (AG_GET, 3, 0, 1), (F_MM, 0, 1, 0, 1), (RS_HOP, 5, 1, 2), (RS_HOP, 5, 0, 3), (AG_GET, 1, 0, 2),
    (RS_HOP, 6, 1, 3), (F_SIB, 0, 1), (GRAD, 0, 1), (AG_GET, 0, 0, 2), (RS_HOP, 6, 0, 3), (F_MM, 0, 4, 0),
    (AG_GET, 3, 1, 2), (AG_GET, 4, 1, 2), (AG_GET, 1, 1, 3), (AG_GET, 4, 0, 2), (F_R1, 0, 1), (RS_HOP, 7, 1, 2),
    (AG_GET, 3, 0, 2), (RS_HOP, 7, 0, 3), (AG_GET, 0, 1, 2), (F_MM, 0, 2, 0, 1), (RS_HOP, 5, 1, 3), (AG_GET, 1, 0, 3),
    (RS_HOP, 6, 1, 4), (F_R2, 0, 1), (F_SIB, 0, 2), (AG_GET, 0, 0, 3), (GRAD, 0, 2), (AG_GET, 4, 0, 3), (DRAIN, 16),
    (RS_HOP, 7, 1, 3), (AG_GET, 2, 1, 3), (RS_HOP, 5, 0, 4), (RS_HOP, 6, 0, 4), (F_R1, 0, 2), (RS_HOP, 5, 1, 4),
    (AG_GET, 4, 1, 3), (AG_GET, 3, 0, 3), (AG_GET, 2, 0, 4), (F_R3, 0, 1), (AG_GET, 0, 1, 3), (AG_GET, 3, 1, 3),
    (F_MM, 0, 3, 0, 1), (RS_HOP, 7, 0, 4), (GRAD, 0, 3), (RS_HOP, 7, 1, 4), (AG_GET, 4, 0, 4), (AG_GET, 0, 0, 4),
    (F_SIB, 0, 3), (AG_GET, 1, 1, 4), (F_R2, 0, 2), (FINISH, 5), (FINISH, 6), (AG_GET, 3, 1, 4), (F_MM, 0, 4, 1),
    (FINISH, 7), (F_R4, 0, 1), (F_MM, 1, 4, 0), (AG_GET, 5, 0, 1), (F_R1, 0, 3), (AG_GET, 5, 1, 1), (F_SIB, 0, 4),
    (AG_GET, 6, 0, 1), (AG_GET, 6, 1, 1), (GRAD, 0, 4), (AG_GET, 7, 1, 1), (AG_GET, 7, 0, 1), (AG_GET, 5, 0, 2),
    (AG_GET, 5, 1, 2), (F_MM, 1, 1, 0, 1), (AG_GET, 6, 1, 2), (F_R3, 0, 2), (F_R2, 0, 3), (AG_GET, 6, 0, 2),
    (F_R1, 0, 4), (AG_GET, 7, 1, 2), (AG_GET, 7, 0, 2), (F_MM, 1, 2, 0, 1), (AG_GET, 5, 1, 3), (GRAD, 1, 1),
    (AG_GET, 6, 0, 3), (AG_GET, 7, 1, 3), (AG_GET, 5, 0, 3), (F_R4, 0, 2), (F_SIB, 1, 1), (AG_GET, 6, 1, 3),
    (F_R3, 0, 3), (F_SIB, 1, 2), (AG_GET, 7, 0, 3), (F_MM, 1, 3, 0, 1), (F_R2, 0, 4), (AG_GET, 5, 1, 4),
    (AG_GET, 7, 1, 4), (AG_GET, 6, 0, 4), (F_MM, 1, 4, 1), (F_R1, 1, 1), (F_SIB, 1, 3), (F_R1, 1, 2), (F_SIB, 1, 4),
    (GRAD, 1, 2), (F_R2, 1, 1), (F_R3, 0, 4), (F_R4, 0, 3), (DRAIN, 16), (F_R1, 1, 3), (F_R1, 1, 4), (DRAIN, 16),
    (GRAD, 1, 3), (F_R3, 1, 1), (F_R2, 1, 2), (F_R4, 0, 4), (F_R2, 1, 3), (SWAP, 0), (F_R2, 1, 4), (F_R3, 1, 2),
    (DRAIN, 16), (F_R3, 1, 3), (F_R4, 1, 1), (F_R3, 1, 4), (GRAD, 1, 4), (F_R4, 1, 2), (F_R4, 1, 3), (F_R4, 1, 4),
    (SWAP, 1), (DRAIN, 16), (SWAPPED, 0), (SWAPPED, 1),
)


def gelu_parts(hidden):
    inner_arg = root_two_pi * (hidden + cubic_coef * hidden * hidden * hidden)
    bent_value = jnp.tanh(inner_arg)
    result = 0.5 * hidden * (1.0 + bent_value)
    slopes = 0.5 * (1.0 + bent_value) + 0.5 * hidden * (
        1.0 - bent_value * bent_value
    ) * root_two_pi * (1.0 + 3.0 * cubic_coef * hidden * hidden)
    return (result, slopes)


def halves(value):
    high = value.astype(BF16)
    return high, (value - high.astype(F32)).astype(BF16)


def kernel(
    tokens, up_weight, down_weight, cotangent,
    output, grad_tokens, grad_up, grad_down,
    gathered, raw, weights, partial, summed, spread, slope, fold, from_sib,
    near, far_x, far_y, last, ends, result, give, take, widths, grads,
    send_sem, recv_sem, local_sem,
):
    row, z, depth = lax.axis_index("row"), lax.axis_index("col"), lax.axis_index("depth")
    y, xl, xh, q = row // 2, row % 2, depth // 2, depth % 2
    xh_r, xh_l, xh_s = (xh + xl) % 2, (xh + xl + 1) % 2, (xh + xl + q) % 2
    sib = (row, z, xh * 2 + 1 - q)
    y_r, y_l = (((y + 1) % 4) * 2 + xl, z, depth), (((y + 3) % 4) * 2 + xl, z, depth)
    x_r, x_l = (y * 2 + 1 - xl, z, xh_r * 2 + q), (y * 2 + 1 - xl, z, xh_l * 2 + q)
    z_r, z_l = (row, (z + 1) % 8, depth), (row, (z + 7) % 8, depth)
    y_s = (((y + 1 + 2 * q) % 4) * 2 + xl, z, depth)
    x_s = (y * 2 + 1 - xl, z, xh_s * 2 + q)
    z_dev, z_sgn = (z_r, z_l), (1, 7)

    slots, pending = {}, []

    def remote(name, src, dst, device):
        at = slots.setdefault(name, len(slots))
        return pltpu.make_async_remote_copy(
            src_ref=src, dst_ref=dst, send_sem=send_sem.at[at], recv_sem=recv_sem.at[at],
            device_id=device, device_id_type=pl.DeviceIdType.MESH,
        )

    def send(name, src, dst, device):
        copy = remote(name, src, dst, device)
        copy.start()
        pending.append(copy)

    def arrive(name, dst):
        remote(name, dst, dst, sib).wait_recv()

    def rows(core, half):
        return pl.ds(pl.multiple_of(core * 96 + half * 48, 8), 48)

    def own_piece(a, g, dy, half):
        return gathered.at[a, g, (y + dy) % 4, rows(q, half)]

    def across_x(a, dy, half):
        piece = rows(q, half)
        src, dst = (gathered.at[a, g, (y + dy) % 4, piece] for g in range(2))
        send(("x", a, dy, half), src, dst, (x_r, x_l)[half])

    def to_core(a, g, dy, half):
        piece = own_piece(a, g, dy, half)
        send(("s", a, g, dy, half), piece, piece, sib)

    def own_x(a):
        if a == 1:
            loads[a].wait()
        for half in range(2):
            across_x(a, 0, half)

    def own_y(a):
        if a == 0:
            loads[a].wait()
        for halves_of in ((0, 1), (1, 0)):
            for way in range(2):
                piece = own_piece(a, 0, 0, halves_of[way])
                send(("y", a, way, halves_of[way]), piece, piece, (y_r, y_l)[way])

    def gy(a, way, half):
        dy = 3 if way == 0 else 1
        piece = own_piece(a, 0, dy, half)
        arrive(("y", a, way, half), piece)
        if half == way:
            send(("yf", a, way), piece, piece, (y_r, y_l)[way])
        across_x(a, dy, half)
        to_core(a, 0, dy, half)

    def gf(a, way):
        arrive(("yf", a, way), own_piece(a, 0, 2, way))
        across_x(a, 2, way)
        to_core(a, 0, 2, way)

    def gx(a, dy, half):
        arrive(("x", a, dy, half), own_piece(a, 1, dy, half))
        to_core(a, 1, dy, half)

    def split_weights(a):
        loads[2 + a].wait()
        high, low = halves(raw[a])
        weights[a, 0:UNITS] = high
        weights[a, UNITS:2 * UNITS] = high
        weights[a, 2 * UNITS:3 * UNITS] = low

    def prod(u):
        def nt(left, right):
            return lax.dot_general(left, right, (((1,), (1,)), ((), ())), preferred_element_type=F32)

        def product(a, blocks):
            high, low = halves(jnp.concatenate([gathered[a, g, (y + dy) % 4] for g, dy in blocks], axis=0))
            w_high, w_low = weights[a, 0:UNITS], weights[a, 2 * UNITS:3 * UNITS]
            return nt(high, w_high) + (nt(low, w_high) + nt(high, w_low))

        for a, g, dy in GROUPS[u]:
            if (g, dy) != (0, 0):
                for half in range(2):
                    arrive(("s", a, g, dy, half), gathered.at[a, g, (y + dy) % 4, rows(1 - q, half)])
        for a in range(2):
            blocks = [block for block in GROUPS[u] if block[0] == a]
            if blocks:
                total = product(a, [block[1:] for block in blocks])
                for n, block in enumerate(blocks):
                    partial[:, PLACE[block]] = total[n * BLOCK:(n + 1) * BLOCK].reshape(8, CHUNK, UNITS)
        rs_send(u, FIRST_WAY[u], 1)
        rs_send(u, 1 - FIRST_WAY[u], 2)

    def z_chunk(way, distance):
        return (z + z_sgn[way] * distance) % 8

    def rs_send(u, way, step):
        src, dst = partial.at[z_chunk(way, 5 - step), SPAN[u]], summed.at[way, step - 1, SPAN[u]]
        send(("rs", u, way, step), src, dst, z_dev[way])

    def rs_hop(u, way, step):
        arrive(("rs", u, way, step - 1), summed.at[way, step - 2, SPAN[u]])
        c = z_chunk(way, 5 - step)
        partial[c, SPAN[u]] = partial[c, SPAN[u]] + summed[way, step - 2, SPAN[u]]
        rs_send(u, way, step)

    def ag_send(u, way, k):
        piece = spread.at[z_chunk(1 - way, k - 1), SPAN[u]]
        send(("ag", u, way, k), piece, piece, z_dev[way])

    def ag_get(u, way, k):
        arrive(("ag", u, way, k), spread.at[z_chunk(1 - way, k), SPAN[u]])
        if k < 3 or (k == 3 and way == FIRST_WAY[u]):
            ag_send(u, way, k + 1)

    def finish(u):
        for way in range(2):
            arrive(("rs", u, way, 4), summed.at[way, 3, SPAN[u]])
        for a, g, dy in GROUPS[u]:
            at = PLACE[(a, g, dy)]
            total = partial[z, at] + summed[0, 3, at] + summed[1, 3, at]
            if a == 0:
                spread[z, at], slope[g, dy] = gelu_parts(total)
            else:
                spread[z, at] = total * slope[g, dy]
        for way in range(2):
            ag_send(u, way, 1)

    def spread_rows(a, chunks):
        return jnp.concatenate([spread[c, PLACE[(a, g, dy)]] for c in chunks for g, dy in BLOCKS], axis=0)

    def round_chunk(r, core):
        if r == 4:
            return (z + 4 * core) % 8
        return (z + r + (8 - 2 * r) * core) % 8

    def f_mm(a, r, *cores):
        high, low = halves(spread_rows(a, [round_chunk(r, core) for core in cores]))
        total = jnp.dot(jnp.concatenate([high, low, high], axis=1), weights[1 - a], preferred_element_type=F32)
        for i, core in enumerate(cores):
            for n, (g, dy) in enumerate(BLOCKS):
                at = i * BLOCK + n * CHUNK
                for side in range(2):
                    fold[r - 1, a, core, side, g, (y + dy) % 4] = total[at:at + CHUNK, side * UNITS:(side + 1) * UNITS]
        if 1 in cores:
            send(("fs", a, r), fold.at[r - 1, a, 1 - q], from_sib.at[r - 1, a], sib)

    def f_sib(a, r):
        i = r - 1
        arrive(("fs", a, r), from_sib.at[i, a])
        fold[i, a, q] = fold[i, a, q] + from_sib[i, a]
        if Y_FIRST[a][i]:
            send(("f1", a, r, 0), fold.at[i, a, q, 0, :, (y + 2) % 4], near.at[i, a, 0], y_r)
            send(("f1", a, r, 1), fold.at[i, a, q, 1, :, (y + 2) % 4], near.at[i, a, 1], y_l)
        else:
            send(("f1", a, r, 0), fold.at[i, a, q, 1 - xh, 0, 0:2], near.at[i, a, 0], x_r)
            send(("f1", a, r, 1), fold.at[i, a, q, 1 - xh, 0, 2:4], near.at[i, a, 1], x_l)

    def f_r1(a, r):
        i = r - 1
        for way, yy, xx in ((0, (y + 1) % 4, xh_r), (1, (y + 3) % 4, xh_l)):
            arrive(("f1", a, r, way), near.at[i, a, way])
            if Y_FIRST[a][i]:
                fold[i, a, q, way, :, yy] = fold[i, a, q, way, :, yy] + near[i, a, way]
                send(("f2", a, r, way), fold.at[i, a, q, :, :, yy], far_y.at[i, a, way], (y_r, y_l)[way])
            else:
                half = slice(2 * way, 2 * way + 2)
                fold[i, a, q, xx, 1, half] = fold[i, a, q, xx, 1, half] + near[i, a, way]
                send(("f2", a, r, way), fold.at[i, a, q, xx, 1], far_x.at[i, a, way], (x_r, x_l)[way])

    def f_r2(a, r):
        i = r - 1
        far = (far_x, far_y)[Y_FIRST[a][i]]
        for way in range(2):
            arrive(("f2", a, r, way), far.at[i, a, way])
        if Y_FIRST[a][i]:
            fold[i, a, q, :, :, y] = fold[i, a, q, :, :, y] + far[i, a, 0] + far[i, a, 1]
            send(("f3", a, r), fold.at[i, a, q, 1 - xh, 0, y], last.at[i, a], x_s)
        else:
            fold[i, a, q, xh, 0] = fold[i, a, q, xh, 0] + far[i, a, 0] + far[i, a, 1]
            send(("f3", a, r), fold.at[i, a, q, xh, 0, (y + 2) % 4], last.at[i, a], y_s)

    def f_r3(a, r):
        i = r - 1
        arrive(("f3", a, r), last.at[i, a])
        if Y_FIRST[a][i]:
            fold[i, a, q, xh_s, 1, y] = fold[i, a, q, xh_s, 1, y] + last[i, a]
            send(("f4", a, r, 0), fold.at[i, a, q, xh_r, 1, y], ends.at[i, a, 0], x_r)
            send(("f4", a, r, 1), fold.at[i, a, q, xh_l, 1, y], ends.at[i, a, 1], x_l)
        else:
            ys = (y + 1 + 2 * q) % 4
            fold[i, a, q, xh, 0, ys] = fold[i, a, q, xh, 0, ys] + last[i, a]
            send(("f4", a, r, 0), fold.at[i, a, q, xh, 0, (y + 1) % 4], ends.at[i, a, 0], y_r)
            send(("f4", a, r, 1), fold.at[i, a, q, xh, 0, (y + 3) % 4], ends.at[i, a, 1], y_l)

    def f_r4(a, r):
        i = r - 1
        arrive(("f4", a, r, 0), ends.at[i, a, 0])
        arrive(("f4", a, r, 1), ends.at[i, a, 1])
        result[a, i] = fold[i, a, q, xh, 0, y] + ends[i, a, 0] + ends[i, a, 1]

    def swap(a):
        first, second = result[a, :, :, 0:BLOCK], result[a, :, :, BLOCK:2 * BLOCK]
        lower = jnp.full(first.shape, q, jnp.int32) == 0
        give[a] = jnp.where(lower, second, first)
        send(("swap", a), give.at[a], take.at[a], sib)
        mine = jnp.where(lower, first, second)
        for r in range(1, 5):
            at = pl.ds(pl.multiple_of(round_chunk(r, q) * CHUNK, 8), CHUNK)
            widths[a, at, :] = mine[r - 1]

    def swapped(a):
        arrive(("swap", a), take.at[a])
        for r in range(1, 5):
            at = pl.ds(pl.multiple_of(round_chunk(r, 1 - q) * CHUNK, 8), CHUNK)
            widths[a, at, :] = take[a, r - 1]
        stores[a].start()

    rounds_done = [0, 0]

    def grad(a, r):
        chunks = (round_chunk(r, 0), round_chunk(r, 1))
        left = spread_rows(a, chunks).T
        right = jnp.concatenate([
            gathered[1 - a, g, (y + dy) % 4, pl.ds(pl.multiple_of(c * CHUNK, 8), CHUNK), :]
            for c in chunks for g, dy in BLOCKS
        ], axis=0)
        l_high, l_low = halves(left)
        r_high, r_low = halves(right)
        term = jnp.dot(
            jnp.concatenate([l_high, l_low, l_high], axis=1), jnp.concatenate([r_high, r_high, r_low], axis=0),
            preferred_element_type=F32)
        grads[a] = term if rounds_done[a] == 0 else grads[a] + term
        rounds_done[a] += 1
        if rounds_done[a] == 4:
            stores[2 + a].start()

    def drain(count):
        for copy in pending[:count]:
            copy.wait_send()
        del pending[:count]

    loads = [
        pltpu.make_async_copy(src, dst, local_sem.at[i])
        for i, (src, dst) in enumerate((
            (tokens, gathered.at[0, 0, y]), (cotangent, gathered.at[1, 0, y]),
            (up_weight, raw.at[0]), (down_weight, raw.at[1]),
        ))
    ]
    stores = [
        pltpu.make_async_copy(src, dst, local_sem.at[4 + i])
        for i, (src, dst) in enumerate((
            (widths.at[0], output), (widths.at[1], grad_tokens), (grads.at[0], grad_down), (grads.at[1], grad_up),
        ))
    ]
    for load in loads:
        load.start()
    barrier = pltpu.get_barrier_semaphore()
    partners = (sib, y_r, y_l, x_r, x_l, z_r, z_l)
    for device in partners:
        pl.semaphore_signal(barrier, inc=1, device_id=device, device_id_type=pl.DeviceIdType.MESH)
    pl.semaphore_wait(barrier, len(partners))

    steps = (
        own_x, own_y, gy, gf, gx, split_weights, prod, rs_hop, finish, ag_get,
        f_mm, f_sib, f_r1, f_r2, f_r3, f_r4, swap, swapped, grad, drain,
    )
    for step, *at in ORDER:
        steps[step](*at)
    drain(len(pending))
    for store in stores:
        store.wait()
    assert len(slots) <= SLOTS, len(slots)


def copy_kernel(*refs):
    sources, targets, held, sem = refs[:4], refs[4:8], refs[8:12], refs[12]
    loads, stores = [], []
    for src, dst, hold in zip(sources, targets, held):
        parts = 4 if src.shape[0] == UNITS else 1
        size = src.shape[0] // parts
        for part in range(parts):
            at, n = pl.ds(part * size, size), len(loads)
            loads.append(pltpu.make_async_copy(src.at[at], hold.at[at], sem.at[0, n]))
            stores.append(pltpu.make_async_copy(hold.at[at], dst.at[at], sem.at[1, n]))
    for load in loads:
        load.start()
    for load, store in zip(loads, stores):
        load.wait()
        store.start()
    for store in stores:
        store.wait()


def shards(tokens, up_weight, down_weight, cotangent):
    anywhere, piece = pl.BlockSpec(memory_space=pl.ANY), (CHUNK, UNITS)
    shapes = (
        jax.ShapeDtypeStruct((BLOCK, BLOCK), F32),
        jax.ShapeDtypeStruct((BLOCK, BLOCK), F32),
        jax.ShapeDtypeStruct((UNITS, WIDTH), F32),
        jax.ShapeDtypeStruct((UNITS, WIDTH), F32),
    )
    results = pl.pallas_call(
        kernel,
        out_shape=shapes,
        in_specs=[anywhere] * 4,
        out_specs=(anywhere,) * 4,
        scratch_shapes=[
            pltpu.VMEM((2, 2, 4, BLOCK, WIDTH), F32),
            pltpu.VMEM((2, UNITS, WIDTH), F32),
            pltpu.VMEM((2, 3 * UNITS, WIDTH), BF16),
            pltpu.VMEM((8, 16) + piece, F32),
            pltpu.VMEM((2, 4, 16) + piece, F32),
            pltpu.VMEM((8, 16) + piece, F32),
            pltpu.VMEM((2, 4) + piece, F32),
            pltpu.VMEM((4, 2, 2, 2, 2, 4) + piece, F32),
            pltpu.VMEM((4, 2, 2, 2, 4) + piece, F32),
            pltpu.VMEM((4, 2, 2, 2) + piece, F32),
            pltpu.VMEM((4, 2, 2, 4) + piece, F32),
            pltpu.VMEM((4, 2, 2, 2, 2) + piece, F32),
            pltpu.VMEM((4, 2) + piece, F32),
            pltpu.VMEM((4, 2, 2) + piece, F32),
            pltpu.VMEM((2, 4) + piece, F32),
            pltpu.VMEM((2, 4, CHUNK, BLOCK), F32),
            pltpu.VMEM((2, 4, CHUNK, BLOCK), F32),
            pltpu.VMEM((2, BLOCK, BLOCK), F32),
            pltpu.VMEM((2, UNITS, WIDTH), F32),
            pltpu.SemaphoreType.DMA((SLOTS,)),
            pltpu.SemaphoreType.DMA((SLOTS,)),
            pltpu.SemaphoreType.DMA((8,)),
        ],
        compiler_params=pltpu.CompilerParams(
            collective_id=0, has_side_effects=True, vmem_limit_bytes=62 * 1024 * 1024),
        cost_estimate=pl.CostEstimate(flops=16_300_000_000, bytes_accessed=6_000_000, transcendentals=73728),
    )(tokens, up_weight, down_weight, cotangent)
    return pl.pallas_call(
        copy_kernel,
        out_shape=shapes,
        in_specs=[anywhere] * 4,
        out_specs=(anywhere,) * 4,
        scratch_shapes=[pltpu.VMEM(shape.shape, F32) for shape in shapes] + [pltpu.SemaphoreType.DMA((2, 10))],
    )(*results)


def solution(mesh):
    return jax.shard_map(
        shards,
        mesh=mesh,
        in_specs=(
            P("row", "col"),
            P(("row", "depth"), "col"),
            P(("row", "depth"), "col"),
            P("row", "col"),
        ),
        out_specs=(
            P("row", ("col", "depth")),
            P("row", ("col", "depth")),
            P(("row", "depth"), "col"),
            P(("row", "depth"), "col"),
        ),
        check_vma=False,
    )
```

```python
import jax
import jax.numpy as jnp
from jax import lax
from jax.experimental import pallas as pl
from jax.experimental.pallas import tpu as pltpu
from jax.sharding import PartitionSpec as P

F32, BF16 = jnp.float32, jnp.bfloat16
root_two_pi = 0.7978845608028654
cubic_coef = 0.044715

SLOTS = 260
BLOCK, WIDTH, UNITS, CHUNK = 192, 768, 384, 24
GROUPS = (
    ((0, 0, 0), (1, 0, 0)),
    ((0, 1, 0), (1, 1, 0)),
    ((0, 0, 1), (0, 0, 3)),
    ((0, 1, 1), (0, 1, 3)),
    ((0, 0, 2), (0, 1, 2)),
    ((1, 0, 1), (1, 0, 3)),
    ((1, 1, 1), (1, 1, 3)),
    ((1, 0, 2), (1, 1, 2)),
)
FIRST_WAY = (0, 1, 0, 1, 0, 1, 0, 1)
PLACE = {block: at for at, block in enumerate(block for group in GROUPS for block in group)}
SPAN = tuple(slice(PLACE[group[0]], PLACE[group[0]] + len(group)) for group in GROUPS)
BLOCKS = tuple((g, dy) for g in range(2) for dy in range(4))
Y_FIRST = ((0, 1, 0, 1), (0, 1, 1, 0))
(
    OWN_X, OWN_Y, GY, GF, GX, SPLIT_WEIGHTS, PROD, RS_HOP, FINISH, AG_GET, F_MM, F_SIB, F_R1, F_R2, F_R3, F_R4,
    SWAP, SWAPPED, GRAD, DRAIN,
) = range(20)
ORDER = (
    (OWN_Y, 0), (OWN_X, 0), (OWN_X, 1), (SPLIT_WEIGHTS, 1), (SPLIT_WEIGHTS, 0), (PROD, 0), (GY, 0, 0, 0),
    (GX, 0, 0, 0), (GX, 0, 0, 1), (GY, 0, 1, 1), (RS_HOP, 0, 0, 2), (RS_HOP, 0, 1, 3), (GY, 0, 0, 1), (GY, 0, 1, 0),
    (GX, 1, 0, 1), (GX, 1, 0, 0), (OWN_Y, 1), (RS_HOP, 0, 0, 3), (RS_HOP, 0, 1, 4), (PROD, 2), (GF, 0, 0), (GF, 0, 1),
    (RS_HOP, 0, 0, 4), (PROD, 1), (GX, 0, 1, 0), (RS_HOP, 2, 0, 2), (RS_HOP, 2, 1, 3), (GY, 1, 0, 0), (GX, 0, 3, 0),
    (GX, 0, 1, 1), (GX, 0, 3, 1), (FINISH, 0), (GY, 1, 0, 1), (GX, 0, 2, 1), (GY, 1, 1, 0), (RS_HOP, 1, 1, 2),
    (RS_HOP, 1, 0, 3), (DRAIN, 16), (GX, 0, 2, 0), (GY, 1, 1, 1), (DRAIN, 16), (RS_HOP, 2, 1, 4), (RS_HOP, 2, 0, 3),
    (PROD, 3), (GF, 1, 0), (GX, 1, 3, 0), (AG_GET, 0, 1, 1), (RS_HOP, 1, 1, 3), (DRAIN, 16), (RS_HOP, 1, 0, 4),
    (GX, 1, 3, 1), (PROD, 4), (DRAIN, 16), (DRAIN, 16), (RS_HOP, 2, 0, 4), (RS_HOP, 3, 0, 3), (GX, 1, 1, 0),
    (GX, 1, 2, 0), (RS_HOP, 3, 1, 2), (GF, 1, 1), (RS_HOP, 1, 1, 4), (RS_HOP, 4, 0, 2), (FINISH, 2),
    (RS_HOP, 3, 0, 4), (RS_HOP, 4, 1, 3), (RS_HOP, 4, 0, 3), (RS_HOP, 3, 1, 3), (GX, 1, 1, 1), (FINISH, 1),
    (RS_HOP, 4, 1, 4), (AG_GET, 2, 0, 1), (AG_GET, 2, 1, 1), (RS_HOP, 4, 0, 4), (RS_HOP, 3, 1, 4), (AG_GET, 1, 0, 1),
    (AG_GET, 0, 1, 2), (PROD, 6), (AG_GET, 2, 0, 2), (GX, 1, 2, 1), (FINISH, 4), (FINISH, 3), (PROD, 7),
    (AG_GET, 1, 1, 1), (PROD, 5), (RS_HOP, 6, 0, 2), (AG_GET, 4, 0, 1), (AG_GET, 3, 1, 1), (AG_GET, 4, 1, 1),
    (AG_GET, 0, 0, 1), (AG_GET, 3, 0, 1), (F_MM, 0, 1, 0, 1), (RS_HOP, 5, 1, 2), (AG_GET, 1, 0, 2), (RS_HOP, 6, 0, 3),
    (AG_GET, 1, 1, 2), (AG_GET, 4, 0, 2), (RS_HOP, 5, 0, 3), (RS_HOP, 6, 1, 3), (AG_GET, 2, 0, 3), (RS_HOP, 7, 1, 2),
    (F_SIB, 0, 1), (GRAD, 0, 1), (AG_GET, 0, 0, 2), (F_MM, 0, 4, 0), (AG_GET, 4, 1, 2), (AG_GET, 2, 1, 2),
    (AG_GET, 3, 1, 2), (AG_GET, 3, 0, 2), (F_MM, 0, 2, 0, 1), (AG_GET, 1, 1, 3), (F_R1, 0, 1), (AG_GET, 1, 0, 3),
    (RS_HOP, 5, 1, 3), (RS_HOP, 5, 0, 4), (F_SIB, 0, 2), (RS_HOP, 7, 1, 3), (AG_GET, 4, 1, 3), (GRAD, 0, 2),
    (RS_HOP, 6, 1, 4), (AG_GET, 0, 1, 3), (RS_HOP, 7, 0, 3), (AG_GET, 0, 0, 3), (AG_GET, 2, 1, 3), (RS_HOP, 6, 0, 4),
    (AG_GET, 3, 0, 3), (F_R1, 0, 2), (RS_HOP, 5, 1, 4), (AG_GET, 4, 0, 3), (AG_GET, 3, 1, 3), (F_R2, 0, 1),
    (F_MM, 0, 3, 0, 1), (RS_HOP, 7, 1, 4), (RS_HOP, 7, 0, 4), (GRAD, 0, 3), (AG_GET, 1, 1, 4), (AG_GET, 2, 0, 4),
    (AG_GET, 0, 0, 4), (FINISH, 5), (F_SIB, 0, 3), (FINISH, 6), (AG_GET, 3, 1, 4), (F_R2, 0, 2), (AG_GET, 4, 0, 4),
    (F_MM, 0, 4, 1), (F_R3, 0, 1), (FINISH, 7), (F_MM, 1, 4, 0), (AG_GET, 5, 0, 1), (AG_GET, 5, 1, 1), (F_R1, 0, 3),
    (F_SIB, 0, 4), (AG_GET, 6, 0, 1), (AG_GET, 6, 1, 1), (AG_GET, 7, 1, 1), (AG_GET, 7, 0, 1), (GRAD, 0, 4),
    (AG_GET, 5, 1, 2), (AG_GET, 5, 0, 2), (F_MM, 1, 1, 0, 1), (AG_GET, 6, 1, 2), (AG_GET, 6, 0, 2), (F_R2, 0, 3),
    (F_R1, 0, 4), (AG_GET, 7, 1, 2), (F_R3, 0, 2), (AG_GET, 7, 0, 2), (F_MM, 1, 2, 0, 1), (AG_GET, 5, 1, 3),
    (GRAD, 1, 1), (AG_GET, 6, 0, 3), (F_SIB, 1, 1), (F_R4, 0, 1), (F_R3, 0, 3), (AG_GET, 7, 1, 3), (AG_GET, 6, 1, 3),
    (AG_GET, 5, 0, 3), (AG_GET, 7, 0, 3), (F_MM, 1, 3, 0, 1), (F_R2, 0, 4), (F_SIB, 1, 2), (AG_GET, 5, 1, 4),
    (AG_GET, 6, 0, 4), (AG_GET, 7, 1, 4), (F_MM, 1, 4, 1), (F_R1, 1, 1), (F_SIB, 1, 3), (DRAIN, 16), (F_R1, 1, 2),
    (F_SIB, 1, 4), (GRAD, 1, 2), (F_R3, 0, 4), (F_R2, 1, 1), (F_R1, 1, 3), (F_R4, 0, 3), (F_R4, 0, 2), (F_R1, 1, 4),
    (GRAD, 1, 3), (F_R3, 1, 1), (F_R2, 1, 2), (F_R4, 0, 4), (DRAIN, 16), (DRAIN, 16), (SWAP, 0), (F_R2, 1, 3),
    (F_R2, 1, 4), (F_R3, 1, 2), (F_R4, 1, 1), (F_R3, 1, 3), (F_R3, 1, 4), (GRAD, 1, 4), (F_R4, 1, 2), (F_R4, 1, 3),
    (F_R4, 1, 4), (SWAP, 1), (DRAIN, 16), (SWAPPED, 0), (SWAPPED, 1),
)


def gelu_parts(hidden):
    inner_arg = root_two_pi * (hidden + cubic_coef * hidden * hidden * hidden)
    bent_value = jnp.tanh(inner_arg)
    result = 0.5 * hidden * (1.0 + bent_value)
    slopes = 0.5 * (1.0 + bent_value) + 0.5 * hidden * (
        1.0 - bent_value * bent_value
    ) * root_two_pi * (1.0 + 3.0 * cubic_coef * hidden * hidden)
    return (result, slopes)


def halves(value):
    high = value.astype(BF16)
    return high, (value - high.astype(F32)).astype(BF16)


def kernel(
    tokens, up_weight, down_weight, cotangent,
    output, grad_tokens, grad_up, grad_down,
    gathered, raw, weights, partial, summed, spread, slope, fold, from_sib,
    near, far_x, far_y, last, ends, result, give, take, widths, grads,
    send_sem, recv_sem, local_sem,
):
    row, z, depth = lax.axis_index("row"), lax.axis_index("col"), lax.axis_index("depth")
    y, xl, xh, q = row // 2, row % 2, depth // 2, depth % 2
    xh_r, xh_l, xh_s = (xh + xl) % 2, (xh + xl + 1) % 2, (xh + xl + q) % 2
    sib = (row, z, xh * 2 + 1 - q)
    y_r, y_l = (((y + 1) % 4) * 2 + xl, z, depth), (((y + 3) % 4) * 2 + xl, z, depth)
    x_r, x_l = (y * 2 + 1 - xl, z, xh_r * 2 + q), (y * 2 + 1 - xl, z, xh_l * 2 + q)
    z_r, z_l = (row, (z + 1) % 8, depth), (row, (z + 7) % 8, depth)
    y_s = (((y + 1 + 2 * q) % 4) * 2 + xl, z, depth)
    x_s = (y * 2 + 1 - xl, z, xh_s * 2 + q)
    z_dev, z_sgn = (z_r, z_l), (1, 7)

    slots, pending = {}, []

    def remote(name, src, dst, device):
        at = slots.setdefault(name, len(slots))
        return pltpu.make_async_remote_copy(
            src_ref=src, dst_ref=dst, send_sem=send_sem.at[at], recv_sem=recv_sem.at[at],
            device_id=device, device_id_type=pl.DeviceIdType.MESH,
        )

    def send(name, src, dst, device):
        copy = remote(name, src, dst, device)
        copy.start()
        pending.append(copy)

    def arrive(name, dst):
        remote(name, dst, dst, sib).wait_recv()

    def rows(core, half):
        return pl.ds(pl.multiple_of(core * 96 + half * 48, 8), 48)

    def own_piece(a, g, dy, half):
        return gathered.at[a, g, (y + dy) % 4, rows(q, half)]

    def own_rows(a, half):
        return (tokens, cotangent)[a].at[rows(q, half)]

    def across_x(a, dy, half):
        src = own_rows(a, half) if dy == 0 else own_piece(a, 0, dy, half)
        send(("x", a, dy, half), src, own_piece(a, 1, dy, half), (x_r, x_l)[half])

    def to_core(a, g, dy, half):
        piece = own_piece(a, g, dy, half)
        send(("s", a, g, dy, half), piece, piece, sib)

    def own_x(a):
        for half in range(2):
            across_x(a, 0, half)

    def own_y(a):
        for halves_of in ((0, 1), (1, 0)):
            for way in range(2):
                half = halves_of[way]
                send(("y", a, way, half), own_rows(a, half), own_piece(a, 0, 0, half), (y_r, y_l)[way])

    def gy(a, way, half):
        dy = 3 if way == 0 else 1
        piece = own_piece(a, 0, dy, half)
        arrive(("y", a, way, half), piece)
        if half == way:
            send(("yf", a, way), piece, piece, (y_r, y_l)[way])
        across_x(a, dy, half)
        to_core(a, 0, dy, half)

    def gf(a, way):
        arrive(("yf", a, way), own_piece(a, 0, 2, way))
        across_x(a, 2, way)
        to_core(a, 0, 2, way)

    def gx(a, dy, half):
        arrive(("x", a, dy, half), own_piece(a, 1, dy, half))
        to_core(a, 1, dy, half)

    def split_weights(a):
        loads[2 + a].wait()
        high, low = halves(raw[a])
        weights[a, 0:UNITS] = high
        weights[a, UNITS:2 * UNITS] = high
        weights[a, 2 * UNITS:3 * UNITS] = low

    def prod(u):
        def nt(left, right):
            return lax.dot_general(left, right, (((1,), (1,)), ((), ())), preferred_element_type=F32)

        def product(a, blocks):
            high, low = halves(jnp.concatenate([gathered[a, g, (y + dy) % 4] for g, dy in blocks], axis=0))
            w_high, w_low = weights[a, 0:UNITS], weights[a, 2 * UNITS:3 * UNITS]
            return nt(high, w_high) + (nt(low, w_high) + nt(high, w_low))

        for a, g, dy in GROUPS[u]:
            if (g, dy) == (0, 0):
                loads[a].wait()
            else:
                for half in range(2):
                    arrive(("s", a, g, dy, half), gathered.at[a, g, (y + dy) % 4, rows(1 - q, half)])
        for a in range(2):
            blocks = [block for block in GROUPS[u] if block[0] == a]
            if blocks:
                total = product(a, [block[1:] for block in blocks])
                for n, block in enumerate(blocks):
                    partial[:, PLACE[block]] = total[n * BLOCK:(n + 1) * BLOCK].reshape(8, CHUNK, UNITS)
        rs_send(u, FIRST_WAY[u], 1)
        rs_send(u, 1 - FIRST_WAY[u], 2)

    def z_chunk(way, distance):
        return (z + z_sgn[way] * distance) % 8

    def rs_send(u, way, step):
        src, dst = partial.at[z_chunk(way, 5 - step), SPAN[u]], summed.at[way, step - 1, SPAN[u]]
        send(("rs", u, way, step), src, dst, z_dev[way])

    def rs_hop(u, way, step):
        arrive(("rs", u, way, step - 1), summed.at[way, step - 2, SPAN[u]])
        c = z_chunk(way, 5 - step)
        partial[c, SPAN[u]] = partial[c, SPAN[u]] + summed[way, step - 2, SPAN[u]]
        rs_send(u, way, step)

    def ag_send(u, way, k):
        piece = spread.at[z_chunk(1 - way, k - 1), SPAN[u]]
        send(("ag", u, way, k), piece, piece, z_dev[way])

    def ag_get(u, way, k):
        arrive(("ag", u, way, k), spread.at[z_chunk(1 - way, k), SPAN[u]])
        if k < 3 or (k == 3 and way == FIRST_WAY[u]):
            ag_send(u, way, k + 1)

    def finish(u):
        for way in range(2):
            arrive(("rs", u, way, 4), summed.at[way, 3, SPAN[u]])
        for a, g, dy in GROUPS[u]:
            at = PLACE[(a, g, dy)]
            total = partial[z, at] + summed[0, 3, at] + summed[1, 3, at]
            if a == 0:
                spread[z, at], slope[g, dy] = gelu_parts(total)
            else:
                spread[z, at] = total * slope[g, dy]
        for way in range(2):
            ag_send(u, way, 1)

    def spread_rows(a, chunks):
        return jnp.concatenate([spread[c, PLACE[(a, g, dy)]] for c in chunks for g, dy in BLOCKS], axis=0)

    def round_chunk(r, core):
        if r == 4:
            return (z + 4 * core) % 8
        return (z + r + (8 - 2 * r) * core) % 8

    def f_mm(a, r, *cores):
        high, low = halves(spread_rows(a, [round_chunk(r, core) for core in cores]))
        total = jnp.dot(jnp.concatenate([high, low, high], axis=1), weights[1 - a], preferred_element_type=F32)
        for i, core in enumerate(cores):
            for n, (g, dy) in enumerate(BLOCKS):
                at = i * BLOCK + n * CHUNK
                for side in range(2):
                    fold[r - 1, a, core, side, g, (y + dy) % 4] = total[at:at + CHUNK, side * UNITS:(side + 1) * UNITS]
        if 1 in cores:
            send(("fs", a, r), fold.at[r - 1, a, 1 - q], from_sib.at[r - 1, a], sib)

    def f_sib(a, r):
        i = r - 1
        arrive(("fs", a, r), from_sib.at[i, a])
        fold[i, a, q] = fold[i, a, q] + from_sib[i, a]
        if Y_FIRST[a][i]:
            send(("f1", a, r, 0), fold.at[i, a, q, 0, :, (y + 2) % 4], near.at[i, a, 0], y_r)
            send(("f1", a, r, 1), fold.at[i, a, q, 1, :, (y + 2) % 4], near.at[i, a, 1], y_l)
        else:
            send(("f1", a, r, 0), fold.at[i, a, q, 1 - xh, 0, 0:2], near.at[i, a, 0], x_r)
            send(("f1", a, r, 1), fold.at[i, a, q, 1 - xh, 0, 2:4], near.at[i, a, 1], x_l)

    def f_r1(a, r):
        i = r - 1
        for way, yy, xx in ((0, (y + 1) % 4, xh_r), (1, (y + 3) % 4, xh_l)):
            arrive(("f1", a, r, way), near.at[i, a, way])
            if Y_FIRST[a][i]:
                fold[i, a, q, way, :, yy] = fold[i, a, q, way, :, yy] + near[i, a, way]
                send(("f2", a, r, way), fold.at[i, a, q, :, :, yy], far_y.at[i, a, way], (y_r, y_l)[way])
            else:
                half = slice(2 * way, 2 * way + 2)
                fold[i, a, q, xx, 1, half] = fold[i, a, q, xx, 1, half] + near[i, a, way]
                send(("f2", a, r, way), fold.at[i, a, q, xx, 1], far_x.at[i, a, way], (x_r, x_l)[way])

    def f_r2(a, r):
        i = r - 1
        far = (far_x, far_y)[Y_FIRST[a][i]]
        for way in range(2):
            arrive(("f2", a, r, way), far.at[i, a, way])
        if Y_FIRST[a][i]:
            fold[i, a, q, :, :, y] = fold[i, a, q, :, :, y] + far[i, a, 0] + far[i, a, 1]
            send(("f3", a, r), fold.at[i, a, q, 1 - xh, 0, y], last.at[i, a], x_s)
        else:
            fold[i, a, q, xh, 0] = fold[i, a, q, xh, 0] + far[i, a, 0] + far[i, a, 1]
            send(("f3", a, r), fold.at[i, a, q, xh, 0, (y + 2) % 4], last.at[i, a], y_s)

    def f_r3(a, r):
        i = r - 1
        arrive(("f3", a, r), last.at[i, a])
        if Y_FIRST[a][i]:
            fold[i, a, q, xh_s, 1, y] = fold[i, a, q, xh_s, 1, y] + last[i, a]
            send(("f4", a, r, 0), fold.at[i, a, q, xh_r, 1, y], ends.at[i, a, 0], x_r)
            send(("f4", a, r, 1), fold.at[i, a, q, xh_l, 1, y], ends.at[i, a, 1], x_l)
        else:
            ys = (y + 1 + 2 * q) % 4
            fold[i, a, q, xh, 0, ys] = fold[i, a, q, xh, 0, ys] + last[i, a]
            send(("f4", a, r, 0), fold.at[i, a, q, xh, 0, (y + 1) % 4], ends.at[i, a, 0], y_r)
            send(("f4", a, r, 1), fold.at[i, a, q, xh, 0, (y + 3) % 4], ends.at[i, a, 1], y_l)

    def f_r4(a, r):
        i = r - 1
        arrive(("f4", a, r, 0), ends.at[i, a, 0])
        arrive(("f4", a, r, 1), ends.at[i, a, 1])
        result[a, i] = fold[i, a, q, xh, 0, y] + ends[i, a, 0] + ends[i, a, 1]

    def swap(a):
        first, second = result[a, :, :, 0:BLOCK], result[a, :, :, BLOCK:2 * BLOCK]
        lower = jnp.full(first.shape, q, jnp.int32) == 0
        give[a] = jnp.where(lower, second, first)
        send(("swap", a), give.at[a], take.at[a], sib)
        mine = jnp.where(lower, first, second)
        for r in range(1, 5):
            at = pl.ds(pl.multiple_of(round_chunk(r, q) * CHUNK, 8), CHUNK)
            widths[a, at, :] = mine[r - 1]

    def swapped(a):
        arrive(("swap", a), take.at[a])
        for r in range(1, 5):
            at = pl.ds(pl.multiple_of(round_chunk(r, 1 - q) * CHUNK, 8), CHUNK)
            widths[a, at, :] = take[a, r - 1]
        stores[a].start()

    rounds_done = [0, 0]

    def grad(a, r):
        chunks = (round_chunk(r, 0), round_chunk(r, 1))
        left = spread_rows(a, chunks).T
        right = jnp.concatenate([
            gathered[1 - a, g, (y + dy) % 4, pl.ds(pl.multiple_of(c * CHUNK, 8), CHUNK), :]
            for c in chunks for g, dy in BLOCKS
        ], axis=0)
        l_high, l_low = halves(left)
        r_high, r_low = halves(right)
        term = jnp.dot(
            jnp.concatenate([l_high, l_low, l_high], axis=1), jnp.concatenate([r_high, r_high, r_low], axis=0),
            preferred_element_type=F32)
        grads[a] = term if rounds_done[a] == 0 else grads[a] + term
        rounds_done[a] += 1
        if rounds_done[a] == 4:
            stores[2 + a].start()

    def drain(count):
        for copy in pending[:count]:
            copy.wait_send()
        del pending[:count]

    loads = [
        pltpu.make_async_copy(src, dst, local_sem.at[i])
        for i, (src, dst) in enumerate((
            (tokens, gathered.at[0, 0, y]), (cotangent, gathered.at[1, 0, y]),
            (up_weight, raw.at[0]), (down_weight, raw.at[1]),
        ))
    ]
    stores = [
        pltpu.make_async_copy(src, dst, local_sem.at[4 + i])
        for i, (src, dst) in enumerate((
            (widths.at[0], output), (widths.at[1], grad_tokens), (grads.at[0], grad_down), (grads.at[1], grad_up),
        ))
    ]
    for load in loads:
        load.start()
    barrier = pltpu.get_barrier_semaphore()
    partners = (sib, y_r, y_l, x_r, x_l, z_r, z_l)
    for device in partners:
        pl.semaphore_signal(barrier, inc=1, device_id=device, device_id_type=pl.DeviceIdType.MESH)
    pl.semaphore_wait(barrier, len(partners))

    steps = (
        own_x, own_y, gy, gf, gx, split_weights, prod, rs_hop, finish, ag_get,
        f_mm, f_sib, f_r1, f_r2, f_r3, f_r4, swap, swapped, grad, drain,
    )
    for step, *at in ORDER:
        steps[step](*at)
    drain(len(pending))
    for store in stores:
        store.wait()
    assert len(slots) <= SLOTS, len(slots)


def copy_kernel(*refs):
    sources, targets, held, sem = refs[:4], refs[4:8], refs[8:12], refs[12]
    loads, stores = [], []
    for src, dst, hold in zip(sources, targets, held):
        parts = 4 if src.shape[0] == UNITS else 1
        size = src.shape[0] // parts
        for part in range(parts):
            at, n = pl.ds(part * size, size), len(loads)
            loads.append(pltpu.make_async_copy(src.at[at], hold.at[at], sem.at[0, n]))
            stores.append(pltpu.make_async_copy(hold.at[at], dst.at[at], sem.at[1, n]))
    for load in loads:
        load.start()
    for load, store in zip(loads, stores):
        load.wait()
        store.start()
    for store in stores:
        store.wait()


def shards(tokens, up_weight, down_weight, cotangent):
    anywhere, piece = pl.BlockSpec(memory_space=pl.ANY), (CHUNK, UNITS)
    shapes = (
        jax.ShapeDtypeStruct((BLOCK, BLOCK), F32),
        jax.ShapeDtypeStruct((BLOCK, BLOCK), F32),
        jax.ShapeDtypeStruct((UNITS, WIDTH), F32),
        jax.ShapeDtypeStruct((UNITS, WIDTH), F32),
    )
    results = pl.pallas_call(
        kernel,
        out_shape=shapes,
        in_specs=[anywhere] * 4,
        out_specs=(anywhere,) * 4,
        scratch_shapes=[
            pltpu.VMEM((2, 2, 4, BLOCK, WIDTH), F32),
            pltpu.VMEM((2, UNITS, WIDTH), F32),
            pltpu.VMEM((2, 3 * UNITS, WIDTH), BF16),
            pltpu.VMEM((8, 16) + piece, F32),
            pltpu.VMEM((2, 4, 16) + piece, F32),
            pltpu.VMEM((8, 16) + piece, F32),
            pltpu.VMEM((2, 4) + piece, F32),
            pltpu.VMEM((4, 2, 2, 2, 2, 4) + piece, F32),
            pltpu.VMEM((4, 2, 2, 2, 4) + piece, F32),
            pltpu.VMEM((4, 2, 2, 2) + piece, F32),
            pltpu.VMEM((4, 2, 2, 4) + piece, F32),
            pltpu.VMEM((4, 2, 2, 2, 2) + piece, F32),
            pltpu.VMEM((4, 2) + piece, F32),
            pltpu.VMEM((4, 2, 2) + piece, F32),
            pltpu.VMEM((2, 4) + piece, F32),
            pltpu.VMEM((2, 4, CHUNK, BLOCK), F32),
            pltpu.VMEM((2, 4, CHUNK, BLOCK), F32),
            pltpu.VMEM((2, BLOCK, BLOCK), F32),
            pltpu.VMEM((2, UNITS, WIDTH), F32),
            pltpu.SemaphoreType.DMA((SLOTS,)),
            pltpu.SemaphoreType.DMA((SLOTS,)),
            pltpu.SemaphoreType.DMA((8,)),
        ],
        compiler_params=pltpu.CompilerParams(
            collective_id=0, has_side_effects=True, vmem_limit_bytes=62 * 1024 * 1024),
        cost_estimate=pl.CostEstimate(flops=16_300_000_000, bytes_accessed=6_000_000, transcendentals=73728),
    )(tokens, up_weight, down_weight, cotangent)
    return pl.pallas_call(
        copy_kernel,
        out_shape=shapes,
        in_specs=[anywhere] * 4,
        out_specs=(anywhere,) * 4,
        scratch_shapes=[pltpu.VMEM(shape.shape, F32) for shape in shapes] + [pltpu.SemaphoreType.DMA((2, 10))],
    )(*results)


def solution(mesh):
    return jax.shard_map(
        shards,
        mesh=mesh,
        in_specs=(
            P("row", "col"),
            P(("row", "depth"), "col"),
            P(("row", "depth"), "col"),
            P("row", "col"),
        ),
        out_specs=(
            P("row", ("col", "depth")),
            P("row", ("col", "depth")),
            P(("row", "depth"), "col"),
            P(("row", "depth"), "col"),
        ),
        check_vma=False,
    )
```

```python
import jax
import jax.numpy as jnp
from jax import lax
from jax.experimental import pallas as pl
from jax.experimental.pallas import tpu as pltpu
from jax.sharding import PartitionSpec as P

F32, BF16 = jnp.float32, jnp.bfloat16
root_two_pi = 0.7978845608028654
cubic_coef = 0.044715

SLOTS = 260
BLOCK, WIDTH, UNITS, CHUNK = 192, 768, 384, 24
GROUPS = (
    ((0, 0, 0), (1, 0, 0)),
    ((0, 1, 0), (1, 1, 0)),
    ((0, 0, 1), (0, 0, 3)),
    ((0, 1, 1), (0, 1, 3)),
    ((0, 0, 2), (0, 1, 2)),
    ((1, 0, 1), (1, 0, 3)),
    ((1, 1, 1), (1, 1, 3)),
    ((1, 0, 2), (1, 1, 2)),
)
FIRST_WAY = (0, 1, 0, 1, 0, 1, 0, 1)
PLACE = {block: at for at, block in enumerate(block for group in GROUPS for block in group)}
SPAN = tuple(slice(PLACE[group[0]], PLACE[group[0]] + len(group)) for group in GROUPS)
BLOCKS = tuple((g, dy) for g in range(2) for dy in range(4))
Y_FIRST = ((0, 1, 0, 1), (0, 1, 1, 0))
(
    OWN_X, OWN_Y, GY, GF, GX, SPLIT_WEIGHTS, PROD, RS_HOP, FINISH, AG_GET, F_MM, F_SIB, F_R1, F_R2, F_R3, F_R4,
    SWAP, SWAPPED, GRAD, DRAIN,
) = range(20)
ORDER = (
    (OWN_Y, 0), (OWN_X, 0), (OWN_X, 1), (SPLIT_WEIGHTS, 1), (SPLIT_WEIGHTS, 0), (PROD, 0), (GY, 0, 0, 0),
    (GX, 0, 0, 0), (GX, 0, 0, 1), (GY, 0, 1, 1), (RS_HOP, 0, 0, 2), (RS_HOP, 0, 1, 3), (GY, 0, 0, 1), (GY, 0, 1, 0),
    (GX, 1, 0, 1), (GX, 1, 0, 0), (OWN_Y, 1), (RS_HOP, 0, 0, 3), (RS_HOP, 0, 1, 4), (PROD, 2), (GF, 0, 0), (GF, 0, 1),
    (RS_HOP, 0, 0, 4), (PROD, 1), (GX, 0, 1, 0), (RS_HOP, 2, 0, 2), (RS_HOP, 2, 1, 3), (GY, 1, 0, 0), (GX, 0, 3, 0),
    (GX, 0, 1, 1), (GX, 0, 3, 1), (FINISH, 0), (GY, 1, 0, 1), (GX, 0, 2, 1), (GY, 1, 1, 0), (RS_HOP, 1, 1, 2),
    (RS_HOP, 1, 0, 3), (GX, 0, 2, 0), (GY, 1, 1, 1), (DRAIN, 16), (RS_HOP, 2, 1, 4), (RS_HOP, 2, 0, 3), (PROD, 3),
    (GF, 1, 0), (GX, 1, 3, 0), (AG_GET, 0, 1, 1), (RS_HOP, 1, 1, 3), (DRAIN, 16), (RS_HOP, 1, 0, 4), (GX, 1, 3, 1),
    (PROD, 4), (DRAIN, 16), (GX, 1, 1, 0), (DRAIN, 16), (RS_HOP, 2, 0, 4), (RS_HOP, 3, 0, 3), (RS_HOP, 3, 1, 2),
    (RS_HOP, 1, 1, 4), (RS_HOP, 4, 0, 2), (GX, 1, 2, 0), (GF, 1, 1), (RS_HOP, 4, 1, 3), (FINISH, 2), (GX, 1, 1, 1),
    (RS_HOP, 3, 0, 4), (RS_HOP, 3, 1, 3), (RS_HOP, 4, 0, 3), (FINISH, 1), (AG_GET, 2, 0, 1), (RS_HOP, 4, 1, 4),
    (AG_GET, 2, 1, 1), (RS_HOP, 3, 1, 4), (RS_HOP, 4, 0, 4), (AG_GET, 1, 0, 1), (PROD, 6), (AG_GET, 1, 1, 1),
    (GX, 1, 2, 1), (AG_GET, 2, 0, 2), (FINISH, 4), (FINISH, 3), (PROD, 5), (RS_HOP, 6, 0, 2), (AG_GET, 0, 0, 1),
    (AG_GET, 2, 0, 3), (PROD, 7), (AG_GET, 4, 0, 1), (AG_GET, 1, 1, 2), (AG_GET, 2, 1, 2), (AG_GET, 3, 1, 1),
    (AG_GET, 4, 1, 1), (AG_GET, 3, 0, 1), (F_MM, 0, 1, 0, 1), (RS_HOP, 5, 1, 2), (RS_HOP, 5, 0, 3), (AG_GET, 1, 0, 2),
    (RS_HOP, 6, 1, 3), (F_SIB, 0, 1), (GRAD, 0, 1), (AG_GET, 0, 0, 2), (RS_HOP, 6, 0, 3), (F_MM, 0, 4, 0),
    (AG_GET, 3, 1, 2), (AG_GET, 4, 1, 2), (AG_GET, 1, 1, 3), (AG_GET, 4, 0, 2), (F_R1, 0, 1), (RS_HOP, 7, 1, 2),
    (AG_GET, 3, 0, 2), (RS_HOP, 7, 0, 3), (AG_GET, 0, 1, 2), (F_MM, 0, 2, 0, 1), (RS_HOP, 5, 1, 3), (AG_GET, 1, 0, 3),
    (RS_HOP, 6, 1, 4), (F_R2, 0, 1), (F_SIB, 0, 2), (AG_GET, 0, 0, 3), (GRAD, 0, 2), (AG_GET, 4, 0, 3), (DRAIN, 16),
    (RS_HOP, 7, 1, 3), (AG_GET, 2, 1, 3), (RS_HOP, 5, 0, 4), (RS_HOP, 6, 0, 4), (F_R1, 0, 2), (RS_HOP, 5, 1, 4),
    (AG_GET, 4, 1, 3), (AG_GET, 3, 0, 3), (AG_GET, 2, 0, 4), (F_R3, 0, 1), (AG_GET, 0, 1, 3), (AG_GET, 3, 1, 3),
    (F_MM, 0, 3, 0, 1), (RS_HOP, 7, 0, 4), (GRAD, 0, 3), (RS_HOP, 7, 1, 4), (AG_GET, 4, 0, 4), (AG_GET, 0, 0, 4),
    (F_SIB, 0, 3), (AG_GET, 1, 1, 4), (F_R2, 0, 2), (FINISH, 5), (FINISH, 6), (AG_GET, 3, 1, 4), (F_MM, 0, 4, 1),
    (FINISH, 7), (F_R4, 0, 1), (F_MM, 1, 4, 0), (AG_GET, 5, 0, 1), (F_R1, 0, 3), (AG_GET, 5, 1, 1), (F_SIB, 0, 4),
    (AG_GET, 6, 0, 1), (AG_GET, 6, 1, 1), (GRAD, 0, 4), (AG_GET, 7, 1, 1), (AG_GET, 7, 0, 1), (AG_GET, 5, 0, 2),
    (AG_GET, 5, 1, 2), (F_MM, 1, 1, 0, 1), (AG_GET, 6, 1, 2), (F_R3, 0, 2), (F_R2, 0, 3), (AG_GET, 6, 0, 2),
    (F_R1, 0, 4), (AG_GET, 7, 1, 2), (AG_GET, 7, 0, 2), (F_MM, 1, 2, 0, 1), (AG_GET, 5, 1, 3), (GRAD, 1, 1),
    (AG_GET, 6, 0, 3), (AG_GET, 7, 1, 3), (AG_GET, 5, 0, 3), (F_R4, 0, 2), (F_SIB, 1, 1), (AG_GET, 6, 1, 3),
    (F_R3, 0, 3), (F_SIB, 1, 2), (AG_GET, 7, 0, 3), (F_MM, 1, 3, 0, 1), (F_R2, 0, 4), (AG_GET, 5, 1, 4),
    (AG_GET, 7, 1, 4), (AG_GET, 6, 0, 4), (F_MM, 1, 4, 1), (F_R1, 1, 1), (F_SIB, 1, 3), (F_R1, 1, 2), (F_SIB, 1, 4),
    (GRAD, 1, 2), (F_R2, 1, 1), (F_R3, 0, 4), (F_R4, 0, 3), (DRAIN, 16), (F_R1, 1, 3), (F_R1, 1, 4), (DRAIN, 16),
    (GRAD, 1, 3), (F_R3, 1, 1), (F_R2, 1, 2), (F_R4, 0, 4), (F_R2, 1, 3), (SWAP, 0), (F_R2, 1, 4), (F_R3, 1, 2),
    (DRAIN, 16), (F_R3, 1, 3), (F_R4, 1, 1), (F_R3, 1, 4), (GRAD, 1, 4), (F_R4, 1, 2), (F_R4, 1, 3), (F_R4, 1, 4),
    (SWAP, 1), (DRAIN, 16), (SWAPPED, 0), (SWAPPED, 1),
)


def gelu_parts(hidden):
    inner_arg = root_two_pi * (hidden + cubic_coef * hidden * hidden * hidden)
    bent_value = jnp.tanh(inner_arg)
    result = 0.5 * hidden * (1.0 + bent_value)
    slopes = 0.5 * (1.0 + bent_value) + 0.5 * hidden * (
        1.0 - bent_value * bent_value
    ) * root_two_pi * (1.0 + 3.0 * cubic_coef * hidden * hidden)
    return (result, slopes)


def halves(value):
    high = value.astype(BF16)
    return high, (value - high.astype(F32)).astype(BF16)


def kernel(
    tokens, up_weight, down_weight, cotangent,
    output, grad_tokens, grad_up, grad_down,
    gathered, raw, weights, partial, summed, spread, slope, fold, from_sib,
    near, far_x, far_y, last, ends, result, give, take, widths, grads,
    send_sem, recv_sem, local_sem,
):
    row, z, depth = lax.axis_index("row"), lax.axis_index("col"), lax.axis_index("depth")
    y, xl, xh, q = row // 2, row % 2, depth // 2, depth % 2
    xh_r, xh_l, xh_s = (xh + xl) % 2, (xh + xl + 1) % 2, (xh + xl + q) % 2
    sib = (row, z, xh * 2 + 1 - q)
    y_r, y_l = (((y + 1) % 4) * 2 + xl, z, depth), (((y + 3) % 4) * 2 + xl, z, depth)
    x_r, x_l = (y * 2 + 1 - xl, z, xh_r * 2 + q), (y * 2 + 1 - xl, z, xh_l * 2 + q)
    z_r, z_l = (row, (z + 1) % 8, depth), (row, (z + 7) % 8, depth)
    y_s = (((y + 1 + 2 * q) % 4) * 2 + xl, z, depth)
    x_s = (y * 2 + 1 - xl, z, xh_s * 2 + q)
    z_dev, z_sgn = (z_r, z_l), (1, 7)

    slots, pending = {}, []

    def remote(name, src, dst, device):
        at = slots.setdefault(name, len(slots))
        return pltpu.make_async_remote_copy(
            src_ref=src, dst_ref=dst, send_sem=send_sem.at[at], recv_sem=recv_sem.at[at],
            device_id=device, device_id_type=pl.DeviceIdType.MESH,
        )

    def send(name, src, dst, device):
        copy = remote(name, src, dst, device)
        copy.start()
        pending.append(copy)

    def arrive(name, dst):
        remote(name, dst, dst, sib).wait_recv()

    def rows(core, half):
        return pl.ds(pl.multiple_of(core * 96 + half * 48, 8), 48)

    def own_piece(a, g, dy, half):
        return gathered.at[a, g, (y + dy) % 4, rows(q, half)]

    def own_rows(a, half):
        return (tokens, cotangent)[a].at[rows(q, half)]

    def across_x(a, dy, half):
        src = own_rows(a, half) if dy == 0 else own_piece(a, 0, dy, half)
        send(("x", a, dy, half), src, own_piece(a, 1, dy, half), (x_r, x_l)[half])

    def to_core(a, g, dy, half):
        piece = own_piece(a, g, dy, half)
        send(("s", a, g, dy, half), piece, piece, sib)

    def own_x(a):
        for half in range(2):
            across_x(a, 0, half)

    def own_y(a):
        for halves_of in ((0, 1), (1, 0)):
            for way in range(2):
                half = halves_of[way]
                send(("y", a, way, half), own_rows(a, half), own_piece(a, 0, 0, half), (y_r, y_l)[way])

    def gy(a, way, half):
        dy = 3 if way == 0 else 1
        piece = own_piece(a, 0, dy, half)
        arrive(("y", a, way, half), piece)
        if half == way:
            send(("yf", a, way), piece, piece, (y_r, y_l)[way])
        across_x(a, dy, half)
        to_core(a, 0, dy, half)

    def gf(a, way):
        arrive(("yf", a, way), own_piece(a, 0, 2, way))
        across_x(a, 2, way)
        to_core(a, 0, 2, way)

    def gx(a, dy, half):
        arrive(("x", a, dy, half), own_piece(a, 1, dy, half))
        to_core(a, 1, dy, half)

    def split_weights(a):
        loads[2 + a].wait()
        high, low = halves(raw[a])
        weights[a, 0:UNITS] = high
        weights[a, UNITS:2 * UNITS] = high
        weights[a, 2 * UNITS:3 * UNITS] = low

    def prod(u):
        def nt(left, right):
            return lax.dot_general(left, right, (((1,), (1,)), ((), ())), preferred_element_type=F32)

        def product(a, blocks):
            high, low = halves(jnp.concatenate([gathered[a, g, (y + dy) % 4] for g, dy in blocks], axis=0))
            w_high, w_low = weights[a, 0:UNITS], weights[a, 2 * UNITS:3 * UNITS]
            return nt(high, w_high) + (nt(low, w_high) + nt(high, w_low))

        for a, g, dy in GROUPS[u]:
            if (g, dy) == (0, 0):
                loads[a].wait()
            else:
                for half in range(2):
                    arrive(("s", a, g, dy, half), gathered.at[a, g, (y + dy) % 4, rows(1 - q, half)])
        for a in range(2):
            blocks = [block for block in GROUPS[u] if block[0] == a]
            if blocks:
                total = product(a, [block[1:] for block in blocks])
                for n, block in enumerate(blocks):
                    partial[:, PLACE[block]] = total[n * BLOCK:(n + 1) * BLOCK].reshape(8, CHUNK, UNITS)
        rs_send(u, FIRST_WAY[u], 1)
        rs_send(u, 1 - FIRST_WAY[u], 2)

    def z_chunk(way, distance):
        return (z + z_sgn[way] * distance) % 8

    def rs_send(u, way, step):
        src, dst = partial.at[z_chunk(way, 5 - step), SPAN[u]], summed.at[way, step - 1, SPAN[u]]
        send(("rs", u, way, step), src, dst, z_dev[way])

    def rs_hop(u, way, step):
        arrive(("rs", u, way, step - 1), summed.at[way, step - 2, SPAN[u]])
        c = z_chunk(way, 5 - step)
        partial[c, SPAN[u]] = partial[c, SPAN[u]] + summed[way, step - 2, SPAN[u]]
        rs_send(u, way, step)

    def ag_send(u, way, k):
        piece = spread.at[z_chunk(1 - way, k - 1), SPAN[u]]
        send(("ag", u, way, k), piece, piece, z_dev[way])

    def ag_get(u, way, k):
        arrive(("ag", u, way, k), spread.at[z_chunk(1 - way, k), SPAN[u]])
        if k < 3 or (k == 3 and way == FIRST_WAY[u]):
            ag_send(u, way, k + 1)

    def finish(u):
        for way in range(2):
            arrive(("rs", u, way, 4), summed.at[way, 3, SPAN[u]])
        for a, g, dy in GROUPS[u]:
            at = PLACE[(a, g, dy)]
            total = partial[z, at] + summed[0, 3, at] + summed[1, 3, at]
            if a == 0:
                spread[z, at], slope[g, dy] = gelu_parts(total)
            else:
                spread[z, at] = total * slope[g, dy]
        for way in range(2):
            ag_send(u, way, 1)

    def spread_rows(a, chunks):
        return jnp.concatenate([spread[c, PLACE[(a, g, dy)]] for c in chunks for g, dy in BLOCKS], axis=0)

    def round_chunk(r, core):
        if r == 4:
            return (z + 4 * core) % 8
        return (z + r + (8 - 2 * r) * core) % 8

    def f_mm(a, r, *cores):
        high, low = halves(spread_rows(a, [round_chunk(r, core) for core in cores]))
        total = jnp.dot(jnp.concatenate([high, low, high], axis=1), weights[1 - a], preferred_element_type=F32)
        for i, core in enumerate(cores):
            for n, (g, dy) in enumerate(BLOCKS):
                at = i * BLOCK + n * CHUNK
                for side in range(2):
                    fold[r - 1, a, core, side, g, (y + dy) % 4] = total[at:at + CHUNK, side * UNITS:(side + 1) * UNITS]
        if 1 in cores:
            send(("fs", a, r), fold.at[r - 1, a, 1 - q], from_sib.at[r - 1, a], sib)

    def f_sib(a, r):
        i = r - 1
        arrive(("fs", a, r), from_sib.at[i, a])
        fold[i, a, q] = fold[i, a, q] + from_sib[i, a]
        if Y_FIRST[a][i]:
            send(("f1", a, r, 0), fold.at[i, a, q, 0, :, (y + 2) % 4], near.at[i, a, 0], y_r)
            send(("f1", a, r, 1), fold.at[i, a, q, 1, :, (y + 2) % 4], near.at[i, a, 1], y_l)
        else:
            send(("f1", a, r, 0), fold.at[i, a, q, 1 - xh, 0, 0:2], near.at[i, a, 0], x_r)
            send(("f1", a, r, 1), fold.at[i, a, q, 1 - xh, 0, 2:4], near.at[i, a, 1], x_l)

    def f_r1(a, r):
        i = r - 1
        for way, yy, xx in ((0, (y + 1) % 4, xh_r), (1, (y + 3) % 4, xh_l)):
            arrive(("f1", a, r, way), near.at[i, a, way])
            if Y_FIRST[a][i]:
                fold[i, a, q, way, :, yy] = fold[i, a, q, way, :, yy] + near[i, a, way]
                send(("f2", a, r, way), fold.at[i, a, q, :, :, yy], far_y.at[i, a, way], (y_r, y_l)[way])
            else:
                half = slice(2 * way, 2 * way + 2)
                fold[i, a, q, xx, 1, half] = fold[i, a, q, xx, 1, half] + near[i, a, way]
                send(("f2", a, r, way), fold.at[i, a, q, xx, 1], far_x.at[i, a, way], (x_r, x_l)[way])

    def f_r2(a, r):
        i = r - 1
        far = (far_x, far_y)[Y_FIRST[a][i]]
        for way in range(2):
            arrive(("f2", a, r, way), far.at[i, a, way])
        if Y_FIRST[a][i]:
            fold[i, a, q, :, :, y] = fold[i, a, q, :, :, y] + far[i, a, 0] + far[i, a, 1]
            send(("f3", a, r), fold.at[i, a, q, 1 - xh, 0, y], last.at[i, a], x_s)
        else:
            fold[i, a, q, xh, 0] = fold[i, a, q, xh, 0] + far[i, a, 0] + far[i, a, 1]
            send(("f3", a, r), fold.at[i, a, q, xh, 0, (y + 2) % 4], last.at[i, a], y_s)

    def f_r3(a, r):
        i = r - 1
        arrive(("f3", a, r), last.at[i, a])
        if Y_FIRST[a][i]:
            fold[i, a, q, xh_s, 1, y] = fold[i, a, q, xh_s, 1, y] + last[i, a]
            send(("f4", a, r, 0), fold.at[i, a, q, xh_r, 1, y], ends.at[i, a, 0], x_r)
            send(("f4", a, r, 1), fold.at[i, a, q, xh_l, 1, y], ends.at[i, a, 1], x_l)
        else:
            ys = (y + 1 + 2 * q) % 4
            fold[i, a, q, xh, 0, ys] = fold[i, a, q, xh, 0, ys] + last[i, a]
            send(("f4", a, r, 0), fold.at[i, a, q, xh, 0, (y + 1) % 4], ends.at[i, a, 0], y_r)
            send(("f4", a, r, 1), fold.at[i, a, q, xh, 0, (y + 3) % 4], ends.at[i, a, 1], y_l)

    def f_r4(a, r):
        i = r - 1
        arrive(("f4", a, r, 0), ends.at[i, a, 0])
        arrive(("f4", a, r, 1), ends.at[i, a, 1])
        result[a, i] = fold[i, a, q, xh, 0, y] + ends[i, a, 0] + ends[i, a, 1]

    def swap(a):
        first, second = result[a, :, :, 0:BLOCK], result[a, :, :, BLOCK:2 * BLOCK]
        lower = jnp.full(first.shape, q, jnp.int32) == 0
        give[a] = jnp.where(lower, second, first)
        send(("swap", a), give.at[a], take.at[a], sib)
        mine = jnp.where(lower, first, second)
        for r in range(1, 5):
            at = pl.ds(pl.multiple_of(round_chunk(r, q) * CHUNK, 8), CHUNK)
            widths[a, at, :] = mine[r - 1]

    def swapped(a):
        arrive(("swap", a), take.at[a])
        for r in range(1, 5):
            at = pl.ds(pl.multiple_of(round_chunk(r, 1 - q) * CHUNK, 8), CHUNK)
            widths[a, at, :] = take[a, r - 1]
        stores[a].start()

    rounds_done = [0, 0]

    def grad(a, r):
        chunks = (round_chunk(r, 0), round_chunk(r, 1))
        left = spread_rows(a, chunks).T
        right = jnp.concatenate([
            gathered[1 - a, g, (y + dy) % 4, pl.ds(pl.multiple_of(c * CHUNK, 8), CHUNK), :]
            for c in chunks for g, dy in BLOCKS
        ], axis=0)
        l_high, l_low = halves(left)
        r_high, r_low = halves(right)
        term = jnp.dot(
            jnp.concatenate([l_high, l_low, l_high], axis=1), jnp.concatenate([r_high, r_high, r_low], axis=0),
            preferred_element_type=F32)
        grads[a] = term if rounds_done[a] == 0 else grads[a] + term
        rounds_done[a] += 1
        if rounds_done[a] == 4:
            stores[2 + a].start()

    def drain(count):
        for copy in pending[:count]:
            copy.wait_send()
        del pending[:count]

    loads = [
        pltpu.make_async_copy(src, dst, local_sem.at[i])
        for i, (src, dst) in enumerate((
            (tokens, gathered.at[0, 0, y]), (cotangent, gathered.at[1, 0, y]),
            (up_weight, raw.at[0]), (down_weight, raw.at[1]),
        ))
    ]
    stores = [
        pltpu.make_async_copy(src, dst, local_sem.at[4 + i])
        for i, (src, dst) in enumerate((
            (widths.at[0], output), (widths.at[1], grad_tokens), (grads.at[0], grad_down), (grads.at[1], grad_up),
        ))
    ]
    for load in loads:
        load.start()
    barrier = pltpu.get_barrier_semaphore()
    partners = (sib, y_r, y_l, x_r, x_l, z_r, z_l)
    for device in partners:
        pl.semaphore_signal(barrier, inc=1, device_id=device, device_id_type=pl.DeviceIdType.MESH)
    pl.semaphore_wait(barrier, len(partners))

    steps = (
        own_x, own_y, gy, gf, gx, split_weights, prod, rs_hop, finish, ag_get,
        f_mm, f_sib, f_r1, f_r2, f_r3, f_r4, swap, swapped, grad, drain,
    )
    for step, *at in ORDER:
        steps[step](*at)
    drain(len(pending))
    for store in stores:
        store.wait()
    assert len(slots) <= SLOTS, len(slots)


def copy_kernel(*refs):
    sources, targets, held, sem = refs[:4], refs[4:8], refs[8:12], refs[12]
    loads, stores = [], []
    for src, dst, hold in zip(sources, targets, held):
        parts = 4 if src.shape[0] == UNITS else 1
        size = src.shape[0] // parts
        for part in range(parts):
            at, n = pl.ds(part * size, size), len(loads)
            loads.append(pltpu.make_async_copy(src.at[at], hold.at[at], sem.at[0, n]))
            stores.append(pltpu.make_async_copy(hold.at[at], dst.at[at], sem.at[1, n]))
    for load in loads:
        load.start()
    for load, store in zip(loads, stores):
        load.wait()
        store.start()
    for store in stores:
        store.wait()


def shards(tokens, up_weight, down_weight, cotangent):
    anywhere, piece = pl.BlockSpec(memory_space=pl.ANY), (CHUNK, UNITS)
    shapes = (
        jax.ShapeDtypeStruct((BLOCK, BLOCK), F32),
        jax.ShapeDtypeStruct((BLOCK, BLOCK), F32),
        jax.ShapeDtypeStruct((UNITS, WIDTH), F32),
        jax.ShapeDtypeStruct((UNITS, WIDTH), F32),
    )
    results = pl.pallas_call(
        kernel,
        out_shape=shapes,
        in_specs=[anywhere] * 4,
        out_specs=(anywhere,) * 4,
        scratch_shapes=[
            pltpu.VMEM((2, 2, 4, BLOCK, WIDTH), F32),
            pltpu.VMEM((2, UNITS, WIDTH), F32),
            pltpu.VMEM((2, 3 * UNITS, WIDTH), BF16),
            pltpu.VMEM((8, 16) + piece, F32),
            pltpu.VMEM((2, 4, 16) + piece, F32),
            pltpu.VMEM((8, 16) + piece, F32),
            pltpu.VMEM((2, 4) + piece, F32),
            pltpu.VMEM((4, 2, 2, 2, 2, 4) + piece, F32),
            pltpu.VMEM((4, 2, 2, 2, 4) + piece, F32),
            pltpu.VMEM((4, 2, 2, 2) + piece, F32),
            pltpu.VMEM((4, 2, 2, 4) + piece, F32),
            pltpu.VMEM((4, 2, 2, 2, 2) + piece, F32),
            pltpu.VMEM((4, 2) + piece, F32),
            pltpu.VMEM((4, 2, 2) + piece, F32),
            pltpu.VMEM((2, 4) + piece, F32),
            pltpu.VMEM((2, 4, CHUNK, BLOCK), F32),
            pltpu.VMEM((2, 4, CHUNK, BLOCK), F32),
            pltpu.VMEM((2, BLOCK, BLOCK), F32),
            pltpu.VMEM((2, UNITS, WIDTH), F32),
            pltpu.SemaphoreType.DMA((SLOTS,)),
            pltpu.SemaphoreType.DMA((SLOTS,)),
            pltpu.SemaphoreType.DMA((8,)),
        ],
        compiler_params=pltpu.CompilerParams(
            collective_id=0, has_side_effects=True, vmem_limit_bytes=62 * 1024 * 1024),
        cost_estimate=pl.CostEstimate(flops=16_300_000_000, bytes_accessed=6_000_000, transcendentals=73728),
    )(tokens, up_weight, down_weight, cotangent)
    return pl.pallas_call(
        copy_kernel,
        out_shape=shapes,
        in_specs=[anywhere] * 4,
        out_specs=(anywhere,) * 4,
        scratch_shapes=[pltpu.VMEM(shape.shape, F32) for shape in shapes] + [pltpu.SemaphoreType.DMA((2, 10))],
    )(*results)


def solution(mesh):
    return jax.shard_map(
        shards,
        mesh=mesh,
        in_specs=(
            P("row", "col"),
            P(("row", "depth"), "col"),
            P(("row", "depth"), "col"),
            P("row", "col"),
        ),
        out_specs=(
            P("row", ("col", "depth")),
            P("row", ("col", "depth")),
            P(("row", "depth"), "col"),
            P(("row", "depth"), "col"),
        ),
        check_vma=False,
    )
```
